512 devices in a mesh: gx: 32 (over x, y), gy: 16 (over z, core).
Axes of the slice: x: 4, y: 8, z: 8, core: 2. Of those that a mesh axis runs over, the one named last changes fastest.
Arguments:
- right_side: float32 [256, 128, 128], P('gx', 'gy'), may hold values from -12 to 12
- coefficient: float32 [256, 128, 128], P('gx', 'gy'), may hold values from 0.3 to 3
- previous: float32 [256, 128, 128], P('gx', 'gy'), may hold values from -6 to 6
Outputs:
- potential: float32 [256, 128, 128], P('gx', 'gy')
The draws below stay inside these ranges and needn't reach their ends.
All inputs are finite; a program needn't handle non-finite values.
Results may differ from the reference program's by a relative error of at most 0.00002.
Values sent between devices are 32-bit elements; how exact they have to be, the bound alone decides.
No kernel may reach another device: no remote copies, remote signals or barrier semaphores. Data moves between devices by JAX's collectives and lax.ppermute only.
A program may use at most 64 MiB of HBM per device.

```python
import math
import jax
import jax.numpy as jnp

NZ = 128
LEVELS = 6
PRE_SWEEPS = 2
POST_SWEEPS = 2
COARSE_SWEEPS = 8
NX = 256
NY = 128


def draw_right_side(key, part):
    key = jax.random.fold_in(key, 11)
    extent = (NX, NY, NZ)
    return jnp.clip(3.0 * jax.random.normal(key, extent, jnp.float32), -12.0, 12.0)


def shard_levels(own_key, shape, pieces, least, largest):
    def one(axis_at, shards_of):
        draws = jax.random.uniform(jax.random.fold_in(jax.random.fold_in(own_key, 6), axis_at), (shards_of,), jnp.float32, least / len(pieces), largest / len(pieces))
        return jnp.repeat(jnp.exp(draws), shape[axis_at] // shards_of).reshape((-1,) + (1,) * (len(shape) - axis_at - 1))

    level = one(*pieces[0])
    for cut in pieces[1:]:
        level = level * one(*cut)
    return level


def centred(stream_key, shape, width, limit, shards=(), kind=jnp.bfloat16):
    result = jax.random.normal(stream_key, shape, jnp.float32) * width
    if len(shards) > 0:
        result = shard_levels(stream_key, shape, shards, -0.22, 0.18) * result
    return jnp.clip(result, min=-limit, max=limit).astype(kind)


def setup_inputs(seed: int = 0) -> dict:
    key_of = jax.random.split(jax.random.key(seed), 4)
    return {
        "right_side": draw_right_side(jax.random.fold_in(key_of[3], 71), 0),
        "coefficient": jnp.clip(jnp.exp(math.log(3.0) - 2.3025851 * jax.random.uniform(key_of[1], (NX, NY, NZ), jnp.float32) ** shard_levels(key_of[1], (NX, NY, NZ), ((0, 32), (1, 16)), -0.2, 0.2)), 0.3, 3.0),
        "previous": centred(key_of[2], (NX, NY, NZ), 1.0, 6.0, ((0, 32), (1, 16)), jnp.float32),
    }


relaxation = 0.8


def neighbours(padded):
    return [padded[2:, 1:-1, 1:-1], padded[:-2, 1:-1, 1:-1],
            padded[1:-1, 2:, 1:-1], padded[1:-1, :-2, 1:-1],
            padded[1:-1, 1:-1, 2:], padded[1:-1, 1:-1, :-2]]


def face_weights(padded_coeff, coeff):
    return [0.5 * (coeff + other) for other in neighbours(padded_coeff)]


def operate(padded_field, field, weights, diagonal, factor):
    others = neighbours(padded_field)
    offdiag = weights[0] * others[0]
    for number in range(1, 6):
        offdiag = offdiag + weights[number] * others[number]
    return factor * (diagonal * field - offdiag)


def restrict(values):
    sizes_here = values.shape
    blocks = values.reshape(sizes_here[0] // 2, 2, sizes_here[1] // 2, 2, sizes_here[2] // 2, 2)
    return jnp.mean(blocks, axis=(1, 3, 5))


def prolong(values):
    sizes_here = values.shape
    spread = jnp.broadcast_to(values[:, None, :, None, :, None],
                              (sizes_here[0], 2, sizes_here[1], 2, sizes_here[2], 2))
    return spread.reshape(2 * sizes_here[0], 2 * sizes_here[1], 2 * sizes_here[2])


def descend(degree, field, source, coeff):
    factor = 0.25 ** degree
    weights = face_weights(jnp.pad(coeff, 1), coeff)
    diagonal = weights[0] + weights[1] + weights[2] + weights[3] + weights[4] + weights[5]
    inverse = relaxation / (factor * diagonal)

    def sweep_once(current):
        return current + inverse * (source - operate(jnp.pad(current, 1), current, weights, diagonal, factor))

    if degree == LEVELS - 1:
        for number in range(COARSE_SWEEPS):
            field = sweep_once(field)
        return field
    for number in range(PRE_SWEEPS):
        field = sweep_once(field)
    residual = source - operate(jnp.pad(field, 1), field, weights, diagonal, factor)
    coarse_source = restrict(residual)
    correction = descend(degree + 1, jnp.zeros(coarse_source.shape, jnp.float32), coarse_source, restrict(coeff))
    field = field + prolong(correction)
    for number in range(POST_SWEEPS):
        field = sweep_once(field)
    return field


def reference(right_side, coefficient, previous):
    return descend(0, previous, right_side, coefficient)
```

```python
import jax
import jax.numpy as jnp
from jax import lax
from jax.experimental import pallas as pl
from jax.experimental.pallas import tpu as pltpu
from jax.sharding import PartitionSpec as P

RELAX = 0.8
KEEP = 1.0 - RELAX
HALO = 7
ROWS = 24
COARSE_SWEEPS = 8
VMEM = 48 * 1024 * 1024
EXACT = lax.Precision.HIGHEST


def lanes(x, n):
    return pltpu.roll(x, (-n) % x.shape[1], axis=1)


def rows(x, n):
    return pltpu.roll(x, (-n) % x.shape[0], axis=0)


def iota(shape, dim):
    return lax.broadcasted_iota(jnp.int32, shape, dim)


class Window:
    def __init__(self, step, planes):
        self.step = step
        self.planes = planes
        lane = iota((ROWS, 128), 1)
        self.last = lane >= 128 - step
        self.edge = (lane < step) | self.last

    def weights(self, coeff):
        first, end = self.planes
        self.wx, self.wy, self.wz, self.diag, self.inv = {}, {}, {}, {}, {}
        for i in range(first - 1, end):
            self.wx[i] = coeff[i] + coeff[i + 1]
        for i in range(first, end):
            k = coeff[i]
            wy = k + rows(k, self.step)
            wz = jnp.where(self.last, 0.0, k + lanes(k, self.step))
            diag = self.wx[i] + self.wx[i - 1] + (wy + rows(wy, -self.step))
            diag = diag + (wz + lanes(wz, -self.step)) + jnp.where(self.edge, k, 0.0)
            self.wy[i], self.wz[i], self.diag[i] = wy, wz, diag
            self.inv[i] = jnp.where(k > 0.0, RELAX / diag, 0.0)

    def around(self, v, i):
        c = v[i]
        wy, wz, step = self.wy[i], self.wz[i], self.step
        total = self.wx[i] * v[i + 1] + self.wx[i - 1] * v[i - 1]
        total = total + (wy * rows(c, step) + rows(wy * c, -step))
        return total + (wz * lanes(c, step) + lanes(wz * c, -step))

    def sweep(self, v, source, first, end):
        return {
            i: KEEP * v[i] + self.inv[i] * (source[i] + self.around(v, i)) for i in range(first, end)
        }

    def residual(self, v, source, first, end):
        return {i: source[i] - self.diag[i] * v[i] + self.around(v, i) for i in range(first, end)}


class Stored:
    def __init__(self, ref, first):
        self.ref, self.first = ref, first

    def __getitem__(self, i):
        return self.ref[i - self.first]

    def __setitem__(self, i, value):
        self.ref[i - self.first] = value


def block_sum(low, high, step):
    s = low + high
    s = s + rows(s, step)
    return s + lanes(s, step)


def down_kernel(mid, low, high, packed, v0_out, k0_out, f0_out, k1_out, f1_out):
    def field(which):
        return {
            i - HALO: jnp.concatenate([low[which, i], mid[which, i], high[which, i]], axis=0)
            for i in range(mid.shape[1])
        }

    source, coeff, v = field(0), field(1), field(2)
    source = {i: 2.0 * source[i] for i in range(-6, 14)}

    fine = Window(1, (-6, 14))
    fine.weights(coeff)
    v = fine.sweep(v, source, -6, 14)
    v = fine.sweep(v, source, -5, 13)
    for i in range(-2, 10):
        v0_out[i + 2] = v[i]
        k0_out[i + 2] = coeff[i]
    for i in range(-1, 9):
        f0_out[i + 1] = source[i]
    r = fine.residual(v, source, -4, 12)

    source = {i: 0.5 * block_sum(r[2 * i], r[2 * i + 1], 1) for i in range(-2, 6)}
    coeff = {i: 0.125 * block_sum(coeff[2 * i], coeff[2 * i + 1], 1) for i in range(-3, 7)}
    for i in range(-2, 6):
        f1_out[i + 2] = source[i]
    for i in range(-3, 7):
        k1_out[i + 3] = coeff[i]
    middle = Window(2, (-2, 6))
    middle.weights(coeff)
    v = {i: middle.inv[i] * source[i] for i in range(-2, 6)}
    v = middle.sweep(v, source, -1, 5)
    even = iota((8, 128), 1) % 2 == 0
    for i in range(4):
        c = v[i][8:16]
        c = jnp.where(even, c, lanes(rows(c, 2), -1))
        packed[2 * i + 2 : 2 * i + 3, :] = c[0:1]
        packed[2 * i + 3 : 2 * i + 4, :] = c[4:5]
    r = middle.residual(v, source, 0, 4)

    source = [0.5 * block_sum(r[2 * i], r[2 * i + 1], 2)[8:16] for i in range(2)]
    coeff = [0.125 * block_sum(coeff[2 * i], coeff[2 * i + 1], 2)[8:16] for i in range(2)]
    table = jnp.concatenate(source + coeff, axis=0)
    pick = jnp.where(iota((128, 128), 0) == 4 * (iota((128, 128), 1) % 32), 1.0, 0.0)
    table = jnp.dot(table, pick, precision=EXACT, preferred_element_type=jnp.float32)
    group = iota((16, 128), 1) // 32
    chosen = iota((16, 128), 0) == 4 * group
    for c in range(2):
        one = jnp.where(chosen, table[16 * c : 16 * c + 16], 0.0)
        packed[c : c + 1, :] = jnp.sum(one, axis=0, keepdims=True)


class Coarse:
    def __init__(self, coeff, nxp, nxm, nyp, nym, ylast, yedge, zstep):
        self.nxp, self.nxm, self.nyp, self.nym, self.zstep = nxp, nxm, nyp, nym, zstep
        z = iota(coeff[0].shape, 1) % 32
        zlast = z >= 32 - zstep
        zedge = (z < zstep) | zlast
        self.wp = [k + n for k, n in zip(coeff, nxp(coeff))]
        self.wm = [k + n for k, n in zip(coeff, nxm(coeff))]
        self.wy = [jnp.where(ylast, 0.0, k + nyp(k)) for k in coeff]
        self.wz = [jnp.where(zlast, 0.0, k + lanes(k, zstep)) for k in coeff]
        self.diag = []
        for k, wp, wm, wy, wz in zip(coeff, self.wp, self.wm, self.wy, self.wz):
            diag = wp + wm + (wy + nym(wy)) + (wz + lanes(wz, -zstep))
            self.diag.append(diag + (jnp.where(yedge, k, 0.0) + jnp.where(zedge, k, 0.0)))
        self.inv = [RELAX / d for d in self.diag]

    def around(self, v):
        out = []
        for c, p, m, wp, wm, wy, wz in zip(
            v, self.nxp(v), self.nxm(v), self.wp, self.wm, self.wy, self.wz
        ):
            total = wp * p + wm * m
            total = total + (wy * self.nyp(c) + self.nym(wy * c))
            out.append(total + (wz * lanes(c, self.zstep) + lanes(wz * c, -self.zstep)))
        return out

    def first(self, source):
        return [i * f for i, f in zip(self.inv, source)]

    def sweep(self, v, source):
        around = self.around(v)
        return [KEEP * c + i * (f + t) for c, i, f, t in zip(v, self.inv, source, around)]

    def sweeps(self, v, source, count):
        step = lambda _, v: tuple(self.sweep(list(v), source))
        return list(lax.fori_loop(0, count, step, tuple(v)))

    def residual(self, v, source):
        around = self.around(v)
        return [f - d * c + t for c, d, f, t in zip(v, self.diag, source, around)]


def above(c):
    return jnp.concatenate([c[8:], rows(c[:8], 1)], axis=0)


def below(c):
    return jnp.concatenate([rows(c[8:], -1), c[:8]], axis=0)


UNROLL = 8
PAD = 3


def up_kernel(
    place, gathered, v0, k0, f0, k1, f1, vmid, vlow, vhigh, out,
    k2, f2, va, vb, wxi, wxe, wyi, wye, wz2, diag2, inv2, sum2, e3,
):
    gx, gy = place[0], place[1]
    lane = iota((16, 128), 1)
    row = iota((16, 128), 0)
    group, z = lane // 32, lane % 32
    xl, yl = group // 2, group % 2
    zero = jnp.zeros((16, 128), jnp.float32)

    for ref in (k2, f2, va, vb, wxi, wxe, wyi, wye, wz2, inv2):
        for i in range(PAD):
            ref[i] = zero
            ref[32 + PAD + i] = zero
    for i in range(32):
        for c, ref in ((0, f2), (1, k2)):
            for core in range(2):
                here = pl.ds(64 * core + 2 * i + c, 8, stride=128)
                ref[i + PAD, 8 * core : 8 * core + 8] = gathered[here, :]

    def sides(c):
        up, down = lanes(c, 32), lanes(c, -32)
        inner = jnp.where(yl == 0, up, down)
        outer = jnp.where(yl == 1, above(down), below(up))
        return inner, outer

    yout = ((yl == 1) & (row == 15)) | ((yl == 0) & (row == 0))
    zlast = z == 31
    zedge = zlast | (z == 0)

    def each(field, body):
        def steps(step, turned):
            before, here = turned
            for u in range(UNROLL):
                i = PAD + UNROLL * step + u
                after = lanes(field[i + 1], 64)
                body(i, field[i], here, jnp.where(xl == 1, after, before))
                before, here = here, after
            return before, here

        lax.fori_loop(0, 32 // UNROLL, steps, (zero, lanes(field[PAD], 64)))

    def summed(k):
        k = k + lanes(k, 64)
        return k + lanes(k, 32)

    def prepare(i, k, inner, outer):
        a, b = k + inner, k + outer
        yi, yo = sides(k)
        c = k + yi
        e = jnp.where(yout, 0.0, k + yo)
        w = jnp.where(zlast, 0.0, k + lanes(k, 1))
        diag = (a + b) + (c + e) + (w + lanes(w, -1))
        diag = diag + (jnp.where(yout, k, 0.0) + jnp.where(zedge, k, 0.0))
        inv = RELAX / diag
        wxi[i], wxe[i], wyi[i], wye[i], wz2[i], diag2[i], inv2[i] = a, b, c, e, w, diag, inv
        va[i] = inv * f2[i]
        sum2[i] = summed(k)

    each(k2, prepare)

    def around2(i, c, inner, outer):
        yi, yo = sides(c)
        w = wz2[i]
        total = wxi[i] * inner + wxe[i] * outer
        total = total + (wyi[i] * yi + wye[i] * yo)
        return total + (w * lanes(c, 1) + lanes(w * c, -1))

    def sweep2(i, c, inner, outer):
        return KEEP * c + inv2[i] * (f2[i] + around2(i, c, inner, outer))

    def first2(i, c, inner, outer):
        vb[i] = sweep2(i, c, inner, outer)

    def four(q):
        t = jnp.where(group == 0, sum2[4 * q + PAD], sum2[4 * q + PAD + 1])
        t = jnp.where(group == 2, sum2[4 * q + PAD + 2], t)
        t = jnp.where(group == 3, sum2[4 * q + PAD + 3], t)
        return t + lanes(t, 1)

    c3 = [0.125 * four(q) for q in range(8)]
    each(va, first2)

    def residual2(i, c, inner, outer):
        sum2[i] = summed(f2[i] - diag2[i] * c + around2(i, c, inner, outer))

    each(vb, residual2)
    f3 = [0.5 * four(q) for q in range(8)]

    def plus3(v):
        up = [lanes(c, 32) for c in v] + [zero]
        return [jnp.where(group < 3, up[q], up[q + 1]) for q in range(8)]

    def minus3(v):
        down = [zero] + [lanes(c, -32) for c in v]
        return [jnp.where(group > 0, down[q + 1], down[q]) for q in range(8)]

    level3 = Coarse(c3, plus3, minus3, above, below, row == 15, (row == 0) | (row == 15), 2)
    v3 = level3.sweep(level3.first(f3), f3)
    r3 = level3.residual(v3, f3)

    def restrict(values, x, y, zz):
        s = [t + lanes(t, x) for t in values]
        s = [y(t) for t in s]
        return [t + lanes(t, zz) for t in s]

    cores = lambda t: t[:8] + t[8:]
    f4 = [0.5 * s for s in restrict(r3, 32, cores, 2)]
    c4 = [0.125 * s for s in restrict(c3, 32, cores, 2)]
    zero8 = zero[:8]
    row8, lane8, group8 = row[:8], lane[:8], group[:8]

    def plus4(v):
        turn = [lanes(c, 64) for c in v] + [zero8]
        return [jnp.where(group8 < 2, turn[q], turn[q + 1]) for q in range(8)]

    def minus4(v):
        turn = [zero8] + [lanes(c, 64) for c in v]
        return [jnp.where(group8 < 2, turn[q], turn[q + 1]) for q in range(8)]

    def next_rows(n):
        return lambda c: rows(c, n)

    level4 = Coarse(
        c4, plus4, minus4, next_rows(1), next_rows(-1), row8 == 7, (row8 == 0) | (row8 == 7), 4
    )
    v4 = level4.sweep(level4.first(f4), f4)
    r4 = level4.residual(v4, f4)

    pair = lambda t: t + rows(t, 1)
    f5 = [0.5 * s for s in restrict(r4, 64, pair, 4)]
    c5 = [0.125 * s for s in restrict(c4, 64, pair, 4)]
    level5 = Coarse(
        c5,
        lambda v: v[1:] + [zero8],
        lambda v: [zero8] + v[:-1],
        next_rows(2),
        next_rows(-2),
        row8 >= 6,
        (row8 < 2) | (row8 >= 6),
        8,
    )
    v5 = level5.sweeps(level5.first(f5), f5, COARSE_SWEEPS - 1)

    def spread(c, bit):
        return jnp.where((iota(c.shape, 1) & bit) != 0, lanes(c, -bit), c)

    v5 = [jnp.where((row8 & 1) != 0, rows(c, -1), c) for c in v5]
    v4 = [c + spread(e, 4) for c, e in zip(v4, v5)]
    v4 = level4.sweeps(v4, f4, 2)

    v4 = [spread(jnp.where(group8 % 2 == 1, lanes(c, -32), c), 2) for c in v4]
    v3 = [c + jnp.concatenate([e, e], axis=0) for c, e in zip(v3, v4)]
    v3 = level3.sweeps(v3, f3, 2)

    for q in range(8):
        e3[q] = spread(v3[q], 1)
    for t in range(5):
        p = gx + t - 2
        inside = (p >= 0) & (p < 32)
        p = jnp.clip(p, 0, 31)
        e = jnp.where(group == jnp.where(inside, p % 4, -1), e3[p // 4], 0.0)
        va[gx + t - 2 + PAD] = vb[gx + t - 2 + PAD] + summed(e)

    def some(read, write, first, end):
        turned = [lanes(read[gx + t + PAD], 64) for t in range(first - 1, end + 1)]
        for u, t in enumerate(range(first, end)):
            i = gx + t + PAD
            outer = jnp.where(xl == 1, turned[u + 2], turned[u])
            write[i] = sweep2(i, read[i], turned[u + 1], outer)

    some(va, vb, -2, 3)
    some(vb, va, -1, 2)

    window = jnp.concatenate([va[gx + t + PAD] for t in range(-1, 2)], axis=1)
    shape = (ROWS, 16)
    column = 2 * (iota(shape, 1) % 8) + iota(shape, 1) // 8
    choose = jnp.where(column == gy - 1 + iota(shape, 0) // 8, 1.0, 0.0)
    window = jnp.dot(choose, window, precision=EXACT, preferred_element_type=jnp.float32)
    wide = jnp.concatenate([window[:, 128 * a : 128 * a + 128] for a in range(3)], axis=0)
    shape = (3 * ROWS, 128)
    wide = jnp.where((iota(shape, 1) // 32) % 2 == (iota(shape, 0) // 4) % 2, wide, 0.0)
    source_lane, target = iota((128, 256), 0), iota((128, 256), 1)
    place_it = (source_lane // 64 == target // 128) & (source_lane % 32 == (target % 128) // 4)
    wide = jnp.dot(
        wide, jnp.where(place_it, 1.0, 0.0), precision=EXACT, preferred_element_type=jnp.float32
    )

    def correction(i):
        a, x = (i + 4) // 4, ((i + 4) % 4) // 2
        return wide[ROWS * a : ROWS * a + ROWS, 128 * x : 128 * x + 128]

    middle = Window(2, (-2, 6))
    middle.weights(Stored(k1, -3))
    source = Stored(f1, -2)
    upper_half = iota((8, 128), 0) >= 4
    second = (iota((ROWS, 128), 0) & 2) != 0

    def received(i):
        n = 2 * i + 8
        c = [jnp.where(upper_half, r[n + 1 : n + 2], r[n : n + 1]) for r in (vlow, vmid, vhigh)]
        c = jnp.concatenate(c, axis=0)
        return jnp.where(second, lanes(c, 1), c)

    v = {i: received(i) + correction(i) for i in range(-3, 7)}
    v = middle.sweep(v, source, -2, 6)
    v = middle.sweep(v, source, -1, 5)

    odd_lane = iota((ROWS, 128), 1) % 2 == 1
    odd_row = iota((ROWS, 128), 0) % 2 == 1
    fine = Window(1, (-1, 9))
    fine.weights(Stored(k0, -2))
    source = Stored(f0, -1)
    base = Stored(v0, -2)
    spread1 = {}
    for i in range(-1, 5):
        c = jnp.where(odd_lane, lanes(v[i], -1), v[i])
        spread1[i] = jnp.where(odd_row, rows(c, -1), c)
    v = {i: base[i] + spread1[i // 2] for i in range(-2, 10)}
    v = fine.sweep(v, source, -1, 9)
    v = fine.sweep(v, source, 0, 8)
    for i in range(8):
        out[i] = v[i][8:16]


def f32(*shape):
    return jax.ShapeDtypeStruct(shape, jnp.float32)


def shift(x, axis, by):
    count = lax.axis_size(axis)
    return lax.ppermute(x, axis, [(i, i + by) for i in range(count) if 0 <= i + by < count])


def to_all(x, axis):
    copies = jnp.broadcast_to(x[None], (lax.axis_size(axis),) + x.shape)
    return lax.all_to_all(copies, axis, 0, 0)


def shards(right_side, coefficient, previous):
    gx, gy = lax.axis_index("gx"), lax.axis_index("gy")
    place = jnp.stack([gx, gy]).astype(jnp.int32)
    own = jnp.stack([right_side, coefficient, previous])
    mid = jnp.concatenate(
        [shift(own[:, -HALO:], "gx", 1), own, shift(own[:, :HALO], "gx", -1)], axis=1
    )
    low, high = shift(mid, "gy", 1), shift(mid, "gy", -1)

    params = pltpu.CompilerParams(vmem_limit_bytes=VMEM)
    scalars = pl.BlockSpec(memory_space=pltpu.SMEM)
    array = pl.BlockSpec(memory_space=pltpu.VMEM)
    packed, v0, k0, f0, k1, f1 = pl.pallas_call(
        down_kernel,
        in_specs=[array] * 3,
        out_shape=(
            f32(10, 128),
            f32(12, ROWS, 128),
            f32(12, ROWS, 128),
            f32(10, ROWS, 128),
            f32(10, ROWS, 128),
            f32(8, ROWS, 128),
        ),
        compiler_params=params,
        name="down",
    )(mid, low, high)

    blocks = to_all(packed.reshape(1, 1280), "gx")
    gathered = to_all(blocks[:, :, :256].reshape(64, 128), "gy").reshape(1024, 128)
    v1 = jnp.pad(blocks[:, 0, 256:], ((1, 1), (0, 0)))
    vmid = lax.dynamic_slice(v1, (gx, jnp.int32(0)), (3, 1024)).reshape(24, 128)
    vlow, vhigh = shift(vmid, "gy", 1), shift(vmid, "gy", -1)

    plane = pltpu.VMEM((32 + 2 * PAD, 16, 128), jnp.float32)
    return pl.pallas_call(
        up_kernel,
        in_specs=[scalars] + [array] * 9,
        out_shape=f32(8, 8, 128),
        scratch_shapes=[plane] * 12 + [pltpu.VMEM((8, 16, 128), jnp.float32)],
        compiler_params=params,
        name="up",
    )(place, gathered, v0, k0, f0, k1, f1, vmid, vlow, vhigh)


def solution(mesh):
    spec = P("gx", "gy", None)
    return jax.shard_map(
        shards, mesh=mesh, in_specs=(spec,) * 3, out_specs=spec, check_vma=False
    )
```

```python
import jax
import jax.numpy as jnp
from jax import lax
from jax.experimental import pallas as pl
from jax.experimental.pallas import tpu as pltpu
from jax.sharding import PartitionSpec as P

RELAX = 0.8
KEEP = 1.0 - RELAX
HALO = 7
ROWS = 24
COARSE_SWEEPS = 8
VMEM = 48 * 1024 * 1024


def lanes(x, n):
    return pltpu.roll(x, (-n) % x.shape[1], axis=1)


def rows(x, n):
    return pltpu.roll(x, (-n) % x.shape[0], axis=0)


def iota(shape, dim):
    return lax.broadcasted_iota(jnp.int32, shape, dim)


class Window:
    def __init__(self, step, planes):
        self.step = step
        self.planes = planes

    def given(self, wx, wy, wz, inv):
        first = self.planes[0]
        self.wx, self.wy = Stored(wx, first - 1), Stored(wy, first)
        self.wz, self.inv = Stored(wz, first), Stored(inv, first)

    def hand_on(self, planes, wx, wy, wz, inv):
        first, end = planes
        for i in range(first - 1, end):
            wx[i - first + 1] = self.wx[i]
        for i in range(first, end):
            wy[i - first], wz[i - first], inv[i - first] = self.wy[i], self.wz[i], self.inv[i]

    def weights(self, coeff):
        first, end = self.planes
        lane = iota((ROWS, 128), 1)
        last = lane >= 128 - self.step
        edge = (lane < self.step) | last
        self.wx, self.wy, self.wz, self.diag, self.inv = {}, {}, {}, {}, {}
        for i in range(first - 1, end):
            self.wx[i] = coeff[i] + coeff[i + 1]
        for i in range(first, end):
            k = coeff[i]
            wy = k + rows(k, self.step)
            wz = jnp.where(last, 0.0, k + lanes(k, self.step))
            diag = self.wx[i] + self.wx[i - 1] + (wy + rows(wy, -self.step))
            diag = diag + (wz + lanes(wz, -self.step)) + jnp.where(edge, k, 0.0)
            self.wy[i], self.wz[i], self.diag[i] = wy, wz, diag
            self.inv[i] = jnp.where(k > 0.0, RELAX / diag, 0.0)

    def around(self, v, i):
        c = v[i]
        wy, wz, step = self.wy[i], self.wz[i], self.step
        total = self.wx[i] * v[i + 1] + self.wx[i - 1] * v[i - 1]
        total = total + (wy * rows(c, step) + rows(wy * c, -step))
        return total + (wz * lanes(c, step) + lanes(wz * c, -step))

    def sweep(self, v, source, first, end):
        return {
            i: KEEP * v[i] + self.inv[i] * (source[i] + self.around(v, i)) for i in range(first, end)
        }

    def residual(self, v, source, first, end):
        return {i: source[i] - self.diag[i] * v[i] + self.around(v, i) for i in range(first, end)}


class Stored:
    def __init__(self, ref, first):
        self.ref, self.first = ref, first

    def __getitem__(self, i):
        return self.ref[i - self.first]

    def __setitem__(self, i, value):
        self.ref[i - self.first] = value


def block_sum(low, high, step):
    s = low + high
    s = s + rows(s, step)
    return s + lanes(s, step)


def down_kernel(
    mid, low, high, packed, v0_out, f0_out, f1_out, wx0, wy0, wz0, inv0, wx1, wy1, wz1, inv1
):
    def field(which):
        return {
            i - HALO: jnp.concatenate([low[which, i], mid[which, i], high[which, i]], axis=0)
            for i in range(mid.shape[1])
        }

    source, coeff, v = field(0), field(1), field(2)
    source = {i: 2.0 * source[i] for i in range(-6, 14)}

    fine = Window(1, (-6, 14))
    fine.weights(coeff)
    v = fine.sweep(v, source, -6, 14)
    v = fine.sweep(v, source, -5, 13)
    for i in range(-2, 10):
        v0_out[i + 2] = v[i]
    for i in range(-1, 9):
        f0_out[i + 1] = source[i]
    fine.hand_on((-1, 9), wx0, wy0, wz0, inv0)
    r = fine.residual(v, source, -4, 12)

    source = {i: 0.5 * block_sum(r[2 * i], r[2 * i + 1], 1) for i in range(-2, 6)}
    coeff = {i: 0.125 * block_sum(coeff[2 * i], coeff[2 * i + 1], 1) for i in range(-3, 7)}
    for i in range(-2, 6):
        f1_out[i + 2] = source[i]
    middle = Window(2, (-2, 6))
    middle.weights(coeff)
    middle.hand_on((-2, 6), wx1, wy1, wz1, inv1)
    v = {i: middle.inv[i] * source[i] for i in range(-2, 6)}
    v = middle.sweep(v, source, -1, 5)
    even = iota((8, 128), 1) % 2 == 0
    for i in range(4):
        c = v[i][8:16]
        c = jnp.where(even, c, lanes(rows(c, 2), -1))
        packed[2 * i + 2 : 2 * i + 3, :] = c[0:1]
        packed[2 * i + 3 : 2 * i + 4, :] = c[4:5]
    r = middle.residual(v, source, 0, 4)

    source = [0.5 * block_sum(r[2 * i], r[2 * i + 1], 2)[8:16] for i in range(2)]
    coeff = [0.125 * block_sum(coeff[2 * i], coeff[2 * i + 1], 2)[8:16] for i in range(2)]
    lane, row = iota((8, 128), 1), iota((8, 128), 0)
    group = lane // 32
    pick = 4 * (lane % 32)
    for c, planes in enumerate((source, coeff)):
        dense = [jnp.take_along_axis(t, pick, axis=1) for t in planes]
        dense = jnp.where(group < 2, dense[0], dense[1])
        dense = jnp.where(row == 4 * (group % 2), dense, 0.0)
        packed[c : c + 1, :] = jnp.sum(dense, axis=0, keepdims=True)


class Coarse:
    def __init__(self, coeff, nxp, nxm, nyp, nym, ylast, yedge, zstep):
        self.nxp, self.nxm, self.nyp, self.nym, self.zstep = nxp, nxm, nyp, nym, zstep
        z = iota(coeff[0].shape, 1) % 32
        zlast = z >= 32 - zstep
        zedge = (z < zstep) | zlast
        self.wp = [k + n for k, n in zip(coeff, nxp(coeff))]
        self.wm = [k + n for k, n in zip(coeff, nxm(coeff))]
        self.wy = [jnp.where(ylast, 0.0, k + nyp(k)) for k in coeff]
        self.wz = [jnp.where(zlast, 0.0, k + lanes(k, zstep)) for k in coeff]
        self.diag = []
        for k, wp, wm, wy, wz in zip(coeff, self.wp, self.wm, self.wy, self.wz):
            diag = wp + wm + (wy + nym(wy)) + (wz + lanes(wz, -zstep))
            self.diag.append(diag + (jnp.where(yedge, k, 0.0) + jnp.where(zedge, k, 0.0)))
        self.inv = [RELAX / d for d in self.diag]

    def around(self, v):
        out = []
        for c, p, m, wp, wm, wy, wz in zip(
            v, self.nxp(v), self.nxm(v), self.wp, self.wm, self.wy, self.wz
        ):
            total = wp * p + wm * m
            total = total + (wy * self.nyp(c) + self.nym(wy * c))
            out.append(total + (wz * lanes(c, self.zstep) + lanes(wz * c, -self.zstep)))
        return out

    def first(self, source):
        return [i * f for i, f in zip(self.inv, source)]

    def sweep(self, v, source):
        around = self.around(v)
        return [KEEP * c + i * (f + t) for c, i, f, t in zip(v, self.inv, source, around)]

    def sweeps(self, v, source, count):
        step = lambda _, v: tuple(self.sweep(list(v), source))
        return list(lax.fori_loop(0, count, step, tuple(v)))

    def residual(self, v, source):
        around = self.around(v)
        return [f - d * c + t for c, d, f, t in zip(v, self.diag, source, around)]


def above(c):
    return jnp.concatenate([c[8:], rows(c[:8], 1)], axis=0)


def below(c):
    return jnp.concatenate([rows(c[8:], -1), c[:8]], axis=0)


UNROLL = 10
PAD = 3


def up_kernel(
    place, gathered, v0, f0, f1, wx0, wy0, wz0, inv0, wx1, wy1, wz1, inv1, vlow, vmid, vhigh, out,
    k2, f2, va, vb, wxi, wxe, wyi, wye, wz2, diag2, inv2, sumk, sumr, e3,
):
    gx, gy = place[0], place[1]
    lane = iota((16, 128), 1)
    row = iota((16, 128), 0)
    group, z = lane // 32, lane % 32
    xl, yl = group // 2, group % 2
    zero = jnp.zeros((16, 128), jnp.float32)

    for ref in (k2, f2, va, vb, wxi, wxe, wyi, wye, wz2, inv2):
        for i in range(PAD):
            ref[i] = zero
            ref[32 + PAD + i] = zero
    for i in range(32):
        for c, ref in ((0, f2), (1, k2)):
            for core in range(2):
                here = pl.ds(32 * i + 2 * core + c, 8, stride=4)
                ref[i + PAD, 8 * core : 8 * core + 8] = gathered[here, :]

    def sides(c):
        up, down = lanes(c, 32), lanes(c, -32)
        inner = jnp.where(yl == 0, up, down)
        outer = jnp.where(yl == 1, above(down), below(up))
        return inner, outer

    yout = ((yl == 1) & (row == 15)) | ((yl == 0) & (row == 0))
    zlast = z == 31
    zedge = zlast | (z == 0)

    def advance(i, field, turned, body):
        before, here = turned
        after = lanes(field[i + 1], 64)
        body(i, field[i], here, jnp.where(xl == 1, after, before))
        return here, after

    def summed(k):
        k = k + lanes(k, 64)
        return k + lanes(k, 32)

    def prepare(i, k, inner, outer):
        a, b = k + inner, k + outer
        yi, yo = sides(k)
        c = k + yi
        e = jnp.where(yout, 0.0, k + yo)
        w = jnp.where(zlast, 0.0, k + lanes(k, 1))
        diag = (a + b) + (c + e) + (w + lanes(w, -1))
        diag = diag + (jnp.where(yout, k, 0.0) + jnp.where(zedge, k, 0.0))
        inv = RELAX / diag
        wxi[i], wxe[i], wyi[i], wye[i], wz2[i], diag2[i], inv2[i] = a, b, c, e, w, diag, inv
        va[i] = inv * f2[i]
        sumk[i] = summed(k)

    def around2(i, c, inner, outer):
        yi, yo = sides(c)
        w = wz2[i]
        total = wxi[i] * inner + wxe[i] * outer
        total = total + (wyi[i] * yi + wye[i] * yo)
        return total + (w * lanes(c, 1) + lanes(w * c, -1))

    def sweep2(i, c, inner, outer):
        return KEEP * c + inv2[i] * (f2[i] + around2(i, c, inner, outer))

    def first2(i, c, inner, outer):
        vb[i] = sweep2(i, c, inner, outer)

    def residual2(i, c, inner, outer):
        sumr[i] = summed(f2[i] - diag2[i] * c + around2(i, c, inner, outer))

    def three(i, state):
        ofk, ofa, ofb = state
        ofk = advance(i, k2, ofk, prepare)
        ofa = advance(i - 1, va, ofa, first2)
        return ofk, ofa, advance(i - 2, vb, ofb, residual2)

    ofk = (zero, lanes(k2[PAD], 64))
    ofk = advance(PAD, k2, ofk, prepare)
    ofk = advance(PAD + 1, k2, ofk, prepare)
    ofa = advance(PAD, va, (zero, lanes(va[PAD], 64)), first2)
    ofb = (zero, lanes(vb[PAD], 64))

    def steps(step, state):
        for u in range(UNROLL):
            state = three(PAD + 2 + UNROLL * step + u, state)
        return state

    _, ofa, ofb = lax.fori_loop(0, 30 // UNROLL, steps, (ofk, ofa, ofb))
    advance(PAD + 31, va, ofa, first2)
    ofb = advance(PAD + 30, vb, ofb, residual2)
    advance(PAD + 31, vb, ofb, residual2)

    def four(sums, q):
        t = jnp.where(group == 0, sums[4 * q + PAD], sums[4 * q + PAD + 1])
        t = jnp.where(group == 2, sums[4 * q + PAD + 2], t)
        t = jnp.where(group == 3, sums[4 * q + PAD + 3], t)
        return t + lanes(t, 1)

    c3 = [0.125 * four(sumk, q) for q in range(8)]
    f3 = [0.5 * four(sumr, q) for q in range(8)]

    def plus3(v):
        up = [lanes(c, 32) for c in v] + [zero]
        return [jnp.where(group < 3, up[q], up[q + 1]) for q in range(8)]

    def minus3(v):
        down = [zero] + [lanes(c, -32) for c in v]
        return [jnp.where(group > 0, down[q + 1], down[q]) for q in range(8)]

    level3 = Coarse(c3, plus3, minus3, above, below, row == 15, (row == 0) | (row == 15), 2)
    v3 = level3.sweep(level3.first(f3), f3)
    r3 = level3.residual(v3, f3)

    def restrict(values, x, y, zz):
        s = [t + lanes(t, x) for t in values]
        s = [y(t) for t in s]
        return [t + lanes(t, zz) for t in s]

    cores = lambda t: t[:8] + t[8:]
    f4 = [0.5 * s for s in restrict(r3, 32, cores, 2)]
    c4 = [0.125 * s for s in restrict(c3, 32, cores, 2)]
    zero8 = zero[:8]
    row8, lane8, group8 = row[:8], lane[:8], group[:8]

    def plus4(v):
        turn = [lanes(c, 64) for c in v] + [zero8]
        return [jnp.where(group8 < 2, turn[q], turn[q + 1]) for q in range(8)]

    def minus4(v):
        turn = [zero8] + [lanes(c, 64) for c in v]
        return [jnp.where(group8 < 2, turn[q], turn[q + 1]) for q in range(8)]

    def next_rows(n):
        return lambda c: rows(c, n)

    level4 = Coarse(
        c4, plus4, minus4, next_rows(1), next_rows(-1), row8 == 7, (row8 == 0) | (row8 == 7), 4
    )
    v4 = level4.sweep(level4.first(f4), f4)
    r4 = level4.residual(v4, f4)

    pair = lambda t: t + rows(t, 1)
    f5 = [0.5 * s for s in restrict(r4, 64, pair, 4)]
    c5 = [0.125 * s for s in restrict(c4, 64, pair, 4)]
    level5 = Coarse(
        c5,
        lambda v: v[1:] + [zero8],
        lambda v: [zero8] + v[:-1],
        next_rows(2),
        next_rows(-2),
        row8 >= 6,
        (row8 < 2) | (row8 >= 6),
        8,
    )
    v5 = level5.sweeps(level5.first(f5), f5, COARSE_SWEEPS - 1)

    def spread(c, bit):
        return jnp.where((iota(c.shape, 1) & bit) != 0, lanes(c, -bit), c)

    v5 = [jnp.where((row8 & 1) != 0, rows(c, -1), c) for c in v5]
    v4 = [c + spread(e, 4) for c, e in zip(v4, v5)]
    v4 = level4.sweeps(v4, f4, 2)

    v4 = [spread(jnp.where(group8 % 2 == 1, lanes(c, -32), c), 2) for c in v4]
    v3 = [c + jnp.concatenate([e, e], axis=0) for c, e in zip(v3, v4)]
    v3 = level3.sweeps(v3, f3, 2)

    for q in range(8):
        e3[q] = spread(v3[q], 1)
    for t in range(5):
        p = gx + t - 2
        inside = (p >= 0) & (p < 32)
        p = jnp.clip(p, 0, 31)
        e = jnp.where(group == jnp.where(inside, p % 4, -1), e3[p // 4], 0.0)
        va[gx + t - 2 + PAD] = vb[gx + t - 2 + PAD] + summed(e)

    def some(read, write, first, end):
        turned = [lanes(read[gx + t + PAD], 64) for t in range(first - 1, end + 1)]
        for u, t in enumerate(range(first, end)):
            i = gx + t + PAD
            outer = jnp.where(xl == 1, turned[u + 2], turned[u])
            write[i] = sweep2(i, read[i], turned[u + 1], outer)

    some(va, vb, -2, 3)
    some(vb, va, -1, 2)

    lane8 = iota((8, 128), 1)
    pick = 32 * (iota((8, 128), 0) // 4) + lane8 // 4
    wide = {}
    for t in range(-1, 2):
        for x in range(2):
            parts = []
            for b in range(-1, 2):
                y = gy + b
                inside = (y >= 0) & (y < 16)
                y = jnp.clip(y, 0, 15)
                line = va[gx + t + PAD, pl.ds(8 * (y % 2) + y // 2, 1), :]
                line = jnp.broadcast_to(jnp.where(inside, line, 0.0), (8, 128))
                parts.append(jnp.take_along_axis(line, 64 * x + pick, axis=1))
            wide[t, x] = jnp.concatenate(parts, axis=0)

    def correction(i):
        return wide[i // 4, (i % 4) // 2]

    middle = Window(2, (-2, 6))
    middle.given(wx1, wy1, wz1, inv1)
    source = Stored(f1, -2)
    upper_half = iota((8, 128), 0) >= 4
    second = (iota((ROWS, 128), 0) & 2) != 0

    def received(i):
        r, n = (vlow, vmid, vhigh)[(i + 4) // 4], 2 * (i % 4)
        c = [jnp.where(upper_half, r[b + 1 : b + 2], r[b : b + 1]) for b in (n, n + 8, n + 16)]
        c = jnp.concatenate(c, axis=0)
        return jnp.where(second, lanes(c, 1), c)

    v = {i: received(i) + correction(i) for i in range(-3, 7)}
    v = middle.sweep(v, source, -2, 6)
    v = middle.sweep(v, source, -1, 5)

    odd_lane = iota((ROWS, 128), 1) % 2 == 1
    odd_row = iota((ROWS, 128), 0) % 2 == 1
    fine = Window(1, (-1, 9))
    fine.given(wx0, wy0, wz0, inv0)
    source = Stored(f0, -1)
    base = Stored(v0, -2)
    spread1 = {}
    for i in range(-1, 5):
        c = jnp.where(odd_lane, lanes(v[i], -1), v[i])
        spread1[i] = jnp.where(odd_row, rows(c, -1), c)
    v = {i: base[i] + spread1[i // 2] for i in range(-2, 10)}
    v = fine.sweep(v, source, -1, 9)
    v = fine.sweep(v, source, 0, 8)
    for i in range(8):
        out[i] = v[i][8:16]


WINDOW_PLANES = (12, 10, 8, 11, 10, 10, 10, 9, 8, 8, 8)


def f32(*shape):
    return jax.ShapeDtypeStruct(shape, jnp.float32)


def shift(x, axis, by):
    count = lax.axis_size(axis)
    return lax.ppermute(x, axis, [(i, i + by) for i in range(count) if 0 <= i + by < count])


def to_all(x, axis):
    copies = jnp.broadcast_to(x[None], (lax.axis_size(axis),) + x.shape)
    return lax.all_to_all(copies, axis, 0, 0)


def shards(right_side, coefficient, previous):
    gx, gy = lax.axis_index("gx"), lax.axis_index("gy")
    place = jnp.stack([gx, gy]).astype(jnp.int32)
    own = jnp.stack([right_side, coefficient, previous])
    mid = jnp.concatenate(
        [shift(own[:, -HALO:], "gx", 1), own, shift(own[:, :HALO], "gx", -1)], axis=1
    )
    low, high = shift(mid, "gy", 1), shift(mid, "gy", -1)

    params = pltpu.CompilerParams(vmem_limit_bytes=VMEM)
    scalars = pl.BlockSpec(memory_space=pltpu.SMEM)
    array = pl.BlockSpec(memory_space=pltpu.VMEM)
    packed, *window = pl.pallas_call(
        down_kernel,
        in_specs=[array] * 3,
        out_shape=(f32(10, 128),) + tuple(f32(n, ROWS, 128) for n in WINDOW_PLANES),
        compiler_params=params,
        name="down",
    )(mid, low, high)

    blocks = to_all(packed.reshape(1, 1280), "gy")
    gathered = to_all(blocks[:, :, :256].reshape(32, 128), "gx").reshape(1024, 128)
    v1 = jnp.pad(blocks[:, 0, 256:], ((1, 1), (0, 0)))
    vmid = lax.dynamic_slice(v1, (gy, jnp.int32(0)), (3, 1024)).reshape(24, 128)
    vlow, vhigh = shift(vmid, "gx", 1), shift(vmid, "gx", -1)

    plane = pltpu.VMEM((32 + 2 * PAD, 16, 128), jnp.float32)
    return pl.pallas_call(
        up_kernel,
        in_specs=[scalars] + [array] * (4 + len(WINDOW_PLANES)),
        out_shape=f32(8, 8, 128),
        scratch_shapes=[plane] * 13 + [pltpu.VMEM((8, 16, 128), jnp.float32)],
        compiler_params=params,
        name="up",
    )(place, gathered, *window, vlow, vmid, vhigh)


def solution(mesh):
    spec = P("gx", "gy", None)
    return jax.shard_map(
        shards, mesh=mesh, in_specs=(spec,) * 3, out_specs=spec, check_vma=False
    )
```

```python
import jax
import jax.numpy as jnp
from jax import lax
from jax.experimental import pallas as pl
from jax.experimental.pallas import tpu as pltpu
from jax.sharding import PartitionSpec as P

RELAX = 0.8
KEEP = 1.0 - RELAX
HALO = 7
ROWS = 24
COARSE_SWEEPS = 8
VMEM = 48 * 1024 * 1024


def lanes(x, n):
    return pltpu.roll(x, (-n) % x.shape[1], axis=1)


def rows(x, n):
    return pltpu.roll(x, (-n) % x.shape[0], axis=0)


def iota(shape, dim):
    return lax.broadcasted_iota(jnp.int32, shape, dim)


class Window:
    def __init__(self, step, planes):
        self.step = step
        self.planes = planes

    def given(self, wx, wy, wz, inv):
        first = self.planes[0]
        self.wx, self.wy = Stored(wx, first - 1), Stored(wy, first)
        self.wz, self.inv = Stored(wz, first), Stored(inv, first)

    def hand_on(self, planes, wx, wy, wz, inv):
        first, end = planes
        for i in range(first - 1, end):
            wx[i - first + 1] = self.wx[i]
        for i in range(first, end):
            wy[i - first], wz[i - first], inv[i - first] = self.wy[i], self.wz[i], self.inv[i]

    def weights(self, coeff):
        first, end = self.planes
        lane = iota((ROWS, 128), 1)
        last = lane >= 128 - self.step
        edge = (lane < self.step) | last
        self.wx, self.wy, self.wz, self.diag, self.inv = {}, {}, {}, {}, {}
        for i in range(first - 1, end):
            self.wx[i] = coeff[i] + coeff[i + 1]
        for i in range(first, end):
            k = coeff[i]
            wy = k + rows(k, self.step)
            wz = jnp.where(last, 0.0, k + lanes(k, self.step))
            diag = self.wx[i] + self.wx[i - 1] + (wy + rows(wy, -self.step))
            diag = diag + (wz + lanes(wz, -self.step)) + jnp.where(edge, k, 0.0)
            self.wy[i], self.wz[i], self.diag[i] = wy, wz, diag
            self.inv[i] = jnp.where(k > 0.0, RELAX / diag, 0.0)

    def around(self, v, i):
        c = v[i]
        wy, wz, step = self.wy[i], self.wz[i], self.step
        total = self.wx[i] * v[i + 1] + self.wx[i - 1] * v[i - 1]
        total = total + (wy * rows(c, step) + rows(wy * c, -step))
        return total + (wz * lanes(c, step) + lanes(wz * c, -step))

    def sweep(self, v, source, first, end):
        return {
            i: KEEP * v[i] + self.inv[i] * (source[i] + self.around(v, i)) for i in range(first, end)
        }

    def residual(self, v, source, first, end):
        return {i: source[i] - self.diag[i] * v[i] + self.around(v, i) for i in range(first, end)}


class Stored:
    def __init__(self, ref, first):
        self.ref, self.first = ref, first

    def __getitem__(self, i):
        return self.ref[i - self.first]

    def __setitem__(self, i, value):
        self.ref[i - self.first] = value


def block_sum(low, high, step):
    s = low + high
    s = s + rows(s, step)
    return s + lanes(s, step)


def core_mask(rows_of):
    core = lax.rem(lax.axis_index("gy"), 2)
    return jnp.broadcast_to(core, (rows_of, 128)) == 0


def joined(first, mid, near, far):
    return jnp.concatenate([jnp.where(first, far, near), mid, jnp.where(first, near, far)], axis=0)


def down_kernel(
    mid, near, far, packed, v0_out, f0_out, f1_out, wx0, wy0, wz0, inv0, wx1, wy1, wz1, inv1
):
    first = core_mask(8)

    def field(which):
        return {
            i - HALO: joined(first, mid[which, i], near[which, i], far[which, i])
            for i in range(mid.shape[1])
        }

    source, coeff, v = field(0), field(1), field(2)
    source = {i: 2.0 * source[i] for i in range(-6, 14)}

    fine = Window(1, (-6, 14))
    fine.weights(coeff)
    v = fine.sweep(v, source, -6, 14)
    v = fine.sweep(v, source, -5, 13)
    for i in range(-2, 10):
        v0_out[i + 2] = v[i]
    for i in range(-1, 9):
        f0_out[i + 1] = source[i]
    fine.hand_on((-1, 9), wx0, wy0, wz0, inv0)
    r = fine.residual(v, source, -4, 12)

    source = {i: 0.5 * block_sum(r[2 * i], r[2 * i + 1], 1) for i in range(-2, 6)}
    coeff = {i: 0.125 * block_sum(coeff[2 * i], coeff[2 * i + 1], 1) for i in range(-3, 7)}
    for i in range(-2, 6):
        f1_out[i + 2] = source[i]
    middle = Window(2, (-2, 6))
    middle.weights(coeff)
    middle.hand_on((-2, 6), wx1, wy1, wz1, inv1)
    v = {i: middle.inv[i] * source[i] for i in range(-2, 6)}
    v = middle.sweep(v, source, -1, 5)
    even = iota((8, 128), 1) % 2 == 0
    for i in range(4):
        c = v[i][8:16]
        c = jnp.where(even, c, lanes(rows(c, 2), -1))
        packed[2 * i + 2 : 2 * i + 3, :] = c[0:1]
        packed[2 * i + 3 : 2 * i + 4, :] = c[4:5]
    r = middle.residual(v, source, 0, 4)

    source = [0.5 * block_sum(r[2 * i], r[2 * i + 1], 2)[8:16] for i in range(2)]
    coeff = [0.125 * block_sum(coeff[2 * i], coeff[2 * i + 1], 2)[8:16] for i in range(2)]
    lane, row = iota((8, 128), 1), iota((8, 128), 0)
    group = lane // 32
    pick = 4 * (lane % 32)
    for c, planes in enumerate((source, coeff)):
        dense = [jnp.take_along_axis(t, pick, axis=1) for t in planes]
        dense = jnp.where(group < 2, dense[0], dense[1])
        dense = jnp.where(row == 4 * (group % 2), dense, 0.0)
        packed[c : c + 1, :] = jnp.sum(dense, axis=0, keepdims=True)


class Coarse:
    def __init__(self, coeff, nxp, nxm, nyp, nym, ylast, yedge, zstep):
        self.nxp, self.nxm, self.nyp, self.nym, self.zstep = nxp, nxm, nyp, nym, zstep
        z = iota(coeff[0].shape, 1) % 32
        zlast = z >= 32 - zstep
        zedge = (z < zstep) | zlast
        self.wp = [k + n for k, n in zip(coeff, nxp(coeff))]
        self.wm = [k + n for k, n in zip(coeff, nxm(coeff))]
        self.wy = [jnp.where(ylast, 0.0, k + nyp(k)) for k in coeff]
        self.wz = [jnp.where(zlast, 0.0, k + lanes(k, zstep)) for k in coeff]
        self.diag = []
        for k, wp, wm, wy, wz in zip(coeff, self.wp, self.wm, self.wy, self.wz):
            diag = wp + wm + (wy + nym(wy)) + (wz + lanes(wz, -zstep))
            self.diag.append(diag + (jnp.where(yedge, k, 0.0) + jnp.where(zedge, k, 0.0)))
        self.inv = [RELAX / d for d in self.diag]

    def around(self, v):
        out = []
        for c, p, m, wp, wm, wy, wz in zip(
            v, self.nxp(v), self.nxm(v), self.wp, self.wm, self.wy, self.wz
        ):
            total = wp * p + wm * m
            total = total + (wy * self.nyp(c) + self.nym(wy * c))
            out.append(total + (wz * lanes(c, self.zstep) + lanes(wz * c, -self.zstep)))
        return out

    def first(self, source):
        return [i * f for i, f in zip(self.inv, source)]

    def sweep(self, v, source):
        around = self.around(v)
        return [KEEP * c + i * (f + t) for c, i, f, t in zip(v, self.inv, source, around)]

    def sweeps(self, v, source, count):
        step = lambda _, v: tuple(self.sweep(list(v), source))
        return list(lax.fori_loop(0, count, step, tuple(v)))

    def residual(self, v, source):
        around = self.around(v)
        return [f - d * c + t for c, d, f, t in zip(v, self.diag, source, around)]


def above(c):
    return jnp.concatenate([c[8:], rows(c[:8], 1)], axis=0)


def below(c):
    return jnp.concatenate([rows(c[8:], -1), c[:8]], axis=0)


UNROLL = 10
PAD = 3


def up_kernel(
    mine, other, v0, f0, f1, wx0, wy0, wz0, inv0, wx1, wy1, wz1, inv1, vmid, vnear, vfar, out,
    k2, f2, va, vb, wxi, wxe, wyi, wye, wz2, diag2, inv2, sumk, sumr, e3,
):
    gx, gy = lax.axis_index("gx"), lax.axis_index("gy")
    first = core_mask(8)
    lane = iota((16, 128), 1)
    row = iota((16, 128), 0)
    group, z = lane // 32, lane % 32
    xl, yl = group // 2, group % 2
    zero = jnp.zeros((16, 128), jnp.float32)

    for ref in (k2, f2, va, vb, wxi, wxe, wyi, wye, wz2, inv2):
        for i in range(PAD):
            ref[i] = zero
            ref[32 + PAD + i] = zero
    for i in range(32):
        for c, ref in ((0, f2), (1, k2)):
            here = pl.ds(2 * i + c, 8, stride=64)
            a, b = mine[here, :], other[here, :]
            ref[i + PAD, :8] = jnp.where(first, a, b)
            ref[i + PAD, 8:] = jnp.where(first, b, a)

    def sides(c):
        up, down = lanes(c, 32), lanes(c, -32)
        inner = jnp.where(yl == 0, up, down)
        outer = jnp.where(yl == 1, above(down), below(up))
        return inner, outer

    yout = ((yl == 1) & (row == 15)) | ((yl == 0) & (row == 0))
    zlast = z == 31
    zedge = zlast | (z == 0)

    def advance(i, field, turned, body):
        before, here = turned
        after = lanes(field[i + 1], 64)
        body(i, field[i], here, jnp.where(xl == 1, after, before))
        return here, after

    def summed(k):
        k = k + lanes(k, 64)
        return k + lanes(k, 32)

    def prepare(i, k, inner, outer):
        a, b = k + inner, k + outer
        yi, yo = sides(k)
        c = k + yi
        e = jnp.where(yout, 0.0, k + yo)
        w = jnp.where(zlast, 0.0, k + lanes(k, 1))
        diag = (a + b) + (c + e) + (w + lanes(w, -1))
        diag = diag + (jnp.where(yout, k, 0.0) + jnp.where(zedge, k, 0.0))
        inv = RELAX / diag
        wxi[i], wxe[i], wyi[i], wye[i], wz2[i], diag2[i], inv2[i] = a, b, c, e, w, diag, inv
        va[i] = inv * f2[i]
        sumk[i] = summed(k)

    def around2(i, c, inner, outer):
        yi, yo = sides(c)
        w = wz2[i]
        total = wxi[i] * inner + wxe[i] * outer
        total = total + (wyi[i] * yi + wye[i] * yo)
        return total + (w * lanes(c, 1) + lanes(w * c, -1))

    def sweep2(i, c, inner, outer):
        return KEEP * c + inv2[i] * (f2[i] + around2(i, c, inner, outer))

    def first2(i, c, inner, outer):
        vb[i] = sweep2(i, c, inner, outer)

    def residual2(i, c, inner, outer):
        sumr[i] = summed(f2[i] - diag2[i] * c + around2(i, c, inner, outer))

    def three(i, state):
        ofk, ofa, ofb = state
        ofk = advance(i, k2, ofk, prepare)
        ofa = advance(i - 1, va, ofa, first2)
        return ofk, ofa, advance(i - 2, vb, ofb, residual2)

    ofk = (zero, lanes(k2[PAD], 64))
    ofk = advance(PAD, k2, ofk, prepare)
    ofk = advance(PAD + 1, k2, ofk, prepare)
    ofa = advance(PAD, va, (zero, lanes(va[PAD], 64)), first2)
    ofb = (zero, lanes(vb[PAD], 64))

    def steps(step, state):
        for u in range(UNROLL):
            state = three(PAD + 2 + UNROLL * step + u, state)
        return state

    _, ofa, ofb = lax.fori_loop(0, 30 // UNROLL, steps, (ofk, ofa, ofb))
    advance(PAD + 31, va, ofa, first2)
    ofb = advance(PAD + 30, vb, ofb, residual2)
    advance(PAD + 31, vb, ofb, residual2)

    def four(sums, q):
        t = jnp.where(group == 0, sums[4 * q + PAD], sums[4 * q + PAD + 1])
        t = jnp.where(group == 2, sums[4 * q + PAD + 2], t)
        t = jnp.where(group == 3, sums[4 * q + PAD + 3], t)
        return t + lanes(t, 1)

    c3 = [0.125 * four(sumk, q) for q in range(8)]
    f3 = [0.5 * four(sumr, q) for q in range(8)]

    def plus3(v):
        up = [lanes(c, 32) for c in v] + [zero]
        return [jnp.where(group < 3, up[q], up[q + 1]) for q in range(8)]

    def minus3(v):
        down = [zero] + [lanes(c, -32) for c in v]
        return [jnp.where(group > 0, down[q + 1], down[q]) for q in range(8)]

    level3 = Coarse(c3, plus3, minus3, above, below, row == 15, (row == 0) | (row == 15), 2)
    v3 = level3.sweep(level3.first(f3), f3)
    r3 = level3.residual(v3, f3)

    def restrict(values, x, y, zz):
        s = [t + lanes(t, x) for t in values]
        s = [y(t) for t in s]
        return [t + lanes(t, zz) for t in s]

    cores = lambda t: t[:8] + t[8:]
    f4 = [0.5 * s for s in restrict(r3, 32, cores, 2)]
    c4 = [0.125 * s for s in restrict(c3, 32, cores, 2)]
    zero8 = zero[:8]
    row8, lane8, group8 = row[:8], lane[:8], group[:8]

    def plus4(v):
        turn = [lanes(c, 64) for c in v] + [zero8]
        return [jnp.where(group8 < 2, turn[q], turn[q + 1]) for q in range(8)]

    def minus4(v):
        turn = [zero8] + [lanes(c, 64) for c in v]
        return [jnp.where(group8 < 2, turn[q], turn[q + 1]) for q in range(8)]

    def next_rows(n):
        return lambda c: rows(c, n)

    level4 = Coarse(
        c4, plus4, minus4, next_rows(1), next_rows(-1), row8 == 7, (row8 == 0) | (row8 == 7), 4
    )
    v4 = level4.sweep(level4.first(f4), f4)
    r4 = level4.residual(v4, f4)

    pair = lambda t: t + rows(t, 1)
    f5 = [0.5 * s for s in restrict(r4, 64, pair, 4)]
    c5 = [0.125 * s for s in restrict(c4, 64, pair, 4)]
    level5 = Coarse(
        c5,
        lambda v: v[1:] + [zero8],
        lambda v: [zero8] + v[:-1],
        next_rows(2),
        next_rows(-2),
        row8 >= 6,
        (row8 < 2) | (row8 >= 6),
        8,
    )
    v5 = level5.sweeps(level5.first(f5), f5, COARSE_SWEEPS - 1)

    def spread(c, bit):
        return jnp.where((iota(c.shape, 1) & bit) != 0, lanes(c, -bit), c)

    v5 = [jnp.where((row8 & 1) != 0, rows(c, -1), c) for c in v5]
    v4 = [c + spread(e, 4) for c, e in zip(v4, v5)]
    v4 = level4.sweeps(v4, f4, 2)

    v4 = [spread(jnp.where(group8 % 2 == 1, lanes(c, -32), c), 2) for c in v4]
    v3 = [c + jnp.concatenate([e, e], axis=0) for c, e in zip(v3, v4)]
    v3 = level3.sweeps(v3, f3, 2)

    for q in range(8):
        e3[q] = spread(v3[q], 1)
    for t in range(5):
        p = gx + t - 2
        inside = (p >= 0) & (p < 32)
        p = jnp.clip(p, 0, 31)
        e = jnp.where(group == jnp.where(inside, p % 4, -1), e3[p // 4], 0.0)
        va[gx + t - 2 + PAD] = vb[gx + t - 2 + PAD] + summed(e)

    def some(read, write, first, end):
        turned = [lanes(read[gx + t + PAD], 64) for t in range(first - 1, end + 1)]
        for u, t in enumerate(range(first, end)):
            i = gx + t + PAD
            outer = jnp.where(xl == 1, turned[u + 2], turned[u])
            write[i] = sweep2(i, read[i], turned[u + 1], outer)

    some(va, vb, -2, 3)
    some(vb, va, -1, 2)

    lane8 = iota((8, 128), 1)
    pick = 32 * (iota((8, 128), 0) // 4) + lane8 // 4
    wide = {}
    for t in range(-1, 2):
        for x in range(2):
            parts = []
            for b in range(-1, 2):
                y = gy + b
                inside = (y >= 0) & (y < 16)
                y = jnp.clip(y, 0, 15)
                line = va[gx + t + PAD, pl.ds(8 * (y % 2) + y // 2, 1), :]
                line = jnp.broadcast_to(jnp.where(inside, line, 0.0), (8, 128))
                parts.append(jnp.take_along_axis(line, 64 * x + pick, axis=1))
            wide[t, x] = jnp.concatenate(parts, axis=0)

    def correction(i):
        return wide[i // 4, (i % 4) // 2]

    middle = Window(2, (-2, 6))
    middle.given(wx1, wy1, wz1, inv1)
    source = Stored(f1, -2)
    upper_half = iota((8, 128), 0) >= 4
    second = (iota((ROWS, 128), 0) & 2) != 0

    def received(i):
        n = 2 * i + 8
        c = [jnp.where(upper_half, r[n + 1 : n + 2], r[n : n + 1]) for r in (vmid, vnear, vfar)]
        c = joined(first, *c)
        return jnp.where(second, lanes(c, 1), c)

    v = {i: received(i) + correction(i) for i in range(-3, 7)}
    v = middle.sweep(v, source, -2, 6)
    v = middle.sweep(v, source, -1, 5)

    odd_lane = iota((ROWS, 128), 1) % 2 == 1
    odd_row = iota((ROWS, 128), 0) % 2 == 1
    fine = Window(1, (-1, 9))
    fine.given(wx0, wy0, wz0, inv0)
    source = Stored(f0, -1)
    base = Stored(v0, -2)
    spread1 = {}
    for i in range(-1, 5):
        c = jnp.where(odd_lane, lanes(v[i], -1), v[i])
        spread1[i] = jnp.where(odd_row, rows(c, -1), c)
    v = {i: base[i] + spread1[i // 2] for i in range(-2, 10)}
    v = fine.sweep(v, source, -1, 9)
    v = fine.sweep(v, source, 0, 8)
    for i in range(8):
        out[i] = v[i][8:16]


WINDOW_PLANES = (12, 10, 8, 11, 10, 10, 10, 9, 8, 8, 8)


def f32(*shape):
    return jax.ShapeDtypeStruct(shape, jnp.float32)


def shift(x, by):
    count = lax.axis_size("gx")
    return lax.ppermute(x, "gx", [(i, i + by) for i in range(count) if 0 <= i + by < count])


def swap(x, first):
    pairs = [(i, i + 1) for i in range(first, lax.axis_size("gy") - 1, 2)]
    return lax.ppermute(x, "gy", pairs + [(b, a) for a, b in pairs])


def to_all(x, axis, count, groups=None):
    copies = jnp.broadcast_to(x[None], (count,) + x.shape)
    return lax.all_to_all(copies, axis, 0, 0, axis_index_groups=groups)


def shards(right_side, coefficient, previous):
    own = jnp.stack([right_side, coefficient, previous])
    mid = jnp.concatenate([shift(own[:, -HALO:], 1), own, shift(own[:, :HALO], -1)], axis=1)
    near, far = swap(mid, 0), swap(mid, 1)

    params = pltpu.CompilerParams(vmem_limit_bytes=VMEM)
    array = pl.BlockSpec(memory_space=pltpu.VMEM)
    packed, *window = pl.pallas_call(
        down_kernel,
        in_specs=[array] * 3,
        out_shape=(f32(10, 128),) + tuple(f32(n, ROWS, 128) for n in WINDOW_PLANES),
        compiler_params=params,
        name="down",
    )(mid, near, far)

    blocks = to_all(packed.reshape(1, 1280), "gx", 32)
    mine = to_all(
        blocks[:, :, :256].reshape(64, 128), "gy", 8, [[2 * z + c for z in range(8)] for c in range(2)]
    ).reshape(512, 128)
    other = swap(mine, 0)
    v1 = jnp.pad(blocks[:, 0, 256:], ((1, 1), (0, 0)))
    start = (lax.axis_index("gx"), jnp.int32(0))
    vmid = lax.dynamic_slice(v1, start, (3, 1024)).reshape(24, 128)
    vnear, vfar = swap(vmid, 0), swap(vmid, 1)

    plane = pltpu.VMEM((32 + 2 * PAD, 16, 128), jnp.float32)
    return pl.pallas_call(
        up_kernel,
        in_specs=[array] * (5 + len(WINDOW_PLANES)),
        out_shape=f32(8, 8, 128),
        scratch_shapes=[plane] * 13 + [pltpu.VMEM((8, 16, 128), jnp.float32)],
        compiler_params=params,
        name="up",
    )(mine, other, *window, vmid, vnear, vfar)


def solution(mesh):
    spec = P("gx", "gy", None)
    return jax.shard_map(
        shards, mesh=mesh, in_specs=(spec,) * 3, out_specs=spec, check_vma=False
    )
```

```python
import jax
import jax.numpy as jnp
from jax import lax
from jax.experimental import pallas as pl
from jax.experimental.pallas import tpu as pltpu
from jax.sharding import PartitionSpec as P

RELAX = 0.8
KEEP = 1.0 - RELAX
HALO = 7
ROWS = 24
COARSE_SWEEPS = 8
VMEM = 48 * 1024 * 1024


def lanes(x, n):
    return pltpu.roll(x, (-n) % x.shape[1], axis=1)


def rows(x, n):
    return pltpu.roll(x, (-n) % x.shape[0], axis=0)


def iota(shape, dim):
    return lax.broadcasted_iota(jnp.int32, shape, dim)


class Window:
    def __init__(self, step, planes):
        self.step = step
        self.planes = planes

    def given(self, wx, wy, wz, inv):
        first = self.planes[0]
        self.wx, self.wy = Stored(wx, first - 1), Stored(wy, first)
        self.wz, self.inv = Stored(wz, first), Stored(inv, first)

    def hand_on(self, planes, wx, wy, wz, inv):
        first, end = planes
        for i in range(first - 1, end):
            wx[i - first + 1] = self.wx[i]
        for i in range(first, end):
            wy[i - first], wz[i - first], inv[i - first] = self.wy[i], self.wz[i], self.inv[i]

    def weights(self, coeff):
        first, end = self.planes
        lane = iota((ROWS, 128), 1)
        last = lane >= 128 - self.step
        edge = (lane < self.step) | last
        self.wx, self.wy, self.wz, self.diag, self.inv = {}, {}, {}, {}, {}
        for i in range(first - 1, end):
            self.wx[i] = coeff[i] + coeff[i + 1]
        for i in range(first, end):
            k = coeff[i]
            wy = k + rows(k, self.step)
            wz = jnp.where(last, 0.0, k + lanes(k, self.step))
            diag = self.wx[i] + self.wx[i - 1] + (wy + rows(wy, -self.step))
            diag = diag + (wz + lanes(wz, -self.step)) + jnp.where(edge, k, 0.0)
            self.wy[i], self.wz[i], self.diag[i] = wy, wz, diag
            self.inv[i] = jnp.where(k > 0.0, RELAX / diag, 0.0)

    def around(self, v, i):
        c = v[i]
        wy, wz, step = self.wy[i], self.wz[i], self.step
        total = self.wx[i] * v[i + 1] + self.wx[i - 1] * v[i - 1]
        total = total + (wy * rows(c, step) + rows(wy * c, -step))
        return total + (wz * lanes(c, step) + lanes(wz * c, -step))

    def sweep(self, v, source, first, end):
        return {
            i: KEEP * v[i] + self.inv[i] * (source[i] + self.around(v, i)) for i in range(first, end)
        }

    def residual(self, v, source, first, end):
        return {i: source[i] - self.diag[i] * v[i] + self.around(v, i) for i in range(first, end)}


class Stored:
    def __init__(self, ref, first):
        self.ref, self.first = ref, first

    def __getitem__(self, i):
        return self.ref[i - self.first]

    def __setitem__(self, i, value):
        self.ref[i - self.first] = value


def block_sum(low, high, step):
    s = low + high
    s = s + rows(s, step)
    return s + lanes(s, step)


def core_mask(rows_of):
    core = lax.rem(lax.axis_index("gy"), 2)
    return jnp.broadcast_to(core, (rows_of, 128)) == 0


def joined(first, mid, near, far):
    return jnp.concatenate([jnp.where(first, far, near), mid, jnp.where(first, near, far)], axis=0)


def down_kernel(
    mid, near, far, packed, v0_out, f0_out, f1_out, wx0, wy0, wz0, inv0, wx1, wy1, wz1, inv1
):
    first = core_mask(8)

    def field(which):
        return {
            i - HALO: joined(first, mid[which, i], near[which, i], far[which, i])
            for i in range(mid.shape[1])
        }

    source, coeff, v = field(0), field(1), field(2)
    source = {i: 2.0 * source[i] for i in range(-6, 14)}

    fine = Window(1, (-6, 14))
    fine.weights(coeff)
    v = fine.sweep(v, source, -6, 14)
    v = fine.sweep(v, source, -5, 13)
    for i in range(-2, 10):
        v0_out[i + 2] = v[i]
    for i in range(-1, 9):
        f0_out[i + 1] = source[i]
    fine.hand_on((-1, 9), wx0, wy0, wz0, inv0)
    r = fine.residual(v, source, -4, 12)

    source = {i: 0.5 * block_sum(r[2 * i], r[2 * i + 1], 1) for i in range(-2, 6)}
    coeff = {i: 0.125 * block_sum(coeff[2 * i], coeff[2 * i + 1], 1) for i in range(-3, 7)}
    for i in range(-2, 6):
        f1_out[i + 2] = source[i]
    middle = Window(2, (-2, 6))
    middle.weights(coeff)
    middle.hand_on((-2, 6), wx1, wy1, wz1, inv1)
    v = {i: middle.inv[i] * source[i] for i in range(-2, 6)}
    v = middle.sweep(v, source, -1, 5)
    even = iota((8, 128), 1) % 2 == 0
    for i in range(4):
        c = v[i][8:16]
        c = jnp.where(even, c, lanes(rows(c, 2), -1))
        packed[2 * i + 2 : 2 * i + 3, :] = c[0:1]
        packed[2 * i + 3 : 2 * i + 4, :] = c[4:5]
    r = middle.residual(v, source, 0, 4)

    source = [0.5 * block_sum(r[2 * i], r[2 * i + 1], 2)[8:16] for i in range(2)]
    coeff = [0.125 * block_sum(coeff[2 * i], coeff[2 * i + 1], 2)[8:16] for i in range(2)]
    lane, row = iota((8, 128), 1), iota((8, 128), 0)
    group = lane // 32
    pick = 4 * (lane % 32)
    for c, planes in enumerate((source, coeff)):
        dense = [jnp.take_along_axis(t, pick, axis=1) for t in planes]
        dense = jnp.where(group < 2, dense[0], dense[1])
        dense = jnp.where(row == 4 * (group % 2), dense, 0.0)
        packed[c : c + 1, :] = jnp.sum(dense, axis=0, keepdims=True)


class Coarse:
    def __init__(self, coeff, nxp, nxm, nyp, nym, ylast, yedge, zstep):
        self.nxp, self.nxm, self.nyp, self.nym, self.zstep = nxp, nxm, nyp, nym, zstep
        z = iota(coeff[0].shape, 1) % 32
        zlast = z >= 32 - zstep
        zedge = (z < zstep) | zlast
        self.wp = [k + n for k, n in zip(coeff, nxp(coeff))]
        self.wm = [k + n for k, n in zip(coeff, nxm(coeff))]
        self.wy = [jnp.where(ylast, 0.0, k + nyp(k)) for k in coeff]
        self.wz = [jnp.where(zlast, 0.0, k + lanes(k, zstep)) for k in coeff]
        self.diag = []
        for k, wp, wm, wy, wz in zip(coeff, self.wp, self.wm, self.wy, self.wz):
            diag = wp + wm + (wy + nym(wy)) + (wz + lanes(wz, -zstep))
            self.diag.append(diag + (jnp.where(yedge, k, 0.0) + jnp.where(zedge, k, 0.0)))
        self.inv = [RELAX / d for d in self.diag]

    def around(self, v):
        out = []
        for c, p, m, wp, wm, wy, wz in zip(
            v, self.nxp(v), self.nxm(v), self.wp, self.wm, self.wy, self.wz
        ):
            total = wp * p + wm * m
            total = total + (wy * self.nyp(c) + self.nym(wy * c))
            out.append(total + (wz * lanes(c, self.zstep) + lanes(wz * c, -self.zstep)))
        return out

    def first(self, source):
        return [i * f for i, f in zip(self.inv, source)]

    def sweep(self, v, source):
        around = self.around(v)
        return [KEEP * c + i * (f + t) for c, i, f, t in zip(v, self.inv, source, around)]

    def sweeps(self, v, source, count):
        step = lambda _, v: tuple(self.sweep(list(v), source))
        return list(lax.fori_loop(0, count, step, tuple(v)))

    def residual(self, v, source):
        around = self.around(v)
        return [f - d * c + t for c, d, f, t in zip(v, self.diag, source, around)]


def above(c):
    return jnp.concatenate([c[8:], rows(c[:8], 1)], axis=0)


def below(c):
    return jnp.concatenate([rows(c[8:], -1), c[:8]], axis=0)


UNROLL = 10
PAD = 3


def up_kernel(
    gathered, v0, f0, f1, wx0, wy0, wz0, inv0, wx1, wy1, wz1, inv1, vmid, vnear, vfar, out,
    k2, f2, va, vb, wxi, wxe, wyi, wye, wz2, diag2, inv2, sumk, sumr, e3,
):
    gx, gy = lax.axis_index("gx"), lax.axis_index("gy")
    first = core_mask(8)
    lane = iota((16, 128), 1)
    row = iota((16, 128), 0)
    group, z = lane // 32, lane % 32
    xl, yl = group // 2, group % 2
    zero = jnp.zeros((16, 128), jnp.float32)

    for ref in (k2, f2, va, vb, wxi, wxe, wyi, wye, wz2, inv2):
        for i in range(PAD):
            ref[i] = zero
            ref[32 + PAD + i] = zero
    for i in range(32):
        for c, ref in ((0, f2), (1, k2)):
            for core in range(2):
                here = pl.ds(64 * core + 2 * i + c, 8, stride=128)
                ref[i + PAD, 8 * core : 8 * core + 8] = gathered[here, :]

    def sides(c):
        up, down = lanes(c, 32), lanes(c, -32)
        inner = jnp.where(yl == 0, up, down)
        outer = jnp.where(yl == 1, above(down), below(up))
        return inner, outer

    yout = ((yl == 1) & (row == 15)) | ((yl == 0) & (row == 0))
    zlast = z == 31
    zedge = zlast | (z == 0)

    def advance(i, field, turned, body):
        before, here = turned
        after = lanes(field[i + 1], 64)
        body(i, field[i], here, jnp.where(xl == 1, after, before))
        return here, after

    def summed(k):
        k = k + lanes(k, 64)
        return k + lanes(k, 32)

    def prepare(i, k, inner, outer):
        a, b = k + inner, k + outer
        yi, yo = sides(k)
        c = k + yi
        e = jnp.where(yout, 0.0, k + yo)
        w = jnp.where(zlast, 0.0, k + lanes(k, 1))
        diag = (a + b) + (c + e) + (w + lanes(w, -1))
        diag = diag + (jnp.where(yout, k, 0.0) + jnp.where(zedge, k, 0.0))
        inv = RELAX / diag
        wxi[i], wxe[i], wyi[i], wye[i], wz2[i], diag2[i], inv2[i] = a, b, c, e, w, diag, inv
        va[i] = inv * f2[i]
        sumk[i] = summed(k)

    def around2(i, c, inner, outer):
        yi, yo = sides(c)
        w = wz2[i]
        total = wxi[i] * inner + wxe[i] * outer
        total = total + (wyi[i] * yi + wye[i] * yo)
        return total + (w * lanes(c, 1) + lanes(w * c, -1))

    def sweep2(i, c, inner, outer):
        return KEEP * c + inv2[i] * (f2[i] + around2(i, c, inner, outer))

    def first2(i, c, inner, outer):
        vb[i] = sweep2(i, c, inner, outer)

    def residual2(i, c, inner, outer):
        sumr[i] = summed(f2[i] - diag2[i] * c + around2(i, c, inner, outer))

    def three(i, state):
        ofk, ofa, ofb = state
        ofk = advance(i, k2, ofk, prepare)
        ofa = advance(i - 1, va, ofa, first2)
        return ofk, ofa, advance(i - 2, vb, ofb, residual2)

    ofk = (zero, lanes(k2[PAD], 64))
    ofk = advance(PAD, k2, ofk, prepare)
    ofk = advance(PAD + 1, k2, ofk, prepare)
    ofa = advance(PAD, va, (zero, lanes(va[PAD], 64)), first2)
    ofb = (zero, lanes(vb[PAD], 64))

    def steps(step, state):
        for u in range(UNROLL):
            state = three(PAD + 2 + UNROLL * step + u, state)
        return state

    _, ofa, ofb = lax.fori_loop(0, 30 // UNROLL, steps, (ofk, ofa, ofb))
    advance(PAD + 31, va, ofa, first2)
    ofb = advance(PAD + 30, vb, ofb, residual2)
    advance(PAD + 31, vb, ofb, residual2)

    def four(sums, q):
        t = jnp.where(group == 0, sums[4 * q + PAD], sums[4 * q + PAD + 1])
        t = jnp.where(group == 2, sums[4 * q + PAD + 2], t)
        t = jnp.where(group == 3, sums[4 * q + PAD + 3], t)
        return t + lanes(t, 1)

    c3 = [0.125 * four(sumk, q) for q in range(8)]
    f3 = [0.5 * four(sumr, q) for q in range(8)]

    def plus3(v):
        up = [lanes(c, 32) for c in v] + [zero]
        return [jnp.where(group < 3, up[q], up[q + 1]) for q in range(8)]

    def minus3(v):
        down = [zero] + [lanes(c, -32) for c in v]
        return [jnp.where(group > 0, down[q + 1], down[q]) for q in range(8)]

    level3 = Coarse(c3, plus3, minus3, above, below, row == 15, (row == 0) | (row == 15), 2)
    v3 = level3.sweep(level3.first(f3), f3)
    r3 = level3.residual(v3, f3)

    def restrict(values, x, y, zz):
        s = [t + lanes(t, x) for t in values]
        s = [y(t) for t in s]
        return [t + lanes(t, zz) for t in s]

    cores = lambda t: t[:8] + t[8:]
    f4 = [0.5 * s for s in restrict(r3, 32, cores, 2)]
    c4 = [0.125 * s for s in restrict(c3, 32, cores, 2)]
    zero8 = zero[:8]
    row8, lane8, group8 = row[:8], lane[:8], group[:8]

    def plus4(v):
        turn = [lanes(c, 64) for c in v] + [zero8]
        return [jnp.where(group8 < 2, turn[q], turn[q + 1]) for q in range(8)]

    def minus4(v):
        turn = [zero8] + [lanes(c, 64) for c in v]
        return [jnp.where(group8 < 2, turn[q], turn[q + 1]) for q in range(8)]

    def next_rows(n):
        return lambda c: rows(c, n)

    level4 = Coarse(
        c4, plus4, minus4, next_rows(1), next_rows(-1), row8 == 7, (row8 == 0) | (row8 == 7), 4
    )
    v4 = level4.sweep(level4.first(f4), f4)
    r4 = level4.residual(v4, f4)

    pair = lambda t: t + rows(t, 1)
    f5 = [0.5 * s for s in restrict(r4, 64, pair, 4)]
    c5 = [0.125 * s for s in restrict(c4, 64, pair, 4)]
    level5 = Coarse(
        c5,
        lambda v: v[1:] + [zero8],
        lambda v: [zero8] + v[:-1],
        next_rows(2),
        next_rows(-2),
        row8 >= 6,
        (row8 < 2) | (row8 >= 6),
        8,
    )
    v5 = level5.sweeps(level5.first(f5), f5, COARSE_SWEEPS - 1)

    def spread(c, bit):
        return jnp.where((iota(c.shape, 1) & bit) != 0, lanes(c, -bit), c)

    v5 = [jnp.where((row8 & 1) != 0, rows(c, -1), c) for c in v5]
    v4 = [c + spread(e, 4) for c, e in zip(v4, v5)]
    v4 = level4.sweeps(v4, f4, 2)

    v4 = [spread(jnp.where(group8 % 2 == 1, lanes(c, -32), c), 2) for c in v4]
    v3 = [c + jnp.concatenate([e, e], axis=0) for c, e in zip(v3, v4)]
    v3 = level3.sweeps(v3, f3, 2)

    for q in range(8):
        e3[q] = spread(v3[q], 1)
    for t in range(5):
        p = gx + t - 2
        inside = (p >= 0) & (p < 32)
        p = jnp.clip(p, 0, 31)
        e = jnp.where(group == jnp.where(inside, p % 4, -1), e3[p // 4], 0.0)
        va[gx + t - 2 + PAD] = vb[gx + t - 2 + PAD] + summed(e)

    def some(read, write, first, end):
        turned = [lanes(read[gx + t + PAD], 64) for t in range(first - 1, end + 1)]
        for u, t in enumerate(range(first, end)):
            i = gx + t + PAD
            outer = jnp.where(xl == 1, turned[u + 2], turned[u])
            write[i] = sweep2(i, read[i], turned[u + 1], outer)

    some(va, vb, -2, 3)
    some(vb, va, -1, 2)

    lane8 = iota((8, 128), 1)
    pick = 32 * (iota((8, 128), 0) // 4) + lane8 // 4
    wide = {}
    for t in range(-1, 2):
        for x in range(2):
            parts = []
            for b in range(-1, 2):
                y = gy + b
                inside = (y >= 0) & (y < 16)
                y = jnp.clip(y, 0, 15)
                line = va[gx + t + PAD, pl.ds(8 * (y % 2) + y // 2, 1), :]
                line = jnp.broadcast_to(jnp.where(inside, line, 0.0), (8, 128))
                parts.append(jnp.take_along_axis(line, 64 * x + pick, axis=1))
            wide[t, x] = jnp.concatenate(parts, axis=0)

    def correction(i):
        return wide[i // 4, (i % 4) // 2]

    middle = Window(2, (-2, 6))
    middle.given(wx1, wy1, wz1, inv1)
    source = Stored(f1, -2)
    upper_half = iota((8, 128), 0) >= 4
    second = (iota((ROWS, 128), 0) & 2) != 0

    def received(i):
        n = 2 * i + 8
        c = [jnp.where(upper_half, r[n + 1 : n + 2], r[n : n + 1]) for r in (vmid, vnear, vfar)]
        c = joined(first, *c)
        return jnp.where(second, lanes(c, 1), c)

    v = {i: received(i) + correction(i) for i in range(-3, 7)}
    v = middle.sweep(v, source, -2, 6)
    v = middle.sweep(v, source, -1, 5)

    odd_lane = iota((ROWS, 128), 1) % 2 == 1
    odd_row = iota((ROWS, 128), 0) % 2 == 1
    fine = Window(1, (-1, 9))
    fine.given(wx0, wy0, wz0, inv0)
    source = Stored(f0, -1)
    base = Stored(v0, -2)
    spread1 = {}
    for i in range(-1, 5):
        c = jnp.where(odd_lane, lanes(v[i], -1), v[i])
        spread1[i] = jnp.where(odd_row, rows(c, -1), c)
    v = {i: base[i] + spread1[i // 2] for i in range(-2, 10)}
    v = fine.sweep(v, source, -1, 9)
    v = fine.sweep(v, source, 0, 8)
    for i in range(8):
        out[i] = v[i][8:16]


WINDOW_PLANES = (12, 10, 8, 11, 10, 10, 10, 9, 8, 8, 8)


def f32(*shape):
    return jax.ShapeDtypeStruct(shape, jnp.float32)


def swap(x, axis, first):
    pairs = [(i, i + 1) for i in range(first, lax.axis_size(axis) - 1, 2)]
    return lax.ppermute(x, axis, pairs + [(b, a) for a, b in pairs])


def to_all(x, axis):
    copies = jnp.broadcast_to(x[None], (lax.axis_size(axis),) + x.shape)
    return lax.all_to_all(copies, axis, 0, 0)


def shards(right_side, coefficient, previous):
    own = jnp.stack([right_side, coefficient, previous])
    even = lax.axis_index("gx") % 2 == 0
    start, end = own[:, :HALO], own[:, -HALO:]
    near = swap(jnp.where(even, end, start), "gx", 0)
    far = swap(jnp.where(even, start, end), "gx", 1)
    mid = jnp.concatenate([jnp.where(even, far, near), own, jnp.where(even, near, far)], axis=1)
    near, far = swap(mid, "gy", 0), swap(mid, "gy", 1)

    params = pltpu.CompilerParams(vmem_limit_bytes=VMEM)
    array = pl.BlockSpec(memory_space=pltpu.VMEM)
    packed, *window = pl.pallas_call(
        down_kernel,
        in_specs=[array] * 3,
        out_shape=(f32(10, 128),) + tuple(f32(n, ROWS, 128) for n in WINDOW_PLANES),
        compiler_params=params,
        name="down",
    )(mid, near, far)

    blocks = to_all(packed.reshape(1, 1280), "gx")
    gathered = to_all(blocks[:, :, :256].reshape(64, 128), "gy").reshape(1024, 128)
    v1 = jnp.pad(blocks[:, 0, 256:], ((1, 1), (0, 0)))
    place = (lax.axis_index("gx"), jnp.int32(0))
    vmid = lax.dynamic_slice(v1, place, (3, 1024)).reshape(24, 128)
    vnear, vfar = swap(vmid, "gy", 0), swap(vmid, "gy", 1)

    plane = pltpu.VMEM((32 + 2 * PAD, 16, 128), jnp.float32)
    return pl.pallas_call(
        up_kernel,
        in_specs=[array] * (4 + len(WINDOW_PLANES)),
        out_shape=f32(8, 8, 128),
        scratch_shapes=[plane] * 13 + [pltpu.VMEM((8, 16, 128), jnp.float32)],
        compiler_params=params,
        name="up",
    )(gathered, *window, vmid, vnear, vfar)


def solution(mesh):
    spec = P("gx", "gy", None)
    return jax.shard_map(
        shards, mesh=mesh, in_specs=(spec,) * 3, out_specs=spec, check_vma=False
    )
```

```python
import jax
import jax.numpy as jnp
from jax import lax
from jax.experimental import pallas as pl
from jax.experimental.pallas import tpu as pltpu
from jax.sharding import PartitionSpec as P

RELAX = 0.8
KEEP = 1.0 - RELAX
HALO = 7
ROWS = 24
COARSE_SWEEPS = 8
VMEM = 48 * 1024 * 1024


def lanes(x, n):
    return pltpu.roll(x, (-n) % x.shape[1], axis=1)


def rows(x, n):
    return pltpu.roll(x, (-n) % x.shape[0], axis=0)


def iota(shape, dim):
    return lax.broadcasted_iota(jnp.int32, shape, dim)


class Window:
    def __init__(self, step, planes):
        self.step = step
        self.planes = planes

    def given(self, wx, wy, wz, inv):
        first = self.planes[0]
        self.wx, self.wy = Stored(wx, first - 1), Stored(wy, first)
        self.wz, self.inv = Stored(wz, first), Stored(inv, first)

    def hand_on(self, planes, wx, wy, wz, inv):
        first, end = planes
        for i in range(first - 1, end):
            wx[i - first + 1] = self.wx[i]
        for i in range(first, end):
            wy[i - first], wz[i - first], inv[i - first] = self.wy[i], self.wz[i], self.inv[i]

    def weights(self, coeff):
        first, end = self.planes
        lane = iota((ROWS, 128), 1)
        last = lane >= 128 - self.step
        edge = (lane < self.step) | last
        self.wx, self.wy, self.wz, self.diag, self.inv = {}, {}, {}, {}, {}
        for i in range(first - 1, end):
            self.wx[i] = coeff[i] + coeff[i + 1]
        for i in range(first, end):
            k = coeff[i]
            wy = k + rows(k, self.step)
            wz = jnp.where(last, 0.0, k + lanes(k, self.step))
            diag = self.wx[i] + self.wx[i - 1] + (wy + rows(wy, -self.step))
            diag = diag + (wz + lanes(wz, -self.step)) + jnp.where(edge, k, 0.0)
            self.wy[i], self.wz[i], self.diag[i] = wy, wz, diag
            self.inv[i] = jnp.where(k > 0.0, RELAX / diag, 0.0)

    def around(self, v, i):
        c = v[i]
        wy, wz, step = self.wy[i], self.wz[i], self.step
        total = self.wx[i] * v[i + 1] + self.wx[i - 1] * v[i - 1]
        total = total + (wy * rows(c, step) + rows(wy * c, -step))
        return total + (wz * lanes(c, step) + lanes(wz * c, -step))

    def sweep(self, v, source, first, end):
        return {
            i: KEEP * v[i] + self.inv[i] * (source[i] + self.around(v, i)) for i in range(first, end)
        }

    def residual(self, v, source, first, end):
        return {i: source[i] - self.diag[i] * v[i] + self.around(v, i) for i in range(first, end)}


class Stored:
    def __init__(self, ref, first):
        self.ref, self.first = ref, first

    def __getitem__(self, i):
        return self.ref[i - self.first]

    def __setitem__(self, i, value):
        self.ref[i - self.first] = value


def block_sum(low, high, step):
    s = low + high
    s = s + rows(s, step)
    return s + lanes(s, step)


def core_mask(rows_of):
    core = lax.rem(lax.axis_index("gy"), 2)
    return jnp.broadcast_to(core, (rows_of, 128)) == 0


def joined(first, mid, near, far):
    return jnp.concatenate([jnp.where(first, far, near), mid, jnp.where(first, near, far)], axis=0)


def down_kernel(
    mid, near, far, packed, v1_out, v0_out, f0_out, f1_out, wx0, wy0, wz0, inv0, wx1, wy1, wz1, inv1
):
    first = core_mask(8)

    def field(which):
        return {
            i - HALO: joined(first, mid[which, i], near[which, i], far[which, i])
            for i in range(mid.shape[1])
        }

    source, coeff, v = field(0), field(1), field(2)
    source = {i: 2.0 * source[i] for i in range(-6, 14)}

    fine = Window(1, (-6, 14))
    fine.weights(coeff)
    v = fine.sweep(v, source, -6, 14)
    v = fine.sweep(v, source, -5, 13)
    for i in range(-2, 10):
        v0_out[i + 2] = v[i]
    for i in range(-1, 9):
        f0_out[i + 1] = source[i]
    fine.hand_on((-1, 9), wx0, wy0, wz0, inv0)
    r = fine.residual(v, source, -4, 12)

    source = {i: 0.5 * block_sum(r[2 * i], r[2 * i + 1], 1) for i in range(-2, 6)}
    coeff = {i: 0.125 * block_sum(coeff[2 * i], coeff[2 * i + 1], 1) for i in range(-3, 7)}
    for i in range(-2, 6):
        f1_out[i + 2] = source[i]
    middle = Window(2, (-2, 6))
    middle.weights(coeff)
    middle.hand_on((-2, 6), wx1, wy1, wz1, inv1)
    v = {i: middle.inv[i] * source[i] for i in range(-2, 6)}
    v = middle.sweep(v, source, -1, 5)
    even = iota((8, 128), 1) % 2 == 0
    for i in range(4):
        c = v[i][8:16]
        c = jnp.where(even, c, lanes(rows(c, 2), -1))
        v1_out[2 * i : 2 * i + 1, :] = c[0:1]
        v1_out[2 * i + 1 : 2 * i + 2, :] = c[4:5]
    r = middle.residual(v, source, 0, 4)

    source = [0.5 * block_sum(r[2 * i], r[2 * i + 1], 2)[8:16] for i in range(2)]
    coeff = [0.125 * block_sum(coeff[2 * i], coeff[2 * i + 1], 2)[8:16] for i in range(2)]
    lane, row = iota((8, 128), 1), iota((8, 128), 0)
    group = lane // 32
    pick = 4 * (lane % 32)
    for c, planes in enumerate((source, coeff)):
        dense = [jnp.take_along_axis(t, pick, axis=1) for t in planes]
        dense = jnp.where(group < 2, dense[0], dense[1])
        dense = jnp.where(row == 4 * (group % 2), dense, 0.0)
        packed[c : c + 1, :] = jnp.sum(dense, axis=0, keepdims=True)


class Coarse:
    def __init__(self, coeff, nxp, nxm, nyp, nym, ylast, yedge, zstep):
        self.nxp, self.nxm, self.nyp, self.nym, self.zstep = nxp, nxm, nyp, nym, zstep
        z = iota(coeff[0].shape, 1) % 32
        zlast = z >= 32 - zstep
        zedge = (z < zstep) | zlast
        self.wp = [k + n for k, n in zip(coeff, nxp(coeff))]
        self.wm = [k + n for k, n in zip(coeff, nxm(coeff))]
        self.wy = [jnp.where(ylast, 0.0, k + nyp(k)) for k in coeff]
        self.wz = [jnp.where(zlast, 0.0, k + lanes(k, zstep)) for k in coeff]
        self.diag = []
        for k, wp, wm, wy, wz in zip(coeff, self.wp, self.wm, self.wy, self.wz):
            diag = wp + wm + (wy + nym(wy)) + (wz + lanes(wz, -zstep))
            self.diag.append(diag + (jnp.where(yedge, k, 0.0) + jnp.where(zedge, k, 0.0)))
        self.inv = [RELAX / d for d in self.diag]

    def around(self, v):
        out = []
        for c, p, m, wp, wm, wy, wz in zip(
            v, self.nxp(v), self.nxm(v), self.wp, self.wm, self.wy, self.wz
        ):
            total = wp * p + wm * m
            total = total + (wy * self.nyp(c) + self.nym(wy * c))
            out.append(total + (wz * lanes(c, self.zstep) + lanes(wz * c, -self.zstep)))
        return out

    def first(self, source):
        return [i * f for i, f in zip(self.inv, source)]

    def sweep(self, v, source):
        around = self.around(v)
        return [KEEP * c + i * (f + t) for c, i, f, t in zip(v, self.inv, source, around)]

    def sweeps(self, v, source, count):
        step = lambda _, v: tuple(self.sweep(list(v), source))
        return list(lax.fori_loop(0, count, step, tuple(v), unroll=True))

    def residual(self, v, source):
        around = self.around(v)
        return [f - d * c + t for c, d, f, t in zip(v, self.diag, source, around)]


def above(c):
    return jnp.concatenate([c[8:], rows(c[:8], 1)], axis=0)


def below(c):
    return jnp.concatenate([rows(c[8:], -1), c[:8]], axis=0)


UNROLL = 10
PAD = 3


def up_kernel(
    gathered, v0, f0, f1, wx0, wy0, wz0, inv0, wx1, wy1, wz1, inv1, vmid, vnear, vfar, out,
    k2, f2, va, vb, wxi, wxe, wyi, wye, wz2, diag2, inv2, sumk, sumr, e3,
):
    gx, gy = lax.axis_index("gx"), lax.axis_index("gy")
    first = core_mask(8)
    lane = iota((16, 128), 1)
    row = iota((16, 128), 0)
    group, z = lane // 32, lane % 32
    xl, yl = group // 2, group % 2
    zero = jnp.zeros((16, 128), jnp.float32)

    for ref in (k2, f2, va, vb, wxi, wxe, wyi, wye, wz2, inv2):
        for i in range(PAD):
            ref[i] = zero
            ref[32 + PAD + i] = zero
    for i in range(32):
        for c, ref in ((0, f2), (1, k2)):
            for core in range(2):
                here = pl.ds(64 * core + 2 * i + c, 8, stride=128)
                ref[i + PAD, 8 * core : 8 * core + 8] = gathered[here, :]

    def sides(c):
        up, down = lanes(c, 32), lanes(c, -32)
        inner = jnp.where(yl == 0, up, down)
        outer = jnp.where(yl == 1, above(down), below(up))
        return inner, outer

    yout = ((yl == 1) & (row == 15)) | ((yl == 0) & (row == 0))
    zlast = z == 31
    zedge = zlast | (z == 0)

    def advance(i, field, turned, body):
        before, here = turned
        after = lanes(field[i + 1], 64)
        body(i, field[i], here, jnp.where(xl == 1, after, before))
        return here, after

    def summed(k):
        k = k + lanes(k, 64)
        return k + lanes(k, 32)

    def prepare(i, k, inner, outer):
        a, b = k + inner, k + outer
        yi, yo = sides(k)
        c = k + yi
        e = jnp.where(yout, 0.0, k + yo)
        w = jnp.where(zlast, 0.0, k + lanes(k, 1))
        diag = (a + b) + (c + e) + (w + lanes(w, -1))
        diag = diag + (jnp.where(yout, k, 0.0) + jnp.where(zedge, k, 0.0))
        inv = RELAX / diag
        wxi[i], wxe[i], wyi[i], wye[i], wz2[i], diag2[i], inv2[i] = a, b, c, e, w, diag, inv
        va[i] = inv * f2[i]
        sumk[i] = summed(k)

    def around2(i, c, inner, outer):
        yi, yo = sides(c)
        w = wz2[i]
        total = wxi[i] * inner + wxe[i] * outer
        total = total + (wyi[i] * yi + wye[i] * yo)
        return total + (w * lanes(c, 1) + lanes(w * c, -1))

    def sweep2(i, c, inner, outer):
        return KEEP * c + inv2[i] * (f2[i] + around2(i, c, inner, outer))

    def first2(i, c, inner, outer):
        vb[i] = sweep2(i, c, inner, outer)

    def residual2(i, c, inner, outer):
        sumr[i] = summed(f2[i] - diag2[i] * c + around2(i, c, inner, outer))

    def three(i, state):
        ofk, ofa, ofb = state
        ofk = advance(i, k2, ofk, prepare)
        ofa = advance(i - 1, va, ofa, first2)
        return ofk, ofa, advance(i - 2, vb, ofb, residual2)

    ofk = (zero, lanes(k2[PAD], 64))
    ofk = advance(PAD, k2, ofk, prepare)
    ofk = advance(PAD + 1, k2, ofk, prepare)
    ofa = advance(PAD, va, (zero, lanes(va[PAD], 64)), first2)
    ofb = (zero, lanes(vb[PAD], 64))

    def steps(step, state):
        for u in range(UNROLL):
            state = three(PAD + 2 + UNROLL * step + u, state)
        return state

    _, ofa, ofb = lax.fori_loop(0, 30 // UNROLL, steps, (ofk, ofa, ofb))
    advance(PAD + 31, va, ofa, first2)
    ofb = advance(PAD + 30, vb, ofb, residual2)
    advance(PAD + 31, vb, ofb, residual2)

    def four(sums, q):
        t = jnp.where(group == 0, sums[4 * q + PAD], sums[4 * q + PAD + 1])
        t = jnp.where(group == 2, sums[4 * q + PAD + 2], t)
        t = jnp.where(group == 3, sums[4 * q + PAD + 3], t)
        return t + lanes(t, 1)

    c3 = [0.125 * four(sumk, q) for q in range(8)]
    f3 = [0.5 * four(sumr, q) for q in range(8)]

    def plus3(v):
        up = [lanes(c, 32) for c in v] + [zero]
        return [jnp.where(group < 3, up[q], up[q + 1]) for q in range(8)]

    def minus3(v):
        down = [zero] + [lanes(c, -32) for c in v]
        return [jnp.where(group > 0, down[q + 1], down[q]) for q in range(8)]

    level3 = Coarse(c3, plus3, minus3, above, below, row == 15, (row == 0) | (row == 15), 2)
    v3 = level3.sweep(level3.first(f3), f3)
    r3 = level3.residual(v3, f3)

    def restrict(values, x, y, zz):
        s = [t + lanes(t, x) for t in values]
        s = [y(t) for t in s]
        return [t + lanes(t, zz) for t in s]

    cores = lambda t: t[:8] + t[8:]
    f4 = [0.5 * s for s in restrict(r3, 32, cores, 2)]
    c4 = [0.125 * s for s in restrict(c3, 32, cores, 2)]
    zero8 = zero[:8]
    row8, lane8, group8 = row[:8], lane[:8], group[:8]

    def plus4(v):
        turn = [lanes(c, 64) for c in v] + [zero8]
        return [jnp.where(group8 < 2, turn[q], turn[q + 1]) for q in range(8)]

    def minus4(v):
        turn = [zero8] + [lanes(c, 64) for c in v]
        return [jnp.where(group8 < 2, turn[q], turn[q + 1]) for q in range(8)]

    def next_rows(n):
        return lambda c: rows(c, n)

    level4 = Coarse(
        c4, plus4, minus4, next_rows(1), next_rows(-1), row8 == 7, (row8 == 0) | (row8 == 7), 4
    )
    v4 = level4.sweep(level4.first(f4), f4)
    r4 = level4.residual(v4, f4)

    pair = lambda t: t + rows(t, 1)
    f5 = [0.5 * s for s in restrict(r4, 64, pair, 4)]
    c5 = [0.125 * s for s in restrict(c4, 64, pair, 4)]
    level5 = Coarse(
        c5,
        lambda v: v[1:] + [zero8],
        lambda v: [zero8] + v[:-1],
        next_rows(2),
        next_rows(-2),
        row8 >= 6,
        (row8 < 2) | (row8 >= 6),
        8,
    )
    v5 = level5.sweeps(level5.first(f5), f5, COARSE_SWEEPS - 1)

    def spread(c, bit):
        return jnp.where((iota(c.shape, 1) & bit) != 0, lanes(c, -bit), c)

    v5 = [jnp.where((row8 & 1) != 0, rows(c, -1), c) for c in v5]
    v4 = [c + spread(e, 4) for c, e in zip(v4, v5)]
    v4 = level4.sweeps(v4, f4, 2)

    v4 = [spread(jnp.where(group8 % 2 == 1, lanes(c, -32), c), 2) for c in v4]
    v3 = [c + jnp.concatenate([e, e], axis=0) for c, e in zip(v3, v4)]
    v3 = level3.sweeps(v3, f3, 2)

    for q in range(8):
        e3[q] = spread(v3[q], 1)
    for t in range(5):
        p = gx + t - 2
        inside = (p >= 0) & (p < 32)
        p = jnp.clip(p, 0, 31)
        e = jnp.where(group == jnp.where(inside, p % 4, -1), e3[p // 4], 0.0)
        va[gx + t - 2 + PAD] = vb[gx + t - 2 + PAD] + summed(e)

    def some(read, write, first, end):
        turned = [lanes(read[gx + t + PAD], 64) for t in range(first - 1, end + 1)]
        for u, t in enumerate(range(first, end)):
            i = gx + t + PAD
            outer = jnp.where(xl == 1, turned[u + 2], turned[u])
            write[i] = sweep2(i, read[i], turned[u + 1], outer)

    some(va, vb, -2, 3)
    some(vb, va, -1, 2)

    lane8 = iota((8, 128), 1)
    pick = 32 * (iota((8, 128), 0) // 4) + lane8 // 4
    wide = {}
    for t in range(-1, 2):
        for x in range(2):
            parts = []
            for b in range(-1, 2):
                y = gy + b
                inside = (y >= 0) & (y < 16)
                y = jnp.clip(y, 0, 15)
                line = va[gx + t + PAD, pl.ds(8 * (y % 2) + y // 2, 1), :]
                line = jnp.broadcast_to(jnp.where(inside, line, 0.0), (8, 128))
                parts.append(jnp.take_along_axis(line, 64 * x + pick, axis=1))
            wide[t, x] = jnp.concatenate(parts, axis=0)

    def correction(i):
        return wide[i // 4, (i % 4) // 2]

    middle = Window(2, (-2, 6))
    middle.given(wx1, wy1, wz1, inv1)
    source = Stored(f1, -2)
    upper_half = iota((8, 128), 0) >= 4
    second = (iota((ROWS, 128), 0) & 2) != 0

    def received(i):
        n = 2 * i + 8
        c = [jnp.where(upper_half, r[n + 1 : n + 2], r[n : n + 1]) for r in (vmid, vnear, vfar)]
        c = joined(first, *c)
        return jnp.where(second, lanes(c, 1), c)

    v = {i: received(i) + correction(i) for i in range(-3, 7)}
    v = middle.sweep(v, source, -2, 6)
    v = middle.sweep(v, source, -1, 5)

    odd_lane = iota((ROWS, 128), 1) % 2 == 1
    odd_row = iota((ROWS, 128), 0) % 2 == 1
    fine = Window(1, (-1, 9))
    fine.given(wx0, wy0, wz0, inv0)
    source = Stored(f0, -1)
    base = Stored(v0, -2)
    spread1 = {}
    for i in range(-1, 5):
        c = jnp.where(odd_lane, lanes(v[i], -1), v[i])
        spread1[i] = jnp.where(odd_row, rows(c, -1), c)
    v = {i: base[i] + spread1[i // 2] for i in range(-2, 10)}
    v = fine.sweep(v, source, -1, 9)
    v = fine.sweep(v, source, 0, 8)
    for i in range(8):
        out[i] = v[i][8:16]


WINDOW_PLANES = (12, 10, 8, 11, 10, 10, 10, 9, 8, 8, 8)


def f32(*shape):
    return jax.ShapeDtypeStruct(shape, jnp.float32)


def swap(x, axis, first):
    pairs = [(i, i + 1) for i in range(first, lax.axis_size(axis) - 1, 2)]
    return lax.ppermute(x, axis, pairs + [(b, a) for a, b in pairs])


def to_all(x, axis):
    copies = jnp.broadcast_to(x[None], (lax.axis_size(axis),) + x.shape)
    return lax.all_to_all(copies, axis, 0, 0)


def shards(right_side, coefficient, previous):
    even = lax.axis_index("gx") % 2 == 0
    own = lax.optimization_barrier(jnp.stack([right_side, coefficient, previous]))
    start, end = own[:, :HALO], own[:, -HALO:]
    near = swap(jnp.where(even, end, start), "gx", 0)
    far = swap(jnp.where(even, start, end), "gx", 1)

    def around(near, own, far, axis):
        return jnp.concatenate([jnp.where(even, far, near), own, jnp.where(even, near, far)], axis=axis)

    mid = around(near, own, far, 1)
    near, far = swap(mid, "gy", 0), swap(mid, "gy", 1)

    params = pltpu.CompilerParams(vmem_limit_bytes=VMEM)
    array = pl.BlockSpec(memory_space=pltpu.VMEM)
    packed, v1, *window = pl.pallas_call(
        down_kernel,
        in_specs=[array] * 3,
        out_shape=(f32(2, 128), f32(8, 128)) + tuple(f32(n, ROWS, 128) for n in WINDOW_PLANES),
        compiler_params=params,
        name="down",
    )(mid, near, far)

    gathered = to_all(to_all(packed, "gx").reshape(64, 128), "gy").reshape(1024, 128)
    vmid = around(swap(v1, "gx", 0), v1, swap(v1, "gx", 1), 0)
    vnear, vfar = swap(vmid, "gy", 0), swap(vmid, "gy", 1)

    plane = pltpu.VMEM((32 + 2 * PAD, 16, 128), jnp.float32)
    return pl.pallas_call(
        up_kernel,
        in_specs=[array] * (4 + len(WINDOW_PLANES)),
        out_shape=f32(8, 8, 128),
        scratch_shapes=[plane] * 13 + [pltpu.VMEM((8, 16, 128), jnp.float32)],
        compiler_params=params,
        name="up",
    )(gathered, *window, vmid, vnear, vfar)


def solution(mesh):
    spec = P("gx", "gy", None)
    return jax.shard_map(
        shards, mesh=mesh, in_specs=(spec,) * 3, out_specs=spec, check_vma=False
    )
```

```python
import jax
import jax.numpy as jnp
from jax import lax
from jax.experimental import pallas as pl
from jax.experimental.pallas import tpu as pltpu
from jax.sharding import PartitionSpec as P

RELAX = 0.8
KEEP = 1.0 - RELAX
HALO = 7
ROWS = 24
COARSE_SWEEPS = 8
VMEM = 48 * 1024 * 1024


def lanes(x, n):
    return pltpu.roll(x, (-n) % x.shape[1], axis=1)


def rows(x, n):
    return pltpu.roll(x, (-n) % x.shape[0], axis=0)


def iota(shape, dim):
    return lax.broadcasted_iota(jnp.int32, shape, dim)


class Window:
    def __init__(self, step, planes):
        self.step = step
        self.planes = planes

    def given(self, wx, wy, wz, inv):
        first = self.planes[0]
        self.wx, self.wy = Stored(wx, first - 1), Stored(wy, first)
        self.wz, self.inv = Stored(wz, first), Stored(inv, first)

    def hand_on(self, planes, wx, wy, wz, inv):
        first, end = planes
        for i in range(first - 1, end):
            wx[i - first + 1] = self.wx[i]
        for i in range(first, end):
            wy[i - first], wz[i - first], inv[i - first] = self.wy[i], self.wz[i], self.inv[i]

    def weights(self, coeff):
        first, end = self.planes
        lane = iota((ROWS, 128), 1)
        last = lane >= 128 - self.step
        edge = (lane < self.step) | last
        self.wx, self.wy, self.wz, self.diag, self.inv = {}, {}, {}, {}, {}
        for i in range(first - 1, end):
            self.wx[i] = coeff[i] + coeff[i + 1]
        for i in range(first, end):
            k = coeff[i]
            wy = k + rows(k, self.step)
            wz = jnp.where(last, 0.0, k + lanes(k, self.step))
            diag = self.wx[i] + self.wx[i - 1] + (wy + rows(wy, -self.step))
            diag = diag + (wz + lanes(wz, -self.step)) + jnp.where(edge, k, 0.0)
            self.wy[i], self.wz[i], self.diag[i] = wy, wz, diag
            self.inv[i] = jnp.where(k > 0.0, RELAX / diag, 0.0)

    def around(self, v, i):
        c = v[i]
        wy, wz, step = self.wy[i], self.wz[i], self.step
        total = self.wx[i] * v[i + 1] + self.wx[i - 1] * v[i - 1]
        total = total + (wy * rows(c, step) + rows(wy * c, -step))
        return total + (wz * lanes(c, step) + lanes(wz * c, -step))

    def sweep(self, v, source, first, end):
        return {
            i: KEEP * v[i] + self.inv[i] * (source[i] + self.around(v, i)) for i in range(first, end)
        }

    def residual(self, v, source, first, end):
        return {i: source[i] - self.diag[i] * v[i] + self.around(v, i) for i in range(first, end)}


class Stored:
    def __init__(self, ref, first):
        self.ref, self.first = ref, first

    def __getitem__(self, i):
        return self.ref[i - self.first]

    def __setitem__(self, i, value):
        self.ref[i - self.first] = value


def block_sum(low, high, step):
    s = low + high
    s = s + rows(s, step)
    return s + lanes(s, step)


def core_mask(rows_of):
    core = lax.rem(lax.axis_index("gy"), 2)
    return jnp.broadcast_to(core, (rows_of, 128)) == 0


def joined(first, mid, near, far):
    return jnp.concatenate([jnp.where(first, far, near), mid, jnp.where(first, near, far)], axis=0)


def down_kernel(
    mid, near, far, packed, v0_out, f0_out, f1_out, wx0, wy0, wz0, inv0, wx1, wy1, wz1, inv1
):
    first = core_mask(8)

    def field(which):
        return {
            i - HALO: joined(first, mid[which, i], near[which, i], far[which, i])
            for i in range(mid.shape[1])
        }

    source, coeff, v = field(0), field(1), field(2)
    source = {i: 2.0 * source[i] for i in range(-6, 14)}

    fine = Window(1, (-6, 14))
    fine.weights(coeff)
    v = fine.sweep(v, source, -6, 14)
    v = fine.sweep(v, source, -5, 13)
    for i in range(-2, 10):
        v0_out[i + 2] = v[i]
    for i in range(-1, 9):
        f0_out[i + 1] = source[i]
    fine.hand_on((-1, 9), wx0, wy0, wz0, inv0)
    r = fine.residual(v, source, -4, 12)

    source = {i: 0.5 * block_sum(r[2 * i], r[2 * i + 1], 1) for i in range(-2, 6)}
    coeff = {i: 0.125 * block_sum(coeff[2 * i], coeff[2 * i + 1], 1) for i in range(-3, 7)}
    for i in range(-2, 6):
        f1_out[i + 2] = source[i]
    middle = Window(2, (-2, 6))
    middle.weights(coeff)
    middle.hand_on((-2, 6), wx1, wy1, wz1, inv1)
    v = {i: middle.inv[i] * source[i] for i in range(-2, 6)}
    v = middle.sweep(v, source, -1, 5)
    even = iota((8, 128), 1) % 2 == 0
    for i in range(4):
        c = v[i][8:16]
        c = jnp.where(even, c, lanes(rows(c, 2), -1))
        packed[2 * i + 2 : 2 * i + 3, :] = c[0:1]
        packed[2 * i + 3 : 2 * i + 4, :] = c[4:5]
    r = middle.residual(v, source, 0, 4)

    source = [0.5 * block_sum(r[2 * i], r[2 * i + 1], 2)[8:16] for i in range(2)]
    coeff = [0.125 * block_sum(coeff[2 * i], coeff[2 * i + 1], 2)[8:16] for i in range(2)]
    lane, row = iota((8, 128), 1), iota((8, 128), 0)
    group = lane // 32
    pick = 4 * (lane % 32)
    for c, planes in enumerate((source, coeff)):
        dense = [jnp.take_along_axis(t, pick, axis=1) for t in planes]
        dense = jnp.where(group < 2, dense[0], dense[1])
        dense = jnp.where(row == 4 * (group % 2), dense, 0.0)
        packed[c : c + 1, :] = jnp.sum(dense, axis=0, keepdims=True)


class Coarse:
    def __init__(self, coeff, nxp, nxm, nyp, nym, ylast, yedge, zstep):
        self.nxp, self.nxm, self.nyp, self.nym, self.zstep = nxp, nxm, nyp, nym, zstep
        z = iota(coeff[0].shape, 1) % 32
        zlast = z >= 32 - zstep
        zedge = (z < zstep) | zlast
        self.wp = [k + n for k, n in zip(coeff, nxp(coeff))]
        self.wm = [k + n for k, n in zip(coeff, nxm(coeff))]
        self.wy = [jnp.where(ylast, 0.0, k + nyp(k)) for k in coeff]
        self.wz = [jnp.where(zlast, 0.0, k + lanes(k, zstep)) for k in coeff]
        self.diag = []
        for k, wp, wm, wy, wz in zip(coeff, self.wp, self.wm, self.wy, self.wz):
            diag = wp + wm + (wy + nym(wy)) + (wz + lanes(wz, -zstep))
            self.diag.append(diag + (jnp.where(yedge, k, 0.0) + jnp.where(zedge, k, 0.0)))
        self.inv = [RELAX / d for d in self.diag]

    def around(self, v):
        out = []
        for c, p, m, wp, wm, wy, wz in zip(
            v, self.nxp(v), self.nxm(v), self.wp, self.wm, self.wy, self.wz
        ):
            total = wp * p + wm * m
            total = total + (wy * self.nyp(c) + self.nym(wy * c))
            out.append(total + (wz * lanes(c, self.zstep) + lanes(wz * c, -self.zstep)))
        return out

    def first(self, source):
        return [i * f for i, f in zip(self.inv, source)]

    def sweep(self, v, source):
        around = self.around(v)
        return [KEEP * c + i * (f + t) for c, i, f, t in zip(v, self.inv, source, around)]

    def sweeps(self, v, source, count):
        step = lambda _, v: tuple(self.sweep(list(v), source))
        return list(lax.fori_loop(0, count, step, tuple(v), unroll=True))

    def residual(self, v, source):
        around = self.around(v)
        return [f - d * c + t for c, d, f, t in zip(v, self.diag, source, around)]


def above(c):
    return jnp.concatenate([c[8:], rows(c[:8], 1)], axis=0)


def below(c):
    return jnp.concatenate([rows(c[8:], -1), c[:8]], axis=0)


UNROLL = 10
PAD = 3


def up_kernel(
    mine, other, v0, f0, f1, wx0, wy0, wz0, inv0, wx1, wy1, wz1, inv1, vmid, vnear, vfar, out,
    k2, f2, va, vb, wxi, wxe, wyi, wye, wz2, diag2, inv2, sumk, sumr, e3,
):
    gx, gy = lax.axis_index("gx"), lax.axis_index("gy")
    first = core_mask(8)
    lane = iota((16, 128), 1)
    row = iota((16, 128), 0)
    group, z = lane // 32, lane % 32
    xl, yl = group // 2, group % 2
    zero = jnp.zeros((16, 128), jnp.float32)

    for ref in (k2, f2, va, vb, wxi, wxe, wyi, wye, wz2, inv2):
        for i in range(PAD):
            ref[i] = zero
            ref[32 + PAD + i] = zero
    for i in range(32):
        for c, ref in ((0, f2), (1, k2)):
            here = pl.ds(2 * i + c, 8, stride=64)
            a, b = mine[here, :], other[here, :]
            ref[i + PAD, :8] = jnp.where(first, a, b)
            ref[i + PAD, 8:] = jnp.where(first, b, a)

    def sides(c):
        up, down = lanes(c, 32), lanes(c, -32)
        inner = jnp.where(yl == 0, up, down)
        outer = jnp.where(yl == 1, above(down), below(up))
        return inner, outer

    yout = ((yl == 1) & (row == 15)) | ((yl == 0) & (row == 0))
    zlast = z == 31
    zedge = zlast | (z == 0)

    def advance(i, field, turned, body):
        before, here = turned
        after = lanes(field[i + 1], 64)
        body(i, field[i], here, jnp.where(xl == 1, after, before))
        return here, after

    def summed(k):
        k = k + lanes(k, 64)
        return k + lanes(k, 32)

    def prepare(i, k, inner, outer):
        a, b = k + inner, k + outer
        yi, yo = sides(k)
        c = k + yi
        e = jnp.where(yout, 0.0, k + yo)
        w = jnp.where(zlast, 0.0, k + lanes(k, 1))
        diag = (a + b) + (c + e) + (w + lanes(w, -1))
        diag = diag + (jnp.where(yout, k, 0.0) + jnp.where(zedge, k, 0.0))
        inv = RELAX / diag
        wxi[i], wxe[i], wyi[i], wye[i], wz2[i], diag2[i], inv2[i] = a, b, c, e, w, diag, inv
        va[i] = inv * f2[i]
        sumk[i] = summed(k)

    def around2(i, c, inner, outer):
        yi, yo = sides(c)
        w = wz2[i]
        total = wxi[i] * inner + wxe[i] * outer
        total = total + (wyi[i] * yi + wye[i] * yo)
        return total + (w * lanes(c, 1) + lanes(w * c, -1))

    def sweep2(i, c, inner, outer):
        return KEEP * c + inv2[i] * (f2[i] + around2(i, c, inner, outer))

    def first2(i, c, inner, outer):
        vb[i] = sweep2(i, c, inner, outer)

    def residual2(i, c, inner, outer):
        sumr[i] = summed(f2[i] - diag2[i] * c + around2(i, c, inner, outer))

    def three(i, state):
        ofk, ofa, ofb = state
        ofk = advance(i, k2, ofk, prepare)
        ofa = advance(i - 1, va, ofa, first2)
        return ofk, ofa, advance(i - 2, vb, ofb, residual2)

    ofk = (zero, lanes(k2[PAD], 64))
    ofk = advance(PAD, k2, ofk, prepare)
    ofk = advance(PAD + 1, k2, ofk, prepare)
    ofa = advance(PAD, va, (zero, lanes(va[PAD], 64)), first2)
    ofb = (zero, lanes(vb[PAD], 64))

    def steps(step, state):
        for u in range(UNROLL):
            state = three(PAD + 2 + UNROLL * step + u, state)
        return state

    _, ofa, ofb = lax.fori_loop(0, 30 // UNROLL, steps, (ofk, ofa, ofb))
    advance(PAD + 31, va, ofa, first2)
    ofb = advance(PAD + 30, vb, ofb, residual2)
    advance(PAD + 31, vb, ofb, residual2)

    def four(sums, q):
        t = jnp.where(group == 0, sums[4 * q + PAD], sums[4 * q + PAD + 1])
        t = jnp.where(group == 2, sums[4 * q + PAD + 2], t)
        t = jnp.where(group == 3, sums[4 * q + PAD + 3], t)
        return t + lanes(t, 1)

    c3 = [0.125 * four(sumk, q) for q in range(8)]
    f3 = [0.5 * four(sumr, q) for q in range(8)]

    def plus3(v):
        up = [lanes(c, 32) for c in v] + [zero]
        return [jnp.where(group < 3, up[q], up[q + 1]) for q in range(8)]

    def minus3(v):
        down = [zero] + [lanes(c, -32) for c in v]
        return [jnp.where(group > 0, down[q + 1], down[q]) for q in range(8)]

    level3 = Coarse(c3, plus3, minus3, above, below, row == 15, (row == 0) | (row == 15), 2)
    v3 = level3.sweep(level3.first(f3), f3)
    r3 = level3.residual(v3, f3)

    def restrict(values, x, y, zz):
        s = [t + lanes(t, x) for t in values]
        s = [y(t) for t in s]
        return [t + lanes(t, zz) for t in s]

    cores = lambda t: t[:8] + t[8:]
    f4 = [0.5 * s for s in restrict(r3, 32, cores, 2)]
    c4 = [0.125 * s for s in restrict(c3, 32, cores, 2)]
    zero8 = zero[:8]
    row8, lane8, group8 = row[:8], lane[:8], group[:8]

    def plus4(v):
        turn = [lanes(c, 64) for c in v] + [zero8]
        return [jnp.where(group8 < 2, turn[q], turn[q + 1]) for q in range(8)]

    def minus4(v):
        turn = [zero8] + [lanes(c, 64) for c in v]
        return [jnp.where(group8 < 2, turn[q], turn[q + 1]) for q in range(8)]

    def next_rows(n):
        return lambda c: rows(c, n)

    level4 = Coarse(
        c4, plus4, minus4, next_rows(1), next_rows(-1), row8 == 7, (row8 == 0) | (row8 == 7), 4
    )
    v4 = level4.sweep(level4.first(f4), f4)
    r4 = level4.residual(v4, f4)

    pair = lambda t: t + rows(t, 1)
    f5 = [0.5 * s for s in restrict(r4, 64, pair, 4)]
    c5 = [0.125 * s for s in restrict(c4, 64, pair, 4)]
    level5 = Coarse(
        c5,
        lambda v: v[1:] + [zero8],
        lambda v: [zero8] + v[:-1],
        next_rows(2),
        next_rows(-2),
        row8 >= 6,
        (row8 < 2) | (row8 >= 6),
        8,
    )
    v5 = level5.sweeps(level5.first(f5), f5, COARSE_SWEEPS - 1)

    def spread(c, bit):
        return jnp.where((iota(c.shape, 1) & bit) != 0, lanes(c, -bit), c)

    v5 = [jnp.where((row8 & 1) != 0, rows(c, -1), c) for c in v5]
    v4 = [c + spread(e, 4) for c, e in zip(v4, v5)]
    v4 = level4.sweeps(v4, f4, 2)

    v4 = [spread(jnp.where(group8 % 2 == 1, lanes(c, -32), c), 2) for c in v4]
    v3 = [c + jnp.concatenate([e, e], axis=0) for c, e in zip(v3, v4)]
    v3 = level3.sweeps(v3, f3, 2)

    for q in range(8):
        e3[q] = spread(v3[q], 1)
    for t in range(5):
        p = gx + t - 2
        inside = (p >= 0) & (p < 32)
        p = jnp.clip(p, 0, 31)
        e = jnp.where(group == jnp.where(inside, p % 4, -1), e3[p // 4], 0.0)
        va[gx + t - 2 + PAD] = vb[gx + t - 2 + PAD] + summed(e)

    def some(read, write, first, end):
        turned = [lanes(read[gx + t + PAD], 64) for t in range(first - 1, end + 1)]
        for u, t in enumerate(range(first, end)):
            i = gx + t + PAD
            outer = jnp.where(xl == 1, turned[u + 2], turned[u])
            write[i] = sweep2(i, read[i], turned[u + 1], outer)

    some(va, vb, -2, 3)
    some(vb, va, -1, 2)

    lane8 = iota((8, 128), 1)
    pick = 32 * (iota((8, 128), 0) // 4) + lane8 // 4
    wide = {}
    for t in range(-1, 2):
        for x in range(2):
            parts = []
            for b in range(-1, 2):
                y = gy + b
                inside = (y >= 0) & (y < 16)
                y = jnp.clip(y, 0, 15)
                line = va[gx + t + PAD, pl.ds(8 * (y % 2) + y // 2, 1), :]
                line = jnp.broadcast_to(jnp.where(inside, line, 0.0), (8, 128))
                parts.append(jnp.take_along_axis(line, 64 * x + pick, axis=1))
            wide[t, x] = jnp.concatenate(parts, axis=0)

    def correction(i):
        return wide[i // 4, (i % 4) // 2]

    middle = Window(2, (-2, 6))
    middle.given(wx1, wy1, wz1, inv1)
    source = Stored(f1, -2)
    upper_half = iota((8, 128), 0) >= 4
    second = (iota((ROWS, 128), 0) & 2) != 0

    def received(i):
        n = 2 * i + 8
        c = [jnp.where(upper_half, r[n + 1 : n + 2], r[n : n + 1]) for r in (vmid, vnear, vfar)]
        c = joined(first, *c)
        return jnp.where(second, lanes(c, 1), c)

    v = {i: received(i) + correction(i) for i in range(-3, 7)}
    v = middle.sweep(v, source, -2, 6)
    v = middle.sweep(v, source, -1, 5)

    odd_lane = iota((ROWS, 128), 1) % 2 == 1
    odd_row = iota((ROWS, 128), 0) % 2 == 1
    fine = Window(1, (-1, 9))
    fine.given(wx0, wy0, wz0, inv0)
    source = Stored(f0, -1)
    base = Stored(v0, -2)
    spread1 = {}
    for i in range(-1, 5):
        c = jnp.where(odd_lane, lanes(v[i], -1), v[i])
        spread1[i] = jnp.where(odd_row, rows(c, -1), c)
    v = {i: base[i] + spread1[i // 2] for i in range(-2, 10)}
    v = fine.sweep(v, source, -1, 9)
    v = fine.sweep(v, source, 0, 8)
    for i in range(8):
        out[i] = v[i][8:16]


WINDOW_PLANES = (12, 10, 8, 11, 10, 10, 10, 9, 8, 8, 8)


def f32(*shape):
    return jax.ShapeDtypeStruct(shape, jnp.float32)


def swap(x, axis, first):
    pairs = [(i, i + 1) for i in range(first, lax.axis_size(axis) - 1, 2)]
    return lax.ppermute(x, axis, pairs + [(b, a) for a, b in pairs])


def to_all(x, axis, count, groups=None):
    copies = jnp.broadcast_to(x[None], (count,) + x.shape)
    return lax.all_to_all(copies, axis, 0, 0, axis_index_groups=groups)


def shards(right_side, coefficient, previous):
    even = lax.axis_index("gx") % 2 == 0
    own = lax.optimization_barrier(jnp.stack([right_side, coefficient, previous]))
    start, end = own[:, :HALO], own[:, -HALO:]
    near = swap(jnp.where(even, end, start), "gx", 0)
    far = swap(jnp.where(even, start, end), "gx", 1)

    mid = jnp.concatenate([jnp.where(even, far, near), own, jnp.where(even, near, far)], axis=1)
    near, far = swap(mid, "gy", 0), swap(mid, "gy", 1)

    params = pltpu.CompilerParams(vmem_limit_bytes=VMEM)
    array = pl.BlockSpec(memory_space=pltpu.VMEM)
    packed, *window = pl.pallas_call(
        down_kernel,
        in_specs=[array] * 3,
        out_shape=(f32(10, 128),) + tuple(f32(n, ROWS, 128) for n in WINDOW_PLANES),
        compiler_params=params,
        name="down",
    )(mid, near, far)

    blocks = to_all(packed.reshape(1, 1280), "gx", 32)
    same_core = [[2 * z + c for z in range(8)] for c in range(2)]
    mine = to_all(blocks[:, :, :256].reshape(64, 128), "gy", 8, same_core).reshape(512, 128)
    v1 = jnp.pad(blocks[:, 0, 256:], ((1, 1), (0, 0)))
    place = (lax.axis_index("gx"), jnp.int32(0))
    vmid = lax.dynamic_slice(v1, place, (3, 1024)).reshape(24, 128)
    vnear, vfar = swap(vmid, "gy", 0), swap(vmid, "gy", 1)
    mine, vnear, vfar = lax.optimization_barrier((mine, vnear, vfar))
    other = swap(mine, "gy", 0)

    plane = pltpu.VMEM((32 + 2 * PAD, 16, 128), jnp.float32)
    return pl.pallas_call(
        up_kernel,
        in_specs=[array] * (5 + len(WINDOW_PLANES)),
        out_shape=f32(8, 8, 128),
        scratch_shapes=[plane] * 13 + [pltpu.VMEM((8, 16, 128), jnp.float32)],
        compiler_params=params,
        name="up",
    )(mine, other, *window, vmid, vnear, vfar)


def solution(mesh):
    spec = P("gx", "gy", None)
    return jax.shard_map(
        shards, mesh=mesh, in_specs=(spec,) * 3, out_specs=spec, check_vma=False
    )
```

```python
import jax
import jax.numpy as jnp
from jax import lax
from jax.experimental import pallas as pl
from jax.experimental.pallas import tpu as pltpu
from jax.sharding import PartitionSpec as P

RELAX = 0.8
KEEP = 1.0 - RELAX
HALO = 7
ROWS = 24
COARSE_SWEEPS = 8
VMEM = 48 * 1024 * 1024


def lanes(x, n):
    return pltpu.roll(x, (-n) % x.shape[1], axis=1)


def rows(x, n):
    return pltpu.roll(x, (-n) % x.shape[0], axis=0)


def iota(shape, dim):
    return lax.broadcasted_iota(jnp.int32, shape, dim)


class Window:
    def __init__(self, step, planes):
        self.step = step
        self.planes = planes

    def given(self, wx, wy, wz, inv):
        first = self.planes[0]
        self.wx, self.wy = Stored(wx, first - 1), Stored(wy, first)
        self.wz, self.inv = Stored(wz, first), Stored(inv, first)

    def hand_on(self, planes, wx, wy, wz, inv):
        first, end = planes
        for i in range(first - 1, end):
            wx[i - first + 1] = self.wx[i]
        for i in range(first, end):
            wy[i - first], wz[i - first], inv[i - first] = self.wy[i], self.wz[i], self.inv[i]

    def weights(self, coeff):
        first, end = self.planes
        lane = iota((ROWS, 128), 1)
        last = lane >= 128 - self.step
        edge = (lane < self.step) | last
        self.wx, self.wy, self.wz, self.diag, self.inv = {}, {}, {}, {}, {}
        for i in range(first - 1, end):
            self.wx[i] = coeff[i] + coeff[i + 1]
        for i in range(first, end):
            k = coeff[i]
            wy = k + rows(k, self.step)
            wz = jnp.where(last, 0.0, k + lanes(k, self.step))
            diag = self.wx[i] + self.wx[i - 1] + (wy + rows(wy, -self.step))
            diag = diag + (wz + lanes(wz, -self.step)) + jnp.where(edge, k, 0.0)
            self.wy[i], self.wz[i], self.diag[i] = wy, wz, diag
            self.inv[i] = jnp.where(k > 0.0, RELAX / diag, 0.0)

    def around(self, v, i):
        c = v[i]
        wy, wz, step = self.wy[i], self.wz[i], self.step
        total = self.wx[i] * v[i + 1] + self.wx[i - 1] * v[i - 1]
        total = total + (wy * rows(c, step) + rows(wy * c, -step))
        return total + (wz * lanes(c, step) + lanes(wz * c, -step))

    def sweep(self, v, source, first, end):
        return {
            i: KEEP * v[i] + self.inv[i] * (source[i] + self.around(v, i)) for i in range(first, end)
        }

    def residual(self, v, source, first, end):
        return {i: source[i] - self.diag[i] * v[i] + self.around(v, i) for i in range(first, end)}


class Stored:
    def __init__(self, ref, first):
        self.ref, self.first = ref, first

    def __getitem__(self, i):
        return self.ref[i - self.first]

    def __setitem__(self, i, value):
        self.ref[i - self.first] = value


def block_sum(low, high, step):
    s = low + high
    s = s + rows(s, step)
    return s + lanes(s, step)


def alone(*planes):
    return [(i, 8, None) for i in planes]


INNER = range(8)
NARROW = [(0, 6, -6), (7, 6, 13)] + alone(1, 2, 3, 4, 5, 6, -1, -2, 8, 9)
NARROW += [(-3, 5, -5), (10, 5, 12), (-4, 4, 11)]
WIDE = alone(*INNER, -1, -2, 8, 9)
WIDE += [(-3, 6, -7), (10, 6, 14), (-4, 5, -6), (11, 5, 13), (-5, 4, 12)]
TILES = (NARROW, WIDE, WIDE)


def planes_of(which, own, near, far):
    even = jnp.broadcast_to(lax.rem(lax.axis_index("gx"), 2), (8, 128)) == 0
    planes = {i: own[which, i] for i in INNER}
    for i in range(HALO):
        a, b = near[which, i], far[which, i]
        planes[i - HALO], planes[i + 8] = jnp.where(even, b, a), jnp.where(even, a, b)
    return planes


def pack_kernel(own, near, far, to_near, to_far):
    first = core_mask(8)
    row = iota((8, 128), 0)
    at = 0
    for which, tiles in enumerate(TILES):
        planes = planes_of(which, own, near, far)
        for a, n, b in tiles:
            upward = downward = planes[a]
            if b is not None:
                upward = jnp.where(row >= 8 - n, planes[a], rows(planes[b], n))
                downward = jnp.where(row < n, planes[a], rows(planes[b], -n))
            to_near[at] = jnp.where(first, upward, downward)
            to_far[at] = jnp.where(first, downward, upward)
            at += 1


def core_mask(rows_of):
    core = lax.rem(lax.axis_index("gy"), 2)
    return jnp.broadcast_to(core, (rows_of, 128)) == 0


def joined(first, mid, near, far):
    return jnp.concatenate([jnp.where(first, far, near), mid, jnp.where(first, near, far)], axis=0)


def down_kernel(
    own, xnear, xfar, near, far, packed, v0_out, f0_out, f1_out, wx0, wy0, wz0, inv0, wx1, wy1, wz1, inv1
):
    first = core_mask(8)

    fields, at = [], 0
    for which, tiles in enumerate(TILES):
        mid = planes_of(which, own, xnear, xfar)
        low, high = {}, {}
        for i, n, other in tiles:
            below_it, above_it = jnp.where(first, far[at], near[at]), jnp.where(first, near[at], far[at])
            low[i], high[i] = below_it, above_it
            if other is not None:
                low[other], high[other] = rows(below_it, -n), rows(above_it, n)
            at += 1
        fields.append({i: jnp.concatenate([low[i], mid[i], high[i]], axis=0) for i in low})
    source, coeff, v = fields
    source = {i: 2.0 * source[i] for i in range(-6, 14)}

    fine = Window(1, (-6, 14))
    fine.weights(coeff)
    v = fine.sweep(v, source, -6, 14)
    v = fine.sweep(v, source, -5, 13)
    for i in range(-2, 10):
        v0_out[i + 2] = v[i]
    for i in range(-1, 9):
        f0_out[i + 1] = source[i]
    fine.hand_on((-1, 9), wx0, wy0, wz0, inv0)
    r = fine.residual(v, source, -4, 12)

    source = {i: 0.5 * block_sum(r[2 * i], r[2 * i + 1], 1) for i in range(-2, 6)}
    coeff = {i: 0.125 * block_sum(coeff[2 * i], coeff[2 * i + 1], 1) for i in range(-3, 7)}
    for i in range(-2, 6):
        f1_out[i + 2] = source[i]
    middle = Window(2, (-2, 6))
    middle.weights(coeff)
    middle.hand_on((-2, 6), wx1, wy1, wz1, inv1)
    v = {i: middle.inv[i] * source[i] for i in range(-2, 6)}
    v = middle.sweep(v, source, -1, 5)
    even = iota((8, 128), 1) % 2 == 0
    for i in range(4):
        c = v[i][8:16]
        c = jnp.where(even, c, lanes(rows(c, 2), -1))
        packed[2 * i + 2 : 2 * i + 3, :] = c[0:1]
        packed[2 * i + 3 : 2 * i + 4, :] = c[4:5]
    r = middle.residual(v, source, 0, 4)

    source = [0.5 * block_sum(r[2 * i], r[2 * i + 1], 2)[8:16] for i in range(2)]
    coeff = [0.125 * block_sum(coeff[2 * i], coeff[2 * i + 1], 2)[8:16] for i in range(2)]
    lane, row = iota((8, 128), 1), iota((8, 128), 0)
    group = lane // 32
    pick = 4 * (lane % 32)
    for c, planes in enumerate((source, coeff)):
        dense = [jnp.take_along_axis(t, pick, axis=1) for t in planes]
        dense = jnp.where(group < 2, dense[0], dense[1])
        dense = jnp.where(row == 4 * (group % 2), dense, 0.0)
        packed[c : c + 1, :] = jnp.sum(dense, axis=0, keepdims=True)


class Coarse:
    def __init__(self, coeff, nxp, nxm, nyp, nym, ylast, yedge, zstep):
        self.nxp, self.nxm, self.nyp, self.nym, self.zstep = nxp, nxm, nyp, nym, zstep
        z = iota(coeff[0].shape, 1) % 32
        zlast = z >= 32 - zstep
        zedge = (z < zstep) | zlast
        self.wp = [k + n for k, n in zip(coeff, nxp(coeff))]
        self.wm = [k + n for k, n in zip(coeff, nxm(coeff))]
        self.wy = [jnp.where(ylast, 0.0, k + nyp(k)) for k in coeff]
        self.wz = [jnp.where(zlast, 0.0, k + lanes(k, zstep)) for k in coeff]
        self.diag = []
        for k, wp, wm, wy, wz in zip(coeff, self.wp, self.wm, self.wy, self.wz):
            diag = wp + wm + (wy + nym(wy)) + (wz + lanes(wz, -zstep))
            self.diag.append(diag + (jnp.where(yedge, k, 0.0) + jnp.where(zedge, k, 0.0)))
        self.inv = [RELAX / d for d in self.diag]

    def around(self, v):
        out = []
        for c, p, m, wp, wm, wy, wz in zip(
            v, self.nxp(v), self.nxm(v), self.wp, self.wm, self.wy, self.wz
        ):
            total = wp * p + wm * m
            total = total + (wy * self.nyp(c) + self.nym(wy * c))
            out.append(total + (wz * lanes(c, self.zstep) + lanes(wz * c, -self.zstep)))
        return out

    def first(self, source):
        return [i * f for i, f in zip(self.inv, source)]

    def sweep(self, v, source):
        around = self.around(v)
        return [KEEP * c + i * (f + t) for c, i, f, t in zip(v, self.inv, source, around)]

    def sweeps(self, v, source, count):
        step = lambda _, v: tuple(self.sweep(list(v), source))
        return list(lax.fori_loop(0, count, step, tuple(v), unroll=True))

    def residual(self, v, source):
        around = self.around(v)
        return [f - d * c + t for c, d, f, t in zip(v, self.diag, source, around)]


def above(c):
    return jnp.concatenate([c[8:], rows(c[:8], 1)], axis=0)


def below(c):
    return jnp.concatenate([rows(c[8:], -1), c[:8]], axis=0)


UNROLL = 10
PAD = 3


def up_kernel(
    mine, other, v0, f0, f1, wx0, wy0, wz0, inv0, wx1, wy1, wz1, inv1, vmid, vnear, vfar, out,
    k2, f2, va, vb, wxi, wxe, wyi, wye, wz2, diag2, inv2, sumk, sumr, e3,
):
    gx, gy = lax.axis_index("gx"), lax.axis_index("gy")
    first = core_mask(8)
    lane = iota((16, 128), 1)
    row = iota((16, 128), 0)
    group, z = lane // 32, lane % 32
    xl, yl = group // 2, group % 2
    zero = jnp.zeros((16, 128), jnp.float32)

    for ref in (k2, f2, va, vb, wxi, wxe, wyi, wye, wz2, inv2):
        for i in range(PAD):
            ref[i] = zero
            ref[32 + PAD + i] = zero
    for i in range(32):
        for c, ref in ((0, f2), (1, k2)):
            here = pl.ds(2 * i + c, 8, stride=64)
            a, b = mine[here, :], other[here, :]
            ref[i + PAD, :8] = jnp.where(first, a, b)
            ref[i + PAD, 8:] = jnp.where(first, b, a)

    def sides(c):
        up, down = lanes(c, 32), lanes(c, -32)
        inner = jnp.where(yl == 0, up, down)
        outer = jnp.where(yl == 1, above(down), below(up))
        return inner, outer

    yout = ((yl == 1) & (row == 15)) | ((yl == 0) & (row == 0))
    zlast = z == 31
    zedge = zlast | (z == 0)

    def advance(i, field, turned, body):
        before, here = turned
        after = lanes(field[i + 1], 64)
        body(i, field[i], here, jnp.where(xl == 1, after, before))
        return here, after

    def summed(k):
        k = k + lanes(k, 64)
        return k + lanes(k, 32)

    def prepare(i, k, inner, outer):
        a, b = k + inner, k + outer
        yi, yo = sides(k)
        c = k + yi
        e = jnp.where(yout, 0.0, k + yo)
        w = jnp.where(zlast, 0.0, k + lanes(k, 1))
        diag = (a + b) + (c + e) + (w + lanes(w, -1))
        diag = diag + (jnp.where(yout, k, 0.0) + jnp.where(zedge, k, 0.0))
        inv = RELAX / diag
        wxi[i], wxe[i], wyi[i], wye[i], wz2[i], diag2[i], inv2[i] = a, b, c, e, w, diag, inv
        va[i] = inv * f2[i]
        sumk[i] = summed(k)

    def around2(i, c, inner, outer):
        yi, yo = sides(c)
        w = wz2[i]
        total = wxi[i] * inner + wxe[i] * outer
        total = total + (wyi[i] * yi + wye[i] * yo)
        return total + (w * lanes(c, 1) + lanes(w * c, -1))

    def sweep2(i, c, inner, outer):
        return KEEP * c + inv2[i] * (f2[i] + around2(i, c, inner, outer))

    def first2(i, c, inner, outer):
        vb[i] = sweep2(i, c, inner, outer)

    def residual2(i, c, inner, outer):
        sumr[i] = summed(f2[i] - diag2[i] * c + around2(i, c, inner, outer))

    def three(i, state):
        ofk, ofa, ofb = state
        ofk = advance(i, k2, ofk, prepare)
        ofa = advance(i - 1, va, ofa, first2)
        return ofk, ofa, advance(i - 2, vb, ofb, residual2)

    ofk = (zero, lanes(k2[PAD], 64))
    ofk = advance(PAD, k2, ofk, prepare)
    ofk = advance(PAD + 1, k2, ofk, prepare)
    ofa = advance(PAD, va, (zero, lanes(va[PAD], 64)), first2)
    ofb = (zero, lanes(vb[PAD], 64))

    def steps(step, state):
        for u in range(UNROLL):
            state = three(PAD + 2 + UNROLL * step + u, state)
        return state

    _, ofa, ofb = lax.fori_loop(0, 30 // UNROLL, steps, (ofk, ofa, ofb))
    advance(PAD + 31, va, ofa, first2)
    ofb = advance(PAD + 30, vb, ofb, residual2)
    advance(PAD + 31, vb, ofb, residual2)

    def four(sums, q):
        t = jnp.where(group == 0, sums[4 * q + PAD], sums[4 * q + PAD + 1])
        t = jnp.where(group == 2, sums[4 * q + PAD + 2], t)
        t = jnp.where(group == 3, sums[4 * q + PAD + 3], t)
        return t + lanes(t, 1)

    c3 = [0.125 * four(sumk, q) for q in range(8)]
    f3 = [0.5 * four(sumr, q) for q in range(8)]

    def plus3(v):
        up = [lanes(c, 32) for c in v] + [zero]
        return [jnp.where(group < 3, up[q], up[q + 1]) for q in range(8)]

    def minus3(v):
        down = [zero] + [lanes(c, -32) for c in v]
        return [jnp.where(group > 0, down[q + 1], down[q]) for q in range(8)]

    level3 = Coarse(c3, plus3, minus3, above, below, row == 15, (row == 0) | (row == 15), 2)
    v3 = level3.sweep(level3.first(f3), f3)
    r3 = level3.residual(v3, f3)

    def restrict(values, x, y, zz):
        s = [t + lanes(t, x) for t in values]
        s = [y(t) for t in s]
        return [t + lanes(t, zz) for t in s]

    cores = lambda t: t[:8] + t[8:]
    f4 = [0.5 * s for s in restrict(r3, 32, cores, 2)]
    c4 = [0.125 * s for s in restrict(c3, 32, cores, 2)]
    zero8 = zero[:8]
    row8, lane8, group8 = row[:8], lane[:8], group[:8]

    def plus4(v):
        turn = [lanes(c, 64) for c in v] + [zero8]
        return [jnp.where(group8 < 2, turn[q], turn[q + 1]) for q in range(8)]

    def minus4(v):
        turn = [zero8] + [lanes(c, 64) for c in v]
        return [jnp.where(group8 < 2, turn[q], turn[q + 1]) for q in range(8)]

    def next_rows(n):
        return lambda c: rows(c, n)

    level4 = Coarse(
        c4, plus4, minus4, next_rows(1), next_rows(-1), row8 == 7, (row8 == 0) | (row8 == 7), 4
    )
    v4 = level4.sweep(level4.first(f4), f4)
    r4 = level4.residual(v4, f4)

    pair = lambda t: t + rows(t, 1)
    f5 = [0.5 * s for s in restrict(r4, 64, pair, 4)]
    c5 = [0.125 * s for s in restrict(c4, 64, pair, 4)]
    level5 = Coarse(
        c5,
        lambda v: v[1:] + [zero8],
        lambda v: [zero8] + v[:-1],
        next_rows(2),
        next_rows(-2),
        row8 >= 6,
        (row8 < 2) | (row8 >= 6),
        8,
    )
    v5 = level5.sweeps(level5.first(f5), f5, COARSE_SWEEPS - 1)

    def spread(c, bit):
        return jnp.where((iota(c.shape, 1) & bit) != 0, lanes(c, -bit), c)

    v5 = [jnp.where((row8 & 1) != 0, rows(c, -1), c) for c in v5]
    v4 = [c + spread(e, 4) for c, e in zip(v4, v5)]
    v4 = level4.sweeps(v4, f4, 2)

    v4 = [spread(jnp.where(group8 % 2 == 1, lanes(c, -32), c), 2) for c in v4]
    v3 = [c + jnp.concatenate([e, e], axis=0) for c, e in zip(v3, v4)]
    v3 = level3.sweeps(v3, f3, 2)

    for q in range(8):
        e3[q] = spread(v3[q], 1)
    for t in range(5):
        p = gx + t - 2
        inside = (p >= 0) & (p < 32)
        p = jnp.clip(p, 0, 31)
        e = jnp.where(group == jnp.where(inside, p % 4, -1), e3[p // 4], 0.0)
        va[gx + t - 2 + PAD] = vb[gx + t - 2 + PAD] + summed(e)

    def some(read, write, first, end):
        turned = [lanes(read[gx + t + PAD], 64) for t in range(first - 1, end + 1)]
        for u, t in enumerate(range(first, end)):
            i = gx + t + PAD
            outer = jnp.where(xl == 1, turned[u + 2], turned[u])
            write[i] = sweep2(i, read[i], turned[u + 1], outer)

    some(va, vb, -2, 3)
    some(vb, va, -1, 2)

    lane8 = iota((8, 128), 1)
    pick = 32 * (iota((8, 128), 0) // 4) + lane8 // 4
    wide = {}
    for t in range(-1, 2):
        for x in range(2):
            parts = []
            for b in range(-1, 2):
                y = gy + b
                inside = (y >= 0) & (y < 16)
                y = jnp.clip(y, 0, 15)
                line = va[gx + t + PAD, pl.ds(8 * (y % 2) + y // 2, 1), :]
                line = jnp.broadcast_to(jnp.where(inside, line, 0.0), (8, 128))
                parts.append(jnp.take_along_axis(line, 64 * x + pick, axis=1))
            wide[t, x] = jnp.concatenate(parts, axis=0)

    def correction(i):
        return wide[i // 4, (i % 4) // 2]

    middle = Window(2, (-2, 6))
    middle.given(wx1, wy1, wz1, inv1)
    source = Stored(f1, -2)
    upper_half = iota((8, 128), 0) >= 4
    second = (iota((ROWS, 128), 0) & 2) != 0

    def received(i):
        n = 2 * i + 8
        c = [jnp.where(upper_half, r[n + 1 : n + 2], r[n : n + 1]) for r in (vmid, vnear, vfar)]
        c = joined(first, *c)
        return jnp.where(second, lanes(c, 1), c)

    v = {i: received(i) + correction(i) for i in range(-3, 7)}
    v = middle.sweep(v, source, -2, 6)
    v = middle.sweep(v, source, -1, 5)

    odd_lane = iota((ROWS, 128), 1) % 2 == 1
    odd_row = iota((ROWS, 128), 0) % 2 == 1
    fine = Window(1, (-1, 9))
    fine.given(wx0, wy0, wz0, inv0)
    source = Stored(f0, -1)
    base = Stored(v0, -2)
    spread1 = {}
    for i in range(-1, 5):
        c = jnp.where(odd_lane, lanes(v[i], -1), v[i])
        spread1[i] = jnp.where(odd_row, rows(c, -1), c)
    v = {i: base[i] + spread1[i // 2] for i in range(-2, 10)}
    v = fine.sweep(v, source, -1, 9)
    v = fine.sweep(v, source, 0, 8)
    for i in range(8):
        out[i] = v[i][8:16]


WINDOW_PLANES = (12, 10, 8, 11, 10, 10, 10, 9, 8, 8, 8)


def f32(*shape):
    return jax.ShapeDtypeStruct(shape, jnp.float32)


def swap(x, axis, first):
    pairs = [(i, i + 1) for i in range(first, lax.axis_size(axis) - 1, 2)]
    return lax.ppermute(x, axis, pairs + [(b, a) for a, b in pairs])


def to_all(x, axis, count, groups=None):
    copies = jnp.broadcast_to(x[None], (count,) + x.shape)
    return lax.all_to_all(copies, axis, 0, 0, axis_index_groups=groups)


def shards(right_side, coefficient, previous):
    even = lax.axis_index("gx") % 2 == 0
    own = lax.optimization_barrier(jnp.concatenate([right_side, coefficient, previous])).reshape(3, 8, 8, 128)
    start, end = own[:, :HALO], own[:, -HALO:]
    near = swap(jnp.where(even, end, start), "gx", 0)
    far = swap(jnp.where(even, start, end), "gx", 1)

    params = pltpu.CompilerParams(vmem_limit_bytes=VMEM)
    array = pl.BlockSpec(memory_space=pltpu.VMEM)
    count = sum(len(tiles) for tiles in TILES)
    to_near, to_far = pl.pallas_call(
        pack_kernel,
        in_specs=[array] * 3,
        out_shape=(f32(count, 8, 128),) * 2,
        compiler_params=params,
        name="pack",
    )(own, near, far)
    from_near, from_far = swap(to_near, "gy", 0), swap(to_far, "gy", 1)

    packed, *window = pl.pallas_call(
        down_kernel,
        in_specs=[array] * 5,
        out_shape=(f32(10, 128),) + tuple(f32(n, ROWS, 128) for n in WINDOW_PLANES),
        compiler_params=params,
        name="down",
    )(own, near, far, from_near, from_far)

    blocks = to_all(packed.reshape(1, 1280), "gx", 32)
    same_core = [[2 * z + c for z in range(8)] for c in range(2)]
    mine = to_all(blocks[:, :, :256].reshape(64, 128), "gy", 8, same_core).reshape(512, 128)
    v1 = jnp.pad(blocks[:, 0, 256:], ((1, 1), (0, 0)))
    place = (lax.axis_index("gx"), jnp.int32(0))
    vmid = lax.dynamic_slice(v1, place, (3, 1024)).reshape(24, 128)
    vnear, vfar = swap(vmid, "gy", 0), swap(vmid, "gy", 1)
    mine, vnear, vfar = lax.optimization_barrier((mine, vnear, vfar))
    other = swap(mine, "gy", 0)

    plane = pltpu.VMEM((32 + 2 * PAD, 16, 128), jnp.float32)
    return pl.pallas_call(
        up_kernel,
        in_specs=[array] * (5 + len(WINDOW_PLANES)),
        out_shape=f32(8, 8, 128),
        scratch_shapes=[plane] * 13 + [pltpu.VMEM((8, 16, 128), jnp.float32)],
        compiler_params=params,
        name="up",
    )(mine, other, *window, vmid, vnear, vfar)


def solution(mesh):
    spec = P("gx", "gy", None)
    return jax.shard_map(
        shards, mesh=mesh, in_specs=(spec,) * 3, out_specs=spec, check_vma=False
    )
```

```python
import jax
import jax.numpy as jnp
from jax import lax
from jax.experimental import pallas as pl
from jax.experimental.pallas import tpu as pltpu
from jax.sharding import PartitionSpec as P

RELAX = 0.8
KEEP = 1.0 - RELAX
HALO = 7
ROWS = 24
COARSE_SWEEPS = 8
VMEM = 48 * 1024 * 1024


def lanes(x, n):
    return pltpu.roll(x, (-n) % x.shape[1], axis=1)


def rows(x, n):
    return pltpu.roll(x, (-n) % x.shape[0], axis=0)


def iota(shape, dim):
    return lax.broadcasted_iota(jnp.int32, shape, dim)


class Window:
    def __init__(self, step, planes):
        self.step = step
        self.planes = planes

    def given(self, wx, wy, wz, inv):
        first = self.planes[0]
        self.wx, self.wy = Stored(wx, first - 1), Stored(wy, first)
        self.wz, self.inv = Stored(wz, first), Stored(inv, first)

    def hand_on(self, planes, wx, wy, wz, inv):
        first, end = planes
        for i in range(first - 1, end):
            wx[i - first + 1] = self.wx[i]
        for i in range(first, end):
            wy[i - first], wz[i - first], inv[i - first] = self.wy[i], self.wz[i], self.inv[i]

    def weights(self, coeff):
        first, end = self.planes
        lane = iota((ROWS, 128), 1)
        last = lane >= 128 - self.step
        edge = (lane < self.step) | last
        self.wx, self.wy, self.wz, self.diag, self.inv = {}, {}, {}, {}, {}
        for i in range(first - 1, end):
            self.wx[i] = coeff[i] + coeff[i + 1]
        for i in range(first, end):
            k = coeff[i]
            wy = k + rows(k, self.step)
            wz = jnp.where(last, 0.0, k + lanes(k, self.step))
            diag = self.wx[i] + self.wx[i - 1] + (wy + rows(wy, -self.step))
            diag = diag + (wz + lanes(wz, -self.step)) + jnp.where(edge, k, 0.0)
            self.wy[i], self.wz[i], self.diag[i] = wy, wz, diag
            self.inv[i] = jnp.where(k > 0.0, RELAX / diag, 0.0)

    def around(self, v, i):
        c = v[i]
        wy, wz, step = self.wy[i], self.wz[i], self.step
        total = self.wx[i] * v[i + 1] + self.wx[i - 1] * v[i - 1]
        total = total + (wy * rows(c, step) + rows(wy * c, -step))
        return total + (wz * lanes(c, step) + lanes(wz * c, -step))

    def sweep(self, v, source, first, end):
        return {
            i: KEEP * v[i] + self.inv[i] * (source[i] + self.around(v, i)) for i in range(first, end)
        }

    def residual(self, v, source, first, end):
        return {i: source[i] - self.diag[i] * v[i] + self.around(v, i) for i in range(first, end)}


class Stored:
    def __init__(self, ref, first):
        self.ref, self.first = ref, first

    def __getitem__(self, i):
        return self.ref[i - self.first]

    def __setitem__(self, i, value):
        self.ref[i - self.first] = value


def block_sum(low, high, step):
    s = low + high
    s = s + rows(s, step)
    return s + lanes(s, step)


def alone(*planes):
    return [(i, 8, None) for i in planes]


INNER = range(8)
NARROW = [(0, 6, -6), (7, 6, 13)] + alone(1, 2, 3, 4, 5, 6, -1, -2, 8, 9)
NARROW += [(-3, 5, -5), (10, 5, 12), (-4, 4, 11)]
WIDE = alone(*INNER, -1, -2, 8, 9)
WIDE += [(-3, 6, -7), (10, 6, 14), (-4, 5, -6), (11, 5, 13), (-5, 4, 12)]
TILES = (NARROW, WIDE, WIDE)


def planes_of(which, own, near, far):
    even = jnp.broadcast_to(lax.rem(lax.axis_index("gx"), 2), (8, 128)) == 0
    planes = {i: own[which, i] for i in INNER}
    for i in range(HALO):
        a, b = near[which, i], far[which, i]
        planes[i - HALO], planes[i + 8] = jnp.where(even, b, a), jnp.where(even, a, b)
    return planes


def pack_kernel(own, near, far, to_near, to_far):
    first = core_mask(8)
    row = iota((8, 128), 0)
    at = 0
    for which, tiles in enumerate(TILES):
        planes = planes_of(which, own, near, far)
        for a, n, b in tiles:
            upward = downward = planes[a]
            if b is not None:
                upward = jnp.where(row >= 8 - n, planes[a], rows(planes[b], n))
                downward = jnp.where(row < n, planes[a], rows(planes[b], -n))
            to_near[at] = jnp.where(first, upward, downward)
            to_far[at] = jnp.where(first, downward, upward)
            at += 1


def core_mask(rows_of):
    core = lax.rem(lax.axis_index("gy"), 2)
    return jnp.broadcast_to(core, (rows_of, 128)) == 0


def joined(first, mid, near, far):
    return jnp.concatenate([jnp.where(first, far, near), mid, jnp.where(first, near, far)], axis=0)


def down_kernel(
    own, xnear, xfar, far, near, packed, v0_out, f0_out, f1_out, wx0, wy0, wz0, inv0, wx1, wy1, wz1, inv1
):
    first = core_mask(8)

    fields, at = [], 0
    for which, tiles in enumerate(TILES):
        mid = planes_of(which, own, xnear, xfar)
        low, high = {}, {}
        for i, n, other in tiles:
            below_it, above_it = jnp.where(first, far[at], near[at]), jnp.where(first, near[at], far[at])
            low[i], high[i] = below_it, above_it
            if other is not None:
                low[other], high[other] = rows(below_it, -n), rows(above_it, n)
            at += 1
        fields.append({i: jnp.concatenate([low[i], mid[i], high[i]], axis=0) for i in low})
    source, coeff, v = fields
    source = {i: 2.0 * source[i] for i in range(-6, 14)}

    fine = Window(1, (-6, 14))
    fine.weights(coeff)
    v = fine.sweep(v, source, -6, 14)
    v = fine.sweep(v, source, -5, 13)
    for i in range(-2, 10):
        v0_out[i + 2] = v[i]
    for i in range(-1, 9):
        f0_out[i + 1] = source[i]
    fine.hand_on((-1, 9), wx0, wy0, wz0, inv0)
    r = fine.residual(v, source, -4, 12)

    source = {i: 0.5 * block_sum(r[2 * i], r[2 * i + 1], 1) for i in range(-2, 6)}
    coeff = {i: 0.125 * block_sum(coeff[2 * i], coeff[2 * i + 1], 1) for i in range(-3, 7)}
    for i in range(-2, 6):
        f1_out[i + 2] = source[i]
    middle = Window(2, (-2, 6))
    middle.weights(coeff)
    middle.hand_on((-2, 6), wx1, wy1, wz1, inv1)
    v = {i: middle.inv[i] * source[i] for i in range(-2, 6)}
    v = middle.sweep(v, source, -1, 5)
    even = iota((8, 128), 1) % 2 == 0
    for i in range(4):
        c = v[i][8:16]
        c = jnp.where(even, c, lanes(rows(c, 2), -1))
        packed[2 * i + 2 : 2 * i + 3, :] = c[0:1]
        packed[2 * i + 3 : 2 * i + 4, :] = c[4:5]
    r = middle.residual(v, source, 0, 4)

    source = [0.5 * block_sum(r[2 * i], r[2 * i + 1], 2)[8:16] for i in range(2)]
    coeff = [0.125 * block_sum(coeff[2 * i], coeff[2 * i + 1], 2)[8:16] for i in range(2)]
    lane, row = iota((8, 128), 1), iota((8, 128), 0)
    group = lane // 32
    pick = 4 * (lane % 32)
    for c, planes in enumerate((source, coeff)):
        dense = [jnp.take_along_axis(t, pick, axis=1) for t in planes]
        dense = jnp.where(group < 2, dense[0], dense[1])
        dense = jnp.where(row == 4 * (group % 2), dense, 0.0)
        packed[c : c + 1, :] = jnp.sum(dense, axis=0, keepdims=True)


class Coarse:
    def __init__(self, coeff, nxp, nxm, nyp, nym, ylast, yedge, zstep):
        self.nxp, self.nxm, self.nyp, self.nym, self.zstep = nxp, nxm, nyp, nym, zstep
        z = iota(coeff[0].shape, 1) % 32
        zlast = z >= 32 - zstep
        zedge = (z < zstep) | zlast
        self.wp = [k + n for k, n in zip(coeff, nxp(coeff))]
        self.wm = [k + n for k, n in zip(coeff, nxm(coeff))]
        self.wy = [jnp.where(ylast, 0.0, k + nyp(k)) for k in coeff]
        self.wz = [jnp.where(zlast, 0.0, k + lanes(k, zstep)) for k in coeff]
        self.diag = []
        for k, wp, wm, wy, wz in zip(coeff, self.wp, self.wm, self.wy, self.wz):
            diag = wp + wm + (wy + nym(wy)) + (wz + lanes(wz, -zstep))
            self.diag.append(diag + (jnp.where(yedge, k, 0.0) + jnp.where(zedge, k, 0.0)))
        self.inv = [RELAX / d for d in self.diag]

    def around(self, v):
        out = []
        for c, p, m, wp, wm, wy, wz in zip(
            v, self.nxp(v), self.nxm(v), self.wp, self.wm, self.wy, self.wz
        ):
            total = wp * p + wm * m
            total = total + (wy * self.nyp(c) + self.nym(wy * c))
            out.append(total + (wz * lanes(c, self.zstep) + lanes(wz * c, -self.zstep)))
        return out

    def first(self, source):
        return [i * f for i, f in zip(self.inv, source)]

    def sweep(self, v, source):
        around = self.around(v)
        return [KEEP * c + i * (f + t) for c, i, f, t in zip(v, self.inv, source, around)]

    def sweeps(self, v, source, count):
        step = lambda _, v: tuple(self.sweep(list(v), source))
        return list(lax.fori_loop(0, count, step, tuple(v), unroll=True))

    def residual(self, v, source):
        around = self.around(v)
        return [f - d * c + t for c, d, f, t in zip(v, self.diag, source, around)]


def above(c):
    return jnp.concatenate([c[8:], rows(c[:8], 1)], axis=0)


def below(c):
    return jnp.concatenate([rows(c[8:], -1), c[:8]], axis=0)


UNROLL = 15
PAD = 3


def up_kernel(
    mine, other, v0, f0, f1, wx0, wy0, wz0, inv0, wx1, wy1, wz1, inv1, vmid, vnear, vfar, out,
    k2, f2, va, vb, wxi, wxe, wyi, wye, wz2, diag2, inv2, sumk, sumr, e3,
):
    gx, gy = lax.axis_index("gx"), lax.axis_index("gy")
    first = core_mask(8)
    lane = iota((16, 128), 1)
    row = iota((16, 128), 0)
    group, z = lane // 32, lane % 32
    xl, yl = group // 2, group % 2
    zero = jnp.zeros((16, 128), jnp.float32)

    for ref in (k2, f2, va, vb, wxi, wxe, wyi, wye, wz2, inv2):
        for i in range(PAD):
            ref[i] = zero
            ref[32 + PAD + i] = zero
    for i in range(32):
        for c, ref in ((0, f2), (1, k2)):
            here = pl.ds(2 * i + c, 8, stride=64)
            a, b = mine[here, :], other[here, :]
            ref[i + PAD, :8] = jnp.where(first, a, b)
            ref[i + PAD, 8:] = jnp.where(first, b, a)

    def sides(c):
        up, down = lanes(c, 32), lanes(c, -32)
        inner = jnp.where(yl == 0, up, down)
        outer = jnp.where(yl == 1, above(down), below(up))
        return inner, outer

    yout = ((yl == 1) & (row == 15)) | ((yl == 0) & (row == 0))
    zlast = z == 31
    zedge = zlast | (z == 0)

    def advance(i, field, turned, body):
        before, here = turned
        after = lanes(field[i + 1], 64)
        body(i, field[i], here, jnp.where(xl == 1, after, before))
        return here, after

    def summed(k):
        k = k + lanes(k, 64)
        return k + lanes(k, 32)

    def prepare(i, k, inner, outer):
        a, b = k + inner, k + outer
        yi, yo = sides(k)
        c = k + yi
        e = jnp.where(yout, 0.0, k + yo)
        w = jnp.where(zlast, 0.0, k + lanes(k, 1))
        diag = (a + b) + (c + e) + (w + lanes(w, -1))
        diag = diag + (jnp.where(yout, k, 0.0) + jnp.where(zedge, k, 0.0))
        inv = RELAX / diag
        wxi[i], wxe[i], wyi[i], wye[i], wz2[i], diag2[i], inv2[i] = a, b, c, e, w, diag, inv
        va[i] = inv * f2[i]
        sumk[i] = summed(k)

    def around2(i, c, inner, outer):
        yi, yo = sides(c)
        w = wz2[i]
        total = wxi[i] * inner + wxe[i] * outer
        total = total + (wyi[i] * yi + wye[i] * yo)
        return total + (w * lanes(c, 1) + lanes(w * c, -1))

    def sweep2(i, c, inner, outer):
        return KEEP * c + inv2[i] * (f2[i] + around2(i, c, inner, outer))

    def first2(i, c, inner, outer):
        vb[i] = sweep2(i, c, inner, outer)

    def residual2(i, c, inner, outer):
        sumr[i] = summed(f2[i] - diag2[i] * c + around2(i, c, inner, outer))

    def three(i, state):
        ofk, ofa, ofb = state
        ofk = advance(i, k2, ofk, prepare)
        ofa = advance(i - 1, va, ofa, first2)
        return ofk, ofa, advance(i - 2, vb, ofb, residual2)

    ofk = (zero, lanes(k2[PAD], 64))
    ofk = advance(PAD, k2, ofk, prepare)
    ofk = advance(PAD + 1, k2, ofk, prepare)
    ofa = advance(PAD, va, (zero, lanes(va[PAD], 64)), first2)
    ofb = (zero, lanes(vb[PAD], 64))

    def steps(step, state):
        for u in range(UNROLL):
            state = three(PAD + 2 + UNROLL * step + u, state)
        return state

    _, ofa, ofb = lax.fori_loop(0, 30 // UNROLL, steps, (ofk, ofa, ofb))
    advance(PAD + 31, va, ofa, first2)
    ofb = advance(PAD + 30, vb, ofb, residual2)
    advance(PAD + 31, vb, ofb, residual2)

    def four(sums, q):
        t = jnp.where(group == 0, sums[4 * q + PAD], sums[4 * q + PAD + 1])
        t = jnp.where(group == 2, sums[4 * q + PAD + 2], t)
        t = jnp.where(group == 3, sums[4 * q + PAD + 3], t)
        return t + lanes(t, 1)

    c3 = [0.125 * four(sumk, q) for q in range(8)]
    f3 = [0.5 * four(sumr, q) for q in range(8)]

    def plus3(v):
        up = [lanes(c, 32) for c in v] + [zero]
        return [jnp.where(group < 3, up[q], up[q + 1]) for q in range(8)]

    def minus3(v):
        down = [zero] + [lanes(c, -32) for c in v]
        return [jnp.where(group > 0, down[q + 1], down[q]) for q in range(8)]

    level3 = Coarse(c3, plus3, minus3, above, below, row == 15, (row == 0) | (row == 15), 2)
    v3 = level3.sweep(level3.first(f3), f3)
    r3 = level3.residual(v3, f3)

    def restrict(values, x, y, zz):
        s = [t + lanes(t, x) for t in values]
        s = [y(t) for t in s]
        return [t + lanes(t, zz) for t in s]

    cores = lambda t: t[:8] + t[8:]
    f4 = [0.5 * s for s in restrict(r3, 32, cores, 2)]
    c4 = [0.125 * s for s in restrict(c3, 32, cores, 2)]
    zero8 = zero[:8]
    row8, lane8, group8 = row[:8], lane[:8], group[:8]

    def plus4(v):
        turn = [lanes(c, 64) for c in v] + [zero8]
        return [jnp.where(group8 < 2, turn[q], turn[q + 1]) for q in range(8)]

    def minus4(v):
        turn = [zero8] + [lanes(c, 64) for c in v]
        return [jnp.where(group8 < 2, turn[q], turn[q + 1]) for q in range(8)]

    def next_rows(n):
        return lambda c: rows(c, n)

    level4 = Coarse(
        c4, plus4, minus4, next_rows(1), next_rows(-1), row8 == 7, (row8 == 0) | (row8 == 7), 4
    )
    v4 = level4.sweep(level4.first(f4), f4)
    r4 = level4.residual(v4, f4)

    pair = lambda t: t + rows(t, 1)
    f5 = [0.5 * s for s in restrict(r4, 64, pair, 4)]
    c5 = [0.125 * s for s in restrict(c4, 64, pair, 4)]
    level5 = Coarse(
        c5,
        lambda v: v[1:] + [zero8],
        lambda v: [zero8] + v[:-1],
        next_rows(2),
        next_rows(-2),
        row8 >= 6,
        (row8 < 2) | (row8 >= 6),
        8,
    )
    v5 = level5.sweeps(level5.first(f5), f5, COARSE_SWEEPS - 1)

    def spread(c, bit):
        return jnp.where((iota(c.shape, 1) & bit) != 0, lanes(c, -bit), c)

    v5 = [jnp.where((row8 & 1) != 0, rows(c, -1), c) for c in v5]
    v4 = [c + spread(e, 4) for c, e in zip(v4, v5)]
    v4 = level4.sweeps(v4, f4, 2)

    v4 = [spread(jnp.where(group8 % 2 == 1, lanes(c, -32), c), 2) for c in v4]
    v3 = [c + jnp.concatenate([e, e], axis=0) for c, e in zip(v3, v4)]
    v3 = level3.sweeps(v3, f3, 2)

    for q in range(8):
        e3[q] = spread(v3[q], 1)
    for t in range(5):
        p = gx + t - 2
        inside = (p >= 0) & (p < 32)
        p = jnp.clip(p, 0, 31)
        e = jnp.where(group == jnp.where(inside, p % 4, -1), e3[p // 4], 0.0)
        va[gx + t - 2 + PAD] = vb[gx + t - 2 + PAD] + summed(e)

    def some(read, write, first, end):
        turned = [lanes(read[gx + t + PAD], 64) for t in range(first - 1, end + 1)]
        for u, t in enumerate(range(first, end)):
            i = gx + t + PAD
            outer = jnp.where(xl == 1, turned[u + 2], turned[u])
            write[i] = sweep2(i, read[i], turned[u + 1], outer)

    some(va, vb, -2, 3)
    some(vb, va, -1, 2)

    lane8 = iota((8, 128), 1)
    pick = 32 * (iota((8, 128), 0) // 4) + lane8 // 4
    wide = {}
    for t in range(-1, 2):
        for x in range(2):
            parts = []
            for b in range(-1, 2):
                y = gy + b
                inside = (y >= 0) & (y < 16)
                y = jnp.clip(y, 0, 15)
                line = va[gx + t + PAD, pl.ds(8 * (y % 2) + y // 2, 1), :]
                line = jnp.broadcast_to(jnp.where(inside, line, 0.0), (8, 128))
                parts.append(jnp.take_along_axis(line, 64 * x + pick, axis=1))
            wide[t, x] = jnp.concatenate(parts, axis=0)

    def correction(i):
        return wide[i // 4, (i % 4) // 2]

    middle = Window(2, (-2, 6))
    middle.given(wx1, wy1, wz1, inv1)
    source = Stored(f1, -2)
    upper_half = iota((8, 128), 0) >= 4
    second = (iota((ROWS, 128), 0) & 2) != 0

    def received(i):
        n = 2 * i + 8
        c = [jnp.where(upper_half, r[n + 1 : n + 2], r[n : n + 1]) for r in (vmid, vnear, vfar)]
        c = joined(first, *c)
        return jnp.where(second, lanes(c, 1), c)

    v = {i: received(i) + correction(i) for i in range(-3, 7)}
    v = middle.sweep(v, source, -2, 6)
    v = middle.sweep(v, source, -1, 5)

    odd_lane = iota((ROWS, 128), 1) % 2 == 1
    odd_row = iota((ROWS, 128), 0) % 2 == 1
    fine = Window(1, (-1, 9))
    fine.given(wx0, wy0, wz0, inv0)
    source = Stored(f0, -1)
    base = Stored(v0, -2)
    spread1 = {}
    for i in range(-1, 5):
        c = jnp.where(odd_lane, lanes(v[i], -1), v[i])
        spread1[i] = jnp.where(odd_row, rows(c, -1), c)
    v = {i: base[i] + spread1[i // 2] for i in range(-2, 10)}
    v = fine.sweep(v, source, -1, 9)
    v = fine.sweep(v, source, 0, 8)
    for i in range(8):
        out[i] = v[i][8:16]


WINDOW_PLANES = (12, 10, 8, 11, 10, 10, 10, 9, 8, 8, 8)


def f32(*shape):
    return jax.ShapeDtypeStruct(shape, jnp.float32)


def swap(x, axis, first):
    pairs = [(i, i + 1) for i in range(first, lax.axis_size(axis) - 1, 2)]
    return lax.ppermute(x, axis, pairs + [(b, a) for a, b in pairs])


def to_all(x, axis, count, groups=None):
    copies = jnp.broadcast_to(x[None], (count,) + x.shape)
    return lax.all_to_all(copies, axis, 0, 0, axis_index_groups=groups)


def shards(right_side, coefficient, previous):
    even = lax.axis_index("gx") % 2 == 0
    own = lax.optimization_barrier(jnp.concatenate([right_side, coefficient, previous])).reshape(3, 8, 8, 128)
    start, end = own[:, :HALO], own[:, -HALO:]
    near = swap(jnp.where(even, end, start), "gx", 0)
    far = swap(jnp.where(even, start, end), "gx", 1)

    params = pltpu.CompilerParams(vmem_limit_bytes=VMEM)
    array = pl.BlockSpec(memory_space=pltpu.VMEM)
    count = sum(len(tiles) for tiles in TILES)
    to_near, to_far = pl.pallas_call(
        pack_kernel,
        in_specs=[array] * 3,
        out_shape=(f32(count, 8, 128),) * 2,
        compiler_params=params,
        name="pack",
    )(own, near, far)
    from_far = swap(to_far, "gy", 1)
    from_near = swap(to_near, "gy", 0)

    packed, *window = pl.pallas_call(
        down_kernel,
        in_specs=[array] * 5,
        out_shape=(f32(10, 128),) + tuple(f32(n, ROWS, 128) for n in WINDOW_PLANES),
        compiler_params=params,
        name="down",
    )(own, near, far, from_far, from_near)

    blocks = to_all(packed.reshape(1, 1280), "gx", 32)
    same_core = [[2 * z + c for z in range(8)] for c in range(2)]
    mine = to_all(blocks[:, :, :256].reshape(64, 128), "gy", 8, same_core).reshape(512, 128)
    v1 = jnp.pad(blocks[:, 0, 256:], ((1, 1), (0, 0)))
    place = (lax.axis_index("gx"), jnp.int32(0))
    vmid = lax.dynamic_slice(v1, place, (3, 1024)).reshape(24, 128)
    vnear, vfar = swap(vmid, "gy", 0), swap(vmid, "gy", 1)
    mine, vnear, vfar = lax.optimization_barrier((mine, vnear, vfar))
    other = swap(mine, "gy", 0)

    plane = pltpu.VMEM((32 + 2 * PAD, 16, 128), jnp.float32)
    return pl.pallas_call(
        up_kernel,
        in_specs=[array] * (5 + len(WINDOW_PLANES)),
        out_shape=f32(8, 8, 128),
        scratch_shapes=[plane] * 13 + [pltpu.VMEM((8, 16, 128), jnp.float32)],
        compiler_params=params,
        name="up",
    )(mine, other, *window, vmid, vnear, vfar)


def solution(mesh):
    spec = P("gx", "gy", None)
    return jax.shard_map(
        shards, mesh=mesh, in_specs=(spec,) * 3, out_specs=spec, check_vma=False
    )
```

```python
import jax
import jax.numpy as jnp
from jax import lax
from jax.experimental import pallas as pl
from jax.experimental.pallas import tpu as pltpu
from jax.sharding import PartitionSpec as P

RELAX = 0.8
KEEP = 1.0 - RELAX
HALO = 7
ROWS = 24
COARSE_SWEEPS = 8
VMEM = 48 * 1024 * 1024


def lanes(x, n):
    return pltpu.roll(x, (-n) % x.shape[1], axis=1)


def rows(x, n):
    return pltpu.roll(x, (-n) % x.shape[0], axis=0)


def iota(shape, dim):
    return lax.broadcasted_iota(jnp.int32, shape, dim)


class Window:
    def __init__(self, step, planes):
        self.step = step
        self.planes = planes

    def given(self, wx, wy, wz, inv):
        first = self.planes[0]
        self.wx, self.wy = Stored(wx, first - 1), Stored(wy, first)
        self.wz, self.inv = Stored(wz, first), Stored(inv, first)

    def hand_on(self, planes, wx, wy, wz, inv):
        first, end = planes
        for i in range(first - 1, end):
            wx[i - first + 1] = self.wx[i]
        for i in range(first, end):
            wy[i - first], wz[i - first], inv[i - first] = self.wy[i], self.wz[i], self.inv[i]

    def weights(self, coeff):
        first, end = self.planes
        lane = iota((ROWS, 128), 1)
        last = lane >= 128 - self.step
        edge = (lane < self.step) | last
        self.wx, self.wy, self.wz, self.diag, self.inv = {}, {}, {}, {}, {}
        for i in range(first - 1, end):
            self.wx[i] = coeff[i] + coeff[i + 1]
        for i in range(first, end):
            k = coeff[i]
            wy = k + rows(k, self.step)
            wz = jnp.where(last, 0.0, k + lanes(k, self.step))
            diag = self.wx[i] + self.wx[i - 1] + (wy + rows(wy, -self.step))
            diag = diag + (wz + lanes(wz, -self.step)) + jnp.where(edge, k, 0.0)
            self.wy[i], self.wz[i], self.diag[i] = wy, wz, diag
            self.inv[i] = jnp.where(k > 0.0, RELAX / diag, 0.0)

    def around(self, v, i):
        c = v[i]
        wy, wz, step = self.wy[i], self.wz[i], self.step
        total = self.wx[i] * v[i + 1] + self.wx[i - 1] * v[i - 1]
        total = total + (wy * rows(c, step) + rows(wy * c, -step))
        return total + (wz * lanes(c, step) + lanes(wz * c, -step))

    def sweep(self, v, source, first, end):
        return {
            i: KEEP * v[i] + self.inv[i] * (source[i] + self.around(v, i)) for i in range(first, end)
        }

    def sweep_into(self, out, v, source, first, end):
        def body(i):
            out[i] = KEEP * v[i] + self.inv[i] * (source[i] + self.around(v, i))

        over(first, end, body)

    def residual(self, v, source, first, end):
        return {i: source[i] - self.diag[i] * v[i] + self.around(v, i) for i in range(first, end)}


def over(first, end, body, step=2):
    def some(s, _):
        for u in range(step):
            body(first + step * s + u)

    lax.fori_loop(0, (end - first) // step, some, None)


class Stored:
    def __init__(self, ref, first):
        self.ref, self.first = ref, first

    def __getitem__(self, i):
        return self.ref[i - self.first]

    def __setitem__(self, i, value):
        self.ref[i - self.first] = value


def block_sum(low, high, step):
    s = low + high
    s = s + rows(s, step)
    return s + lanes(s, step)


def alone(*planes):
    return [(i, 8, None) for i in planes]


INNER = range(8)
NARROW = [(0, 6, -6), (7, 6, 13)] + alone(1, 2, 3, 4, 5, 6, -1, -2, 8, 9)
NARROW += [(-3, 5, -5), (10, 5, 12), (-4, 4, 11)]
WIDE = alone(*INNER, -1, -2, 8, 9)
WIDE += [(-3, 6, -7), (10, 6, 14), (-4, 5, -6), (11, 5, 13), (-5, 4, 12)]
TILES = (NARROW, WIDE, WIDE)


def planes_of(which, own, near, far):
    even = jnp.broadcast_to(lax.rem(lax.axis_index("gx"), 2), (8, 128)) == 0
    planes = {i: own[which, i] for i in INNER}
    for i in range(HALO):
        a, b = near[which, i], far[which, i]
        planes[i - HALO], planes[i + 8] = jnp.where(even, b, a), jnp.where(even, a, b)
    return planes


def pack_kernel(own, near, far, to_near, to_far):
    first = core_mask(8)
    row = iota((8, 128), 0)
    at = 0
    for which, tiles in enumerate(TILES):
        planes = planes_of(which, own, near, far)
        for a, n, b in tiles:
            upward = downward = planes[a]
            if b is not None:
                upward = jnp.where(row >= 8 - n, planes[a], rows(planes[b], n))
                downward = jnp.where(row < n, planes[a], rows(planes[b], -n))
            to_near[at] = jnp.where(first, upward, downward)
            to_far[at] = jnp.where(first, downward, upward)
            at += 1


def core_mask(rows_of):
    core = lax.rem(lax.axis_index("gy"), 2)
    return jnp.broadcast_to(core, (rows_of, 128)) == 0


def joined(first, mid, near, far):
    return jnp.concatenate([jnp.where(first, far, near), mid, jnp.where(first, near, far)], axis=0)


def down_kernel(
    own, xnear, xfar, far, near, packed, v0_out, f0_out, f1_out, wx0, wy0, wz0, inv0, wx1, wy1, wz1, inv1
):
    first = core_mask(8)

    fields, at = [], 0
    for which, tiles in enumerate(TILES):
        mid = planes_of(which, own, xnear, xfar)
        low, high = {}, {}
        for i, n, other in tiles:
            below_it, above_it = jnp.where(first, far[at], near[at]), jnp.where(first, near[at], far[at])
            low[i], high[i] = below_it, above_it
            if other is not None:
                low[other], high[other] = rows(below_it, -n), rows(above_it, n)
            at += 1
        fields.append({i: jnp.concatenate([low[i], mid[i], high[i]], axis=0) for i in low})
    source, coeff, v = fields
    source = {i: 2.0 * source[i] for i in range(-6, 14)}

    fine = Window(1, (-6, 14))
    fine.weights(coeff)
    v = fine.sweep(v, source, -6, 14)
    v = fine.sweep(v, source, -5, 13)
    for i in range(-2, 10):
        v0_out[i + 2] = v[i]
    for i in range(-1, 9):
        f0_out[i + 1] = source[i]
    fine.hand_on((-1, 9), wx0, wy0, wz0, inv0)
    r = fine.residual(v, source, -4, 12)

    source = {i: 0.5 * block_sum(r[2 * i], r[2 * i + 1], 1) for i in range(-2, 6)}
    coeff = {i: 0.125 * block_sum(coeff[2 * i], coeff[2 * i + 1], 1) for i in range(-3, 7)}
    for i in range(-2, 6):
        f1_out[i + 2] = source[i]
    middle = Window(2, (-2, 6))
    middle.weights(coeff)
    middle.hand_on((-2, 6), wx1, wy1, wz1, inv1)
    v = {i: middle.inv[i] * source[i] for i in range(-2, 6)}
    v = middle.sweep(v, source, -1, 5)
    even = iota((8, 128), 1) % 2 == 0
    for i in range(4):
        c = v[i][8:16]
        c = jnp.where(even, c, lanes(rows(c, 2), -1))
        packed[2 * i + 2 : 2 * i + 3, :] = c[0:1]
        packed[2 * i + 3 : 2 * i + 4, :] = c[4:5]
    r = middle.residual(v, source, 0, 4)

    source = [0.5 * block_sum(r[2 * i], r[2 * i + 1], 2)[8:16] for i in range(2)]
    coeff = [0.125 * block_sum(coeff[2 * i], coeff[2 * i + 1], 2)[8:16] for i in range(2)]
    lane, row = iota((8, 128), 1), iota((8, 128), 0)
    group = lane // 32
    pick = 4 * (lane % 32)
    for c, planes in enumerate((source, coeff)):
        dense = [jnp.take_along_axis(t, pick, axis=1) for t in planes]
        dense = jnp.where(group < 2, dense[0], dense[1])
        dense = jnp.where(row == 4 * (group % 2), dense, 0.0)
        packed[c : c + 1, :] = jnp.sum(dense, axis=0, keepdims=True)


class Coarse:
    def __init__(self, coeff, nxp, nxm, nyp, nym, ylast, yedge, zstep):
        self.nxp, self.nxm, self.nyp, self.nym, self.zstep = nxp, nxm, nyp, nym, zstep
        z = iota(coeff[0].shape, 1) % 32
        zlast = z >= 32 - zstep
        zedge = (z < zstep) | zlast
        self.wp = [k + n for k, n in zip(coeff, nxp(coeff))]
        self.wm = [k + n for k, n in zip(coeff, nxm(coeff))]
        self.wy = [jnp.where(ylast, 0.0, k + nyp(k)) for k in coeff]
        self.wz = [jnp.where(zlast, 0.0, k + lanes(k, zstep)) for k in coeff]
        self.diag = []
        for k, wp, wm, wy, wz in zip(coeff, self.wp, self.wm, self.wy, self.wz):
            diag = wp + wm + (wy + nym(wy)) + (wz + lanes(wz, -zstep))
            self.diag.append(diag + (jnp.where(yedge, k, 0.0) + jnp.where(zedge, k, 0.0)))
        self.inv = [RELAX / d for d in self.diag]

    def around(self, v):
        out = []
        for c, p, m, wp, wm, wy, wz in zip(
            v, self.nxp(v), self.nxm(v), self.wp, self.wm, self.wy, self.wz
        ):
            total = wp * p + wm * m
            total = total + (wy * self.nyp(c) + self.nym(wy * c))
            out.append(total + (wz * lanes(c, self.zstep) + lanes(wz * c, -self.zstep)))
        return out

    def first(self, source):
        return [i * f for i, f in zip(self.inv, source)]

    def sweep(self, v, source):
        around = self.around(v)
        return [KEEP * c + i * (f + t) for c, i, f, t in zip(v, self.inv, source, around)]

    def sweeps(self, v, source, count):
        step = lambda _, v: tuple(self.sweep(list(v), source))
        return list(lax.fori_loop(0, count, step, tuple(v)))

    def residual(self, v, source):
        around = self.around(v)
        return [f - d * c + t for c, d, f, t in zip(v, self.diag, source, around)]


def above(c):
    return jnp.concatenate([c[8:], rows(c[:8], 1)], axis=0)


def below(c):
    return jnp.concatenate([rows(c[8:], -1), c[:8]], axis=0)


UNROLL = 5
PAD = 3


def up_kernel(
    mine, other, v0, f0, f1, wx0, wy0, wz0, inv0, wx1, wy1, wz1, inv1, vmid, vnear, vfar, out,
    k2, f2, va, vb, wxi, wxe, wyi, wye, wz2, diag2, inv2, sumk, sumr, e3, v1a, v1b, v0a, v0b,
):
    gx, gy = lax.axis_index("gx"), lax.axis_index("gy")
    first = core_mask(8)
    lane = iota((16, 128), 1)
    row = iota((16, 128), 0)
    group, z = lane // 32, lane % 32
    xl, yl = group // 2, group % 2
    zero = jnp.zeros((16, 128), jnp.float32)

    for ref in (k2, f2, va, vb, wxi, wxe, wyi, wye, wz2, inv2):
        for i in range(PAD):
            ref[i] = zero
            ref[32 + PAD + i] = zero
    def unpack(i):
        for c, ref in ((0, f2), (1, k2)):
            here = pl.ds(2 * i + c, 8, stride=64)
            a, b = mine[here, :], other[here, :]
            ref[i + PAD, :8] = jnp.where(first, a, b)
            ref[i + PAD, 8:] = jnp.where(first, b, a)

    over(0, 32, unpack, 8)

    def sides(c):
        up, down = lanes(c, 32), lanes(c, -32)
        inner = jnp.where(yl == 0, up, down)
        outer = jnp.where(yl == 1, above(down), below(up))
        return inner, outer

    yout = ((yl == 1) & (row == 15)) | ((yl == 0) & (row == 0))
    zlast = z == 31
    zedge = zlast | (z == 0)

    def advance(i, field, turned, body):
        before, here = turned
        after = lanes(field[i + 1], 64)
        body(i, field[i], here, jnp.where(xl == 1, after, before))
        return here, after

    def summed(k):
        k = k + lanes(k, 64)
        return k + lanes(k, 32)

    def prepare(i, k, inner, outer):
        a, b = k + inner, k + outer
        yi, yo = sides(k)
        c = k + yi
        e = jnp.where(yout, 0.0, k + yo)
        w = jnp.where(zlast, 0.0, k + lanes(k, 1))
        diag = (a + b) + (c + e) + (w + lanes(w, -1))
        diag = diag + (jnp.where(yout, k, 0.0) + jnp.where(zedge, k, 0.0))
        inv = RELAX / diag
        wxi[i], wxe[i], wyi[i], wye[i], wz2[i], diag2[i], inv2[i] = a, b, c, e, w, diag, inv
        va[i] = inv * f2[i]
        sumk[i] = summed(k)

    def around2(i, c, inner, outer):
        yi, yo = sides(c)
        w = wz2[i]
        total = wxi[i] * inner + wxe[i] * outer
        total = total + (wyi[i] * yi + wye[i] * yo)
        return total + (w * lanes(c, 1) + lanes(w * c, -1))

    def sweep2(i, c, inner, outer):
        return KEEP * c + inv2[i] * (f2[i] + around2(i, c, inner, outer))

    def first2(i, c, inner, outer):
        vb[i] = sweep2(i, c, inner, outer)

    def residual2(i, c, inner, outer):
        sumr[i] = summed(f2[i] - diag2[i] * c + around2(i, c, inner, outer))

    def three(i, state):
        ofk, ofa, ofb = state
        ofk = advance(i, k2, ofk, prepare)
        ofa = advance(i - 1, va, ofa, first2)
        return ofk, ofa, advance(i - 2, vb, ofb, residual2)

    ofk = (zero, lanes(k2[PAD], 64))
    ofk = advance(PAD, k2, ofk, prepare)
    ofk = advance(PAD + 1, k2, ofk, prepare)
    ofa = advance(PAD, va, (zero, lanes(va[PAD], 64)), first2)
    ofb = (zero, lanes(vb[PAD], 64))

    def steps(step, state):
        for u in range(UNROLL):
            state = three(PAD + 2 + UNROLL * step + u, state)
        return state

    _, ofa, ofb = lax.fori_loop(0, 30 // UNROLL, steps, (ofk, ofa, ofb))
    advance(PAD + 31, va, ofa, first2)
    ofb = advance(PAD + 30, vb, ofb, residual2)
    advance(PAD + 31, vb, ofb, residual2)

    def four(sums, q):
        t = jnp.where(group == 0, sums[4 * q + PAD], sums[4 * q + PAD + 1])
        t = jnp.where(group == 2, sums[4 * q + PAD + 2], t)
        t = jnp.where(group == 3, sums[4 * q + PAD + 3], t)
        return t + lanes(t, 1)

    c3 = [0.125 * four(sumk, q) for q in range(8)]
    f3 = [0.5 * four(sumr, q) for q in range(8)]

    def plus3(v):
        up = [lanes(c, 32) for c in v] + [zero]
        return [jnp.where(group < 3, up[q], up[q + 1]) for q in range(8)]

    def minus3(v):
        down = [zero] + [lanes(c, -32) for c in v]
        return [jnp.where(group > 0, down[q + 1], down[q]) for q in range(8)]

    level3 = Coarse(c3, plus3, minus3, above, below, row == 15, (row == 0) | (row == 15), 2)
    v3 = level3.sweep(level3.first(f3), f3)
    r3 = level3.residual(v3, f3)

    def restrict(values, x, y, zz):
        s = [t + lanes(t, x) for t in values]
        s = [y(t) for t in s]
        return [t + lanes(t, zz) for t in s]

    cores = lambda t: t[:8] + t[8:]
    f4 = [0.5 * s for s in restrict(r3, 32, cores, 2)]
    c4 = [0.125 * s for s in restrict(c3, 32, cores, 2)]
    zero8 = zero[:8]
    row8, lane8, group8 = row[:8], lane[:8], group[:8]

    def plus4(v):
        turn = [lanes(c, 64) for c in v] + [zero8]
        return [jnp.where(group8 < 2, turn[q], turn[q + 1]) for q in range(8)]

    def minus4(v):
        turn = [zero8] + [lanes(c, 64) for c in v]
        return [jnp.where(group8 < 2, turn[q], turn[q + 1]) for q in range(8)]

    def next_rows(n):
        return lambda c: rows(c, n)

    level4 = Coarse(
        c4, plus4, minus4, next_rows(1), next_rows(-1), row8 == 7, (row8 == 0) | (row8 == 7), 4
    )
    v4 = level4.sweep(level4.first(f4), f4)
    r4 = level4.residual(v4, f4)

    pair = lambda t: t + rows(t, 1)
    f5 = [0.5 * s for s in restrict(r4, 64, pair, 4)]
    c5 = [0.125 * s for s in restrict(c4, 64, pair, 4)]
    level5 = Coarse(
        c5,
        lambda v: v[1:] + [zero8],
        lambda v: [zero8] + v[:-1],
        next_rows(2),
        next_rows(-2),
        row8 >= 6,
        (row8 < 2) | (row8 >= 6),
        8,
    )
    v5 = level5.sweeps(level5.first(f5), f5, COARSE_SWEEPS - 1)

    def spread(c, bit):
        return jnp.where((iota(c.shape, 1) & bit) != 0, lanes(c, -bit), c)

    v5 = [jnp.where((row8 & 1) != 0, rows(c, -1), c) for c in v5]
    v4 = [c + spread(e, 4) for c, e in zip(v4, v5)]
    v4 = level4.sweeps(v4, f4, 2)

    v4 = [spread(jnp.where(group8 % 2 == 1, lanes(c, -32), c), 2) for c in v4]
    v3 = [c + jnp.concatenate([e, e], axis=0) for c, e in zip(v3, v4)]
    v3 = level3.sweeps(v3, f3, 2)

    for q in range(8):
        e3[q] = spread(v3[q], 1)
    for t in range(5):
        p = gx + t - 2
        inside = (p >= 0) & (p < 32)
        p = jnp.clip(p, 0, 31)
        e = jnp.where(group == jnp.where(inside, p % 4, -1), e3[p // 4], 0.0)
        va[gx + t - 2 + PAD] = vb[gx + t - 2 + PAD] + summed(e)

    def some(read, write, first, end):
        turned = [lanes(read[gx + t + PAD], 64) for t in range(first - 1, end + 1)]
        for u, t in enumerate(range(first, end)):
            i = gx + t + PAD
            outer = jnp.where(xl == 1, turned[u + 2], turned[u])
            write[i] = sweep2(i, read[i], turned[u + 1], outer)

    some(va, vb, -2, 3)
    some(vb, va, -1, 2)

    lane8 = iota((8, 128), 1)
    pick = 32 * (iota((8, 128), 0) // 4) + lane8 // 4
    wide = {}
    for t in range(-1, 2):
        for x in range(2):
            parts = []
            for b in range(-1, 2):
                y = gy + b
                inside = (y >= 0) & (y < 16)
                y = jnp.clip(y, 0, 15)
                line = va[gx + t + PAD, pl.ds(8 * (y % 2) + y // 2, 1), :]
                line = jnp.broadcast_to(jnp.where(inside, line, 0.0), (8, 128))
                parts.append(jnp.take_along_axis(line, 64 * x + pick, axis=1))
            wide[t, x] = jnp.concatenate(parts, axis=0)

    def correction(i):
        return wide[i // 4, (i % 4) // 2]

    middle = Window(2, (-2, 6))
    middle.given(wx1, wy1, wz1, inv1)
    source = Stored(f1, -2)
    upper_half = iota((8, 128), 0) >= 4
    second = (iota((ROWS, 128), 0) & 2) != 0

    def received(i):
        n = 2 * i + 8
        c = [jnp.where(upper_half, r[n + 1 : n + 2], r[n : n + 1]) for r in (vmid, vnear, vfar)]
        c = joined(first, *c)
        return jnp.where(second, lanes(c, 1), c)

    v, w = Stored(v1a, -3), Stored(v1b, -2)
    for i in range(-3, 7):
        v[i] = received(i) + correction(i)
    middle.sweep_into(w, v, source, -2, 6)
    middle.sweep_into(v, w, source, -1, 5)

    odd_lane = iota((ROWS, 128), 1) % 2 == 1
    odd_row = iota((ROWS, 128), 0) % 2 == 1
    fine = Window(1, (-1, 9))
    fine.given(wx0, wy0, wz0, inv0)
    source, base, post, half = Stored(f0, -1), Stored(v0, -2), Stored(v0a, -2), Stored(v0b, -1)

    def prolong(i):
        c = jnp.where(odd_lane, lanes(v[i], -1), v[i])
        c = jnp.where(odd_row, rows(c, -1), c)
        post[2 * i] = base[2 * i] + c
        post[2 * i + 1] = base[2 * i + 1] + c

    over(-1, 5, prolong)
    fine.sweep_into(half, post, source, -1, 9)

    def last(i):
        c = KEEP * half[i] + fine.inv[i] * (source[i] + fine.around(half, i))
        out[i] = c[8:16]

    over(0, 8, last)


WINDOW_PLANES = (12, 10, 8, 11, 10, 10, 10, 9, 8, 8, 8)


def f32(*shape):
    return jax.ShapeDtypeStruct(shape, jnp.float32)


def swap(x, axis, first):
    pairs = [(i, i + 1) for i in range(first, lax.axis_size(axis) - 1, 2)]
    return lax.ppermute(x, axis, pairs + [(b, a) for a, b in pairs])


def to_all(x, axis, count, groups=None):
    copies = jnp.broadcast_to(x[None], (count,) + x.shape)
    return lax.all_to_all(copies, axis, 0, 0, axis_index_groups=groups)


def shards(right_side, coefficient, previous):
    even = lax.axis_index("gx") % 2 == 0
    own = lax.optimization_barrier(jnp.concatenate([right_side, coefficient, previous])).reshape(3, 8, 8, 128)
    start, end = own[:, :HALO], own[:, -HALO:]
    near = swap(jnp.where(even, end, start), "gx", 0)
    far = swap(jnp.where(even, start, end), "gx", 1)

    params = pltpu.CompilerParams(vmem_limit_bytes=VMEM)
    array = pl.BlockSpec(memory_space=pltpu.VMEM)
    count = sum(len(tiles) for tiles in TILES)
    to_near, to_far = pl.pallas_call(
        pack_kernel,
        in_specs=[array] * 3,
        out_shape=(f32(count, 8, 128),) * 2,
        compiler_params=params,
        name="pack",
    )(own, near, far)
    from_far = swap(to_far, "gy", 1)
    from_near = swap(to_near, "gy", 0)

    packed, *window = pl.pallas_call(
        down_kernel,
        in_specs=[array] * 5,
        out_shape=(f32(10, 128),) + tuple(f32(n, ROWS, 128) for n in WINDOW_PLANES),
        compiler_params=params,
        name="down",
    )(own, near, far, from_far, from_near)

    blocks = to_all(packed.reshape(1, 1280), "gx", 32)
    same_core = [[2 * z + c for z in range(8)] for c in range(2)]
    mine = to_all(blocks[:, :, :256].reshape(64, 128), "gy", 8, same_core).reshape(512, 128)
    v1 = jnp.pad(blocks[:, 0, 256:], ((1, 1), (0, 0)))
    place = (lax.axis_index("gx"), jnp.int32(0))
    vmid = lax.dynamic_slice(v1, place, (3, 1024)).reshape(24, 128)
    vnear, vfar = swap(vmid, "gy", 0), swap(vmid, "gy", 1)
    mine, vnear, vfar = lax.optimization_barrier((mine, vnear, vfar))
    other = swap(mine, "gy", 0)

    plane = pltpu.VMEM((32 + 2 * PAD, 16, 128), jnp.float32)
    return pl.pallas_call(
        up_kernel,
        in_specs=[array] * (5 + len(WINDOW_PLANES)),
        out_shape=f32(8, 8, 128),
        scratch_shapes=[plane] * 13
        + [pltpu.VMEM((8, 16, 128), jnp.float32)]
        + [pltpu.VMEM((n, ROWS, 128), jnp.float32) for n in (10, 8, 12, 10)],
        compiler_params=params,
        name="up",
    )(mine, other, *window, vmid, vnear, vfar)


def solution(mesh):
    spec = P("gx", "gy", None)
    return jax.shard_map(
        shards, mesh=mesh, in_specs=(spec,) * 3, out_specs=spec, check_vma=False
    )
```

```python
import jax
import jax.numpy as jnp
from jax import lax
from jax.experimental import pallas as pl
from jax.experimental.pallas import tpu as pltpu
from jax.sharding import PartitionSpec as P

RELAX = 0.8
KEEP = 1.0 - RELAX
HALO = 7
ROWS = 24
COARSE_SWEEPS = 8
VMEM = 48 * 1024 * 1024


def lanes(x, n):
    return pltpu.roll(x, (-n) % x.shape[1], axis=1)


def rows(x, n):
    return pltpu.roll(x, (-n) % x.shape[0], axis=0)


def iota(shape, dim):
    return lax.broadcasted_iota(jnp.int32, shape, dim)


class Window:
    def __init__(self, step, planes):
        self.step = step
        self.planes = planes

    def given(self, wx, wy, wz, inv):
        first = self.planes[0]
        self.wx, self.wy = Stored(wx, first - 1), Stored(wy, first)
        self.wz, self.inv = Stored(wz, first), Stored(inv, first)

    def hand_on(self, planes, wx, wy, wz, inv):
        first, end = planes
        for i in range(first - 1, end):
            wx[i - first + 1] = self.wx[i]
        for i in range(first, end):
            wy[i - first], wz[i - first], inv[i - first] = self.wy[i], self.wz[i], self.inv[i]

    def weights(self, coeff):
        first, end = self.planes
        lane = iota((ROWS, 128), 1)
        last = lane >= 128 - self.step
        edge = (lane < self.step) | last
        self.wx, self.wy, self.wz, self.diag, self.inv = {}, {}, {}, {}, {}
        for i in range(first - 1, end):
            self.wx[i] = coeff[i] + coeff[i + 1]
        for i in range(first, end):
            k = coeff[i]
            wy = k + rows(k, self.step)
            wz = jnp.where(last, 0.0, k + lanes(k, self.step))
            diag = self.wx[i] + self.wx[i - 1] + (wy + rows(wy, -self.step))
            diag = diag + (wz + lanes(wz, -self.step)) + jnp.where(edge, k, 0.0)
            self.wy[i], self.wz[i], self.diag[i] = wy, wz, diag
            self.inv[i] = jnp.where(k > 0.0, RELAX / diag, 0.0)

    def around(self, v, i):
        c = v[i]
        wy, wz, step = self.wy[i], self.wz[i], self.step
        total = self.wx[i] * v[i + 1] + self.wx[i - 1] * v[i - 1]
        total = total + (wy * rows(c, step) + rows(wy * c, -step))
        return total + (wz * lanes(c, step) + lanes(wz * c, -step))

    def sweep(self, v, source, first, end):
        return {
            i: KEEP * v[i] + self.inv[i] * (source[i] + self.around(v, i)) for i in range(first, end)
        }

    def residual(self, v, source, first, end):
        return {i: source[i] - self.diag[i] * v[i] + self.around(v, i) for i in range(first, end)}


class Stored:
    def __init__(self, ref, first):
        self.ref, self.first = ref, first

    def __getitem__(self, i):
        return self.ref[i - self.first]

    def __setitem__(self, i, value):
        self.ref[i - self.first] = value


def block_sum(low, high, step):
    s = low + high
    s = s + rows(s, step)
    return s + lanes(s, step)


def alone(*planes):
    return [(i, 8, None) for i in planes]


INNER = range(8)
NARROW = [(0, 6, -6), (7, 6, 13)] + alone(1, 2, 3, 4, 5, 6, -1, -2, 8, 9)
NARROW += [(-3, 5, -5), (10, 5, 12), (-4, 4, 11)]
WIDE = alone(*INNER, -1, -2, 8, 9)
WIDE += [(-3, 6, -7), (10, 6, 14), (-4, 5, -6), (11, 5, 13), (-5, 4, 12)]
TILES = (NARROW, WIDE, WIDE)


def planes_of(which, own, near, far):
    even = jnp.broadcast_to(lax.rem(lax.axis_index("gx"), 2), (8, 128)) == 0
    planes = {i: own[which, i] for i in INNER}
    for i in range(HALO):
        a, b = near[which, i], far[which, i]
        planes[i - HALO], planes[i + 8] = jnp.where(even, b, a), jnp.where(even, a, b)
    return planes


def pack_kernel(own, near, far, to_near, to_far):
    first = core_mask(8)
    row = iota((8, 128), 0)
    at = 0
    for which, tiles in enumerate(TILES):
        planes = planes_of(which, own, near, far)
        for a, n, b in tiles:
            upward = downward = planes[a]
            if b is not None:
                upward = jnp.where(row >= 8 - n, planes[a], rows(planes[b], n))
                downward = jnp.where(row < n, planes[a], rows(planes[b], -n))
            to_near[at] = jnp.where(first, upward, downward)
            to_far[at] = jnp.where(first, downward, upward)
            at += 1


def core_mask(rows_of):
    core = lax.rem(lax.axis_index("gy"), 2)
    return jnp.broadcast_to(core, (rows_of, 128)) == 0


def joined(first, mid, near, far):
    return jnp.concatenate([jnp.where(first, far, near), mid, jnp.where(first, near, far)], axis=0)


def down_kernel(
    own, xnear, xfar, far, near, lower, higher, v1_out, v0_out, f0_out, f1_out, wx0, wy0, wz0, inv0, wx1, wy1, wz1, inv1
):
    first = core_mask(8)

    fields, at = [], 0
    for which, tiles in enumerate(TILES):
        mid = planes_of(which, own, xnear, xfar)
        low, high = {}, {}
        for i, n, other in tiles:
            below_it, above_it = jnp.where(first, far[at], near[at]), jnp.where(first, near[at], far[at])
            low[i], high[i] = below_it, above_it
            if other is not None:
                low[other], high[other] = rows(below_it, -n), rows(above_it, n)
            at += 1
        fields.append({i: jnp.concatenate([low[i], mid[i], high[i]], axis=0) for i in low})
    source, coeff, v = fields
    source = {i: 2.0 * source[i] for i in range(-6, 14)}

    fine = Window(1, (-6, 14))
    fine.weights(coeff)
    v = fine.sweep(v, source, -6, 14)
    v = fine.sweep(v, source, -5, 13)
    for i in range(-2, 10):
        v0_out[i + 2] = v[i]
    for i in range(-1, 9):
        f0_out[i + 1] = source[i]
    fine.hand_on((-1, 9), wx0, wy0, wz0, inv0)
    r = fine.residual(v, source, -4, 12)

    source = {i: 0.5 * block_sum(r[2 * i], r[2 * i + 1], 1) for i in range(-2, 6)}
    coeff = {i: 0.125 * block_sum(coeff[2 * i], coeff[2 * i + 1], 1) for i in range(-3, 7)}
    for i in range(-2, 6):
        f1_out[i + 2] = source[i]
    middle = Window(2, (-2, 6))
    middle.weights(coeff)
    middle.hand_on((-2, 6), wx1, wy1, wz1, inv1)
    v = {i: middle.inv[i] * source[i] for i in range(-2, 6)}
    v = middle.sweep(v, source, -1, 5)
    even = iota((8, 128), 1) % 2 == 0
    for i in range(4):
        c = v[i][8:16]
        c = jnp.where(even, c, lanes(rows(c, 2), -1))
        for n, line in enumerate((c[0:1], c[4:5])):
            v1_out[2 * i + n : 2 * i + n + 1, :] = line
            if i < 3:
                lower[2 * i + n + 2 : 2 * i + n + 3, :] = line
            if i > 0:
                higher[2 * i + n : 2 * i + n + 1, :] = line
    r = middle.residual(v, source, 0, 4)

    source = [0.5 * block_sum(r[2 * i], r[2 * i + 1], 2)[8:16] for i in range(2)]
    coeff = [0.125 * block_sum(coeff[2 * i], coeff[2 * i + 1], 2)[8:16] for i in range(2)]
    lane, row = iota((8, 128), 1), iota((8, 128), 0)
    group = lane // 32
    pick = 4 * (lane % 32)
    for c, planes in enumerate((source, coeff)):
        dense = [jnp.take_along_axis(t, pick, axis=1) for t in planes]
        dense = jnp.where(group < 2, dense[0], dense[1])
        dense = jnp.where(row == 4 * (group % 2), dense, 0.0)
        dense = jnp.sum(dense, axis=0, keepdims=True)
        lower[c : c + 1, :] = dense
        higher[c : c + 1, :] = dense


class Coarse:
    def __init__(self, coeff, nxp, nxm, nyp, nym, ylast, yedge, zstep):
        self.nxp, self.nxm, self.nyp, self.nym, self.zstep = nxp, nxm, nyp, nym, zstep
        z = iota(coeff[0].shape, 1) % 32
        zlast = z >= 32 - zstep
        zedge = (z < zstep) | zlast
        self.wp = [k + n for k, n in zip(coeff, nxp(coeff))]
        self.wm = [k + n for k, n in zip(coeff, nxm(coeff))]
        self.wy = [jnp.where(ylast, 0.0, k + nyp(k)) for k in coeff]
        self.wz = [jnp.where(zlast, 0.0, k + lanes(k, zstep)) for k in coeff]
        self.diag = []
        for k, wp, wm, wy, wz in zip(coeff, self.wp, self.wm, self.wy, self.wz):
            diag = wp + wm + (wy + nym(wy)) + (wz + lanes(wz, -zstep))
            self.diag.append(diag + (jnp.where(yedge, k, 0.0) + jnp.where(zedge, k, 0.0)))
        self.inv = [RELAX / d for d in self.diag]

    def around(self, v):
        out = []
        for c, p, m, wp, wm, wy, wz in zip(
            v, self.nxp(v), self.nxm(v), self.wp, self.wm, self.wy, self.wz
        ):
            total = wp * p + wm * m
            total = total + (wy * self.nyp(c) + self.nym(wy * c))
            out.append(total + (wz * lanes(c, self.zstep) + lanes(wz * c, -self.zstep)))
        return out

    def first(self, source):
        return [i * f for i, f in zip(self.inv, source)]

    def sweep(self, v, source):
        around = self.around(v)
        return [KEEP * c + i * (f + t) for c, i, f, t in zip(v, self.inv, source, around)]

    def sweeps(self, v, source, count):
        step = lambda _, v: tuple(self.sweep(list(v), source))
        return list(lax.fori_loop(0, count, step, tuple(v), unroll=True))

    def residual(self, v, source):
        around = self.around(v)
        return [f - d * c + t for c, d, f, t in zip(v, self.diag, source, around)]


def above(c):
    return jnp.concatenate([c[8:], rows(c[:8], 1)], axis=0)


def below(c):
    return jnp.concatenate([rows(c[8:], -1), c[:8]], axis=0)


UNROLL = 10
PAD = 3


def up_kernel(
    mine, other, v0, f0, f1, wx0, wy0, wz0, inv0, wx1, wy1, wz1, inv1, vmid, vfar, vnear, out,
    k2, f2, va, vb, wxi, wxe, wyi, wye, wz2, diag2, inv2, sumk, sumr, e3,
):
    gx, gy = lax.axis_index("gx"), lax.axis_index("gy")
    first = core_mask(8)
    lane = iota((16, 128), 1)
    row = iota((16, 128), 0)
    group, z = lane // 32, lane % 32
    xl, yl = group // 2, group % 2
    zero = jnp.zeros((16, 128), jnp.float32)

    for ref in (k2, f2, va, vb, wxi, wxe, wyi, wye, wz2, inv2):
        for i in range(PAD):
            ref[i] = zero
            ref[32 + PAD + i] = zero
    for i in range(32):
        for c, ref in ((0, f2), (1, k2)):
            here = pl.ds(2 * i + c, 8, stride=64)
            a, b = mine[here, :], other[here, :]
            ref[i + PAD, :8] = jnp.where(first, a, b)
            ref[i + PAD, 8:] = jnp.where(first, b, a)

    def sides(c):
        up, down = lanes(c, 32), lanes(c, -32)
        inner = jnp.where(yl == 0, up, down)
        outer = jnp.where(yl == 1, above(down), below(up))
        return inner, outer

    yout = ((yl == 1) & (row == 15)) | ((yl == 0) & (row == 0))
    zlast = z == 31
    zedge = zlast | (z == 0)

    def advance(i, field, turned, body):
        before, here = turned
        after = lanes(field[i + 1], 64)
        body(i, field[i], here, jnp.where(xl == 1, after, before))
        return here, after

    def summed(k):
        k = k + lanes(k, 64)
        return k + lanes(k, 32)

    def prepare(i, k, inner, outer):
        a, b = k + inner, k + outer
        yi, yo = sides(k)
        c = k + yi
        e = jnp.where(yout, 0.0, k + yo)
        w = jnp.where(zlast, 0.0, k + lanes(k, 1))
        diag = (a + b) + (c + e) + (w + lanes(w, -1))
        diag = diag + (jnp.where(yout, k, 0.0) + jnp.where(zedge, k, 0.0))
        inv = RELAX / diag
        wxi[i], wxe[i], wyi[i], wye[i], wz2[i], diag2[i], inv2[i] = a, b, c, e, w, diag, inv
        va[i] = inv * f2[i]
        sumk[i] = summed(k)

    def around2(i, c, inner, outer):
        yi, yo = sides(c)
        w = wz2[i]
        total = wxi[i] * inner + wxe[i] * outer
        total = total + (wyi[i] * yi + wye[i] * yo)
        return total + (w * lanes(c, 1) + lanes(w * c, -1))

    def sweep2(i, c, inner, outer):
        return KEEP * c + inv2[i] * (f2[i] + around2(i, c, inner, outer))

    def first2(i, c, inner, outer):
        vb[i] = sweep2(i, c, inner, outer)

    def residual2(i, c, inner, outer):
        sumr[i] = summed(f2[i] - diag2[i] * c + around2(i, c, inner, outer))

    def three(i, state):
        ofk, ofa, ofb = state
        ofk = advance(i, k2, ofk, prepare)
        ofa = advance(i - 1, va, ofa, first2)
        return ofk, ofa, advance(i - 2, vb, ofb, residual2)

    ofk = (zero, lanes(k2[PAD], 64))
    ofk = advance(PAD, k2, ofk, prepare)
    ofk = advance(PAD + 1, k2, ofk, prepare)
    ofa = advance(PAD, va, (zero, lanes(va[PAD], 64)), first2)
    ofb = (zero, lanes(vb[PAD], 64))

    def steps(step, state):
        for u in range(UNROLL):
            state = three(PAD + 2 + UNROLL * step + u, state)
        return state

    _, ofa, ofb = lax.fori_loop(0, 30 // UNROLL, steps, (ofk, ofa, ofb))
    advance(PAD + 31, va, ofa, first2)
    ofb = advance(PAD + 30, vb, ofb, residual2)
    advance(PAD + 31, vb, ofb, residual2)

    def four(sums, q):
        t = jnp.where(group == 0, sums[4 * q + PAD], sums[4 * q + PAD + 1])
        t = jnp.where(group == 2, sums[4 * q + PAD + 2], t)
        t = jnp.where(group == 3, sums[4 * q + PAD + 3], t)
        return t + lanes(t, 1)

    c3 = [0.125 * four(sumk, q) for q in range(8)]
    f3 = [0.5 * four(sumr, q) for q in range(8)]

    def plus3(v):
        up = [lanes(c, 32) for c in v] + [zero]
        return [jnp.where(group < 3, up[q], up[q + 1]) for q in range(8)]

    def minus3(v):
        down = [zero] + [lanes(c, -32) for c in v]
        return [jnp.where(group > 0, down[q + 1], down[q]) for q in range(8)]

    level3 = Coarse(c3, plus3, minus3, above, below, row == 15, (row == 0) | (row == 15), 2)
    v3 = level3.sweep(level3.first(f3), f3)
    r3 = level3.residual(v3, f3)

    def restrict(values, x, y, zz):
        s = [t + lanes(t, x) for t in values]
        s = [y(t) for t in s]
        return [t + lanes(t, zz) for t in s]

    cores = lambda t: t[:8] + t[8:]
    f4 = [0.5 * s for s in restrict(r3, 32, cores, 2)]
    c4 = [0.125 * s for s in restrict(c3, 32, cores, 2)]
    zero8 = zero[:8]
    row8, lane8, group8 = row[:8], lane[:8], group[:8]

    def plus4(v):
        turn = [lanes(c, 64) for c in v] + [zero8]
        return [jnp.where(group8 < 2, turn[q], turn[q + 1]) for q in range(8)]

    def minus4(v):
        turn = [zero8] + [lanes(c, 64) for c in v]
        return [jnp.where(group8 < 2, turn[q], turn[q + 1]) for q in range(8)]

    def next_rows(n):
        return lambda c: rows(c, n)

    level4 = Coarse(
        c4, plus4, minus4, next_rows(1), next_rows(-1), row8 == 7, (row8 == 0) | (row8 == 7), 4
    )
    v4 = level4.sweep(level4.first(f4), f4)
    r4 = level4.residual(v4, f4)

    pair = lambda t: t + rows(t, 1)
    f5 = [0.5 * s for s in restrict(r4, 64, pair, 4)]
    c5 = [0.125 * s for s in restrict(c4, 64, pair, 4)]
    level5 = Coarse(
        c5,
        lambda v: v[1:] + [zero8],
        lambda v: [zero8] + v[:-1],
        next_rows(2),
        next_rows(-2),
        row8 >= 6,
        (row8 < 2) | (row8 >= 6),
        8,
    )
    v5 = level5.sweeps(level5.first(f5), f5, COARSE_SWEEPS - 1)

    def spread(c, bit):
        return jnp.where((iota(c.shape, 1) & bit) != 0, lanes(c, -bit), c)

    v5 = [jnp.where((row8 & 1) != 0, rows(c, -1), c) for c in v5]
    v4 = [c + spread(e, 4) for c, e in zip(v4, v5)]
    v4 = level4.sweeps(v4, f4, 2)

    v4 = [spread(jnp.where(group8 % 2 == 1, lanes(c, -32), c), 2) for c in v4]
    v3 = [c + jnp.concatenate([e, e], axis=0) for c, e in zip(v3, v4)]
    v3 = level3.sweeps(v3, f3, 2)

    for q in range(8):
        e3[q] = spread(v3[q], 1)
    for t in range(5):
        p = gx + t - 2
        inside = (p >= 0) & (p < 32)
        p = jnp.clip(p, 0, 31)
        e = jnp.where(group == jnp.where(inside, p % 4, -1), e3[p // 4], 0.0)
        va[gx + t - 2 + PAD] = vb[gx + t - 2 + PAD] + summed(e)

    def some(read, write, first, end):
        turned = [lanes(read[gx + t + PAD], 64) for t in range(first - 1, end + 1)]
        for u, t in enumerate(range(first, end)):
            i = gx + t + PAD
            outer = jnp.where(xl == 1, turned[u + 2], turned[u])
            write[i] = sweep2(i, read[i], turned[u + 1], outer)

    some(va, vb, -2, 3)
    some(vb, va, -1, 2)

    lane8 = iota((8, 128), 1)
    pick = 32 * (iota((8, 128), 0) // 4) + lane8 // 4
    wide = {}
    for t in range(-1, 2):
        for x in range(2):
            parts = []
            for b in range(-1, 2):
                y = gy + b
                inside = (y >= 0) & (y < 16)
                y = jnp.clip(y, 0, 15)
                line = va[gx + t + PAD, pl.ds(8 * (y % 2) + y // 2, 1), :]
                line = jnp.broadcast_to(jnp.where(inside, line, 0.0), (8, 128))
                parts.append(jnp.take_along_axis(line, 64 * x + pick, axis=1))
            wide[t, x] = jnp.concatenate(parts, axis=0)

    def correction(i):
        return wide[i // 4, (i % 4) // 2]

    middle = Window(2, (-2, 6))
    middle.given(wx1, wy1, wz1, inv1)
    source = Stored(f1, -2)
    upper_half = iota((8, 128), 0) >= 4
    second = (iota((ROWS, 128), 0) & 2) != 0

    def received(i):
        n = 2 * i + 6
        c = [jnp.where(upper_half, r[n + 1 : n + 2], r[n : n + 1]) for r in (vmid, vnear, vfar)]
        c = joined(first, *c)
        return jnp.where(second, lanes(c, 1), c)

    v = {i: received(i) + correction(i) for i in range(-3, 7)}
    v = middle.sweep(v, source, -2, 6)
    v = middle.sweep(v, source, -1, 5)

    odd_lane = iota((ROWS, 128), 1) % 2 == 1
    odd_row = iota((ROWS, 128), 0) % 2 == 1
    fine = Window(1, (-1, 9))
    fine.given(wx0, wy0, wz0, inv0)
    source = Stored(f0, -1)
    base = Stored(v0, -2)
    spread1 = {}
    for i in range(-1, 5):
        c = jnp.where(odd_lane, lanes(v[i], -1), v[i])
        spread1[i] = jnp.where(odd_row, rows(c, -1), c)
    v = {i: base[i] + spread1[i // 2] for i in range(-2, 10)}
    v = fine.sweep(v, source, -1, 9)
    v = fine.sweep(v, source, 0, 8)
    for i in range(8):
        out[i] = v[i][8:16]


WINDOW_PLANES = (12, 10, 8, 11, 10, 10, 10, 9, 8, 8, 8)


def f32(*shape):
    return jax.ShapeDtypeStruct(shape, jnp.float32)


def swap(x, axis, first):
    pairs = [(i, i + 1) for i in range(first, lax.axis_size(axis) - 1, 2)]
    return lax.ppermute(x, axis, pairs + [(b, a) for a, b in pairs])


def to_all(x, axis, count, groups=None):
    copies = jnp.broadcast_to(x[None], (count,) + x.shape)
    return lax.all_to_all(copies, axis, 0, 0, axis_index_groups=groups)


def shards(right_side, coefficient, previous):
    even = lax.axis_index("gx") % 2 == 0
    own = lax.optimization_barrier(jnp.concatenate([right_side, coefficient, previous])).reshape(3, 8, 8, 128)
    start, end = own[:, :HALO], own[:, -HALO:]
    near = swap(jnp.where(even, end, start), "gx", 0)
    far = swap(jnp.where(even, start, end), "gx", 1)

    params = pltpu.CompilerParams(vmem_limit_bytes=VMEM)
    array = pl.BlockSpec(memory_space=pltpu.VMEM)
    count = sum(len(tiles) for tiles in TILES)
    to_near, to_far = pl.pallas_call(
        pack_kernel,
        in_specs=[array] * 3,
        out_shape=(f32(count, 8, 128),) * 2,
        compiler_params=params,
        name="pack",
    )(own, near, far)
    from_far = swap(to_far, "gy", 1)
    from_near = swap(to_near, "gy", 0)

    lower, higher, v1, *window = pl.pallas_call(
        down_kernel,
        in_specs=[array] * 5,
        out_shape=(f32(8, 128),) * 3 + tuple(f32(n, ROWS, 128) for n in WINDOW_PLANES),
        compiler_params=params,
        name="down",
    )(own, near, far, from_far, from_near)

    gx = lax.axis_index("gx")
    before = lax.broadcasted_iota(jnp.int32, (32, 1, 1), 0) < gx
    blocks = jnp.where(before, lower.reshape(1, 1, 1024), higher.reshape(1, 1, 1024))
    blocks = lax.all_to_all(blocks, "gx", 0, 0)
    same_core = [[2 * z + c for z in range(8)] for c in range(2)]
    mine = to_all(blocks[:, :, :256].reshape(64, 128), "gy", 8, same_core).reshape(512, 128)
    beside = jnp.pad(blocks[:, 0, 256:], ((1, 1), (0, 0)))
    low = lax.dynamic_slice(beside, (gx, jnp.int32(0)), (1, 768))
    high = lax.dynamic_slice(beside, (gx + 2, jnp.int32(0)), (1, 768))
    vmid = jnp.concatenate([low.reshape(6, 128), v1, high.reshape(6, 128)])
    vnear, vfar = swap(vmid, "gy", 0), swap(vmid, "gy", 1)
    mine, vfar, vnear = lax.optimization_barrier((mine, vfar, vnear))
    other = swap(mine, "gy", 0)

    plane = pltpu.VMEM((32 + 2 * PAD, 16, 128), jnp.float32)
    return pl.pallas_call(
        up_kernel,
        in_specs=[array] * (5 + len(WINDOW_PLANES)),
        out_shape=f32(8, 8, 128),
        scratch_shapes=[plane] * 13 + [pltpu.VMEM((8, 16, 128), jnp.float32)],
        compiler_params=params,
        name="up",
    )(mine, other, *window, vmid, vfar, vnear)


def solution(mesh):
    spec = P("gx", "gy", None)
    return jax.shard_map(
        shards, mesh=mesh, in_specs=(spec,) * 3, out_specs=spec, check_vma=False
    )
```

```python
import jax
import jax.numpy as jnp
from jax import lax
from jax.experimental import pallas as pl
from jax.experimental.pallas import tpu as pltpu
from jax.sharding import PartitionSpec as P

RELAX = 0.8
KEEP = 1.0 - RELAX
HALO = 7
ROWS = 24
COARSE_SWEEPS = 8
VMEM = 48 * 1024 * 1024


def lanes(x, n):
    return pltpu.roll(x, (-n) % x.shape[1], axis=1)


def rows(x, n):
    return pltpu.roll(x, (-n) % x.shape[0], axis=0)


def iota(shape, dim):
    return lax.broadcasted_iota(jnp.int32, shape, dim)


class Window:
    def __init__(self, step, planes):
        self.step = step
        self.planes = planes

    def given(self, wx, wy, wz, inv):
        first = self.planes[0]
        self.wx, self.wy = Stored(wx, first - 1), Stored(wy, first)
        self.wz, self.inv = Stored(wz, first), Stored(inv, first)

    def hand_on(self, planes, wx, wy, wz, inv):
        first, end = planes
        for i in range(first - 1, end):
            wx[i - first + 1] = self.wx[i]
        for i in range(first, end):
            wy[i - first], wz[i - first], inv[i - first] = self.wy[i], self.wz[i], self.inv[i]

    def weights(self, coeff):
        first, end = self.planes
        lane = iota((ROWS, 128), 1)
        last = lane >= 128 - self.step
        edge = (lane < self.step) | last
        self.wx, self.wy, self.wz, self.diag, self.inv = {}, {}, {}, {}, {}
        for i in range(first - 1, end):
            self.wx[i] = coeff[i] + coeff[i + 1]
        for i in range(first, end):
            k = coeff[i]
            wy = k + rows(k, self.step)
            wz = jnp.where(last, 0.0, k + lanes(k, self.step))
            diag = self.wx[i] + self.wx[i - 1] + (wy + rows(wy, -self.step))
            diag = diag + (wz + lanes(wz, -self.step)) + jnp.where(edge, k, 0.0)
            self.wy[i], self.wz[i], self.diag[i] = wy, wz, diag
            self.inv[i] = jnp.where(k > 0.0, RELAX / diag, 0.0)

    def around(self, v, i):
        c = v[i]
        wy, wz, step = self.wy[i], self.wz[i], self.step
        total = self.wx[i] * v[i + 1] + self.wx[i - 1] * v[i - 1]
        total = total + (wy * rows(c, step) + rows(wy * c, -step))
        return total + (wz * lanes(c, step) + lanes(wz * c, -step))

    def sweep(self, v, source, first, end):
        return {
            i: KEEP * v[i] + self.inv[i] * (source[i] + self.around(v, i)) for i in range(first, end)
        }

    def residual(self, v, source, first, end):
        return {i: source[i] - self.diag[i] * v[i] + self.around(v, i) for i in range(first, end)}


class Stored:
    def __init__(self, ref, first):
        self.ref, self.first = ref, first

    def __getitem__(self, i):
        return self.ref[i - self.first]

    def __setitem__(self, i, value):
        self.ref[i - self.first] = value


def block_sum(low, high, step):
    s = low + high
    s = s + rows(s, step)
    return s + lanes(s, step)


def alone(*planes):
    return [(i, 8, None) for i in planes]


INNER = range(8)
NARROW = [(0, 6, -6), (7, 6, 13)] + alone(1, 2, 3, 4, 5, 6, -1, -2, 8, 9)
NARROW += [(-3, 5, -5), (10, 5, 12), (-4, 4, 11)]
WIDE = alone(*INNER, -1, -2, 8, 9)
WIDE += [(-3, 6, -7), (10, 6, 14), (-4, 5, -6), (11, 5, 13), (-5, 4, 12)]
TILES = (NARROW, WIDE, WIDE)


def planes_of(which, own, near, far):
    even = jnp.broadcast_to(lax.rem(lax.axis_index("gx"), 2), (8, 128)) == 0
    planes = {i: own[which, i] for i in INNER}
    for i in range(HALO):
        a, b = near[which, i], far[which, i]
        planes[i - HALO], planes[i + 8] = jnp.where(even, b, a), jnp.where(even, a, b)
    return planes


def pack_kernel(own, far, near, to_near, to_far):
    first = core_mask(8)
    row = iota((8, 128), 0)
    at = 0
    for which, tiles in enumerate(TILES):
        planes = planes_of(which, own, near, far)
        for a, n, b in tiles:
            upward = downward = planes[a]
            if b is not None:
                upward = jnp.where(row >= 8 - n, planes[a], rows(planes[b], n))
                downward = jnp.where(row < n, planes[a], rows(planes[b], -n))
            to_near[at] = jnp.where(first, upward, downward)
            to_far[at] = jnp.where(first, downward, upward)
            at += 1


def core_mask(rows_of):
    core = lax.rem(lax.axis_index("gy"), 2)
    return jnp.broadcast_to(core, (rows_of, 128)) == 0


def joined(first, mid, near, far):
    return jnp.concatenate([jnp.where(first, far, near), mid, jnp.where(first, near, far)], axis=0)


def down_kernel(
    own, xfar, xnear, far, near, lower, higher, v1_out, v0_out, f0_out, f1_out, wx0, wy0, wz0, inv0, wx1, wy1, wz1, inv1
):
    first = core_mask(8)

    fields, at = [], 0
    for which, tiles in enumerate(TILES):
        mid = planes_of(which, own, xnear, xfar)
        low, high = {}, {}
        for i, n, other in tiles:
            below_it, above_it = jnp.where(first, far[at], near[at]), jnp.where(first, near[at], far[at])
            low[i], high[i] = below_it, above_it
            if other is not None:
                low[other], high[other] = rows(below_it, -n), rows(above_it, n)
            at += 1
        fields.append({i: jnp.concatenate([low[i], mid[i], high[i]], axis=0) for i in low})
    source, coeff, v = fields
    source = {i: 2.0 * source[i] for i in range(-6, 14)}

    fine = Window(1, (-6, 14))
    fine.weights(coeff)
    v = fine.sweep(v, source, -6, 14)
    v = fine.sweep(v, source, -5, 13)
    for i in range(-2, 10):
        v0_out[i + 2] = v[i]
    for i in range(-1, 9):
        f0_out[i + 1] = source[i]
    fine.hand_on((-1, 9), wx0, wy0, wz0, inv0)
    r = fine.residual(v, source, -4, 12)

    source = {i: 0.5 * block_sum(r[2 * i], r[2 * i + 1], 1) for i in range(-2, 6)}
    coeff = {i: 0.125 * block_sum(coeff[2 * i], coeff[2 * i + 1], 1) for i in range(-3, 7)}
    for i in range(-2, 6):
        f1_out[i + 2] = source[i]
    middle = Window(2, (-2, 6))
    middle.weights(coeff)
    middle.hand_on((-2, 6), wx1, wy1, wz1, inv1)
    v = {i: middle.inv[i] * source[i] for i in range(-2, 6)}
    v = middle.sweep(v, source, -1, 5)
    even = iota((8, 128), 1) % 2 == 0
    for i in range(4):
        c = v[i][8:16]
        c = jnp.where(even, c, lanes(rows(c, 2), -1))
        for n, line in enumerate((c[0:1], c[4:5])):
            v1_out[2 * i + n : 2 * i + n + 1, :] = line
            if i < 3:
                lower[2 * i + n + 2 : 2 * i + n + 3, :] = line
            if i > 0:
                higher[2 * i + n : 2 * i + n + 1, :] = line
    r = middle.residual(v, source, 0, 4)

    source = [0.5 * block_sum(r[2 * i], r[2 * i + 1], 2)[8:16] for i in range(2)]
    coeff = [0.125 * block_sum(coeff[2 * i], coeff[2 * i + 1], 2)[8:16] for i in range(2)]
    lane, row = iota((8, 128), 1), iota((8, 128), 0)
    group = lane // 32
    pick = 4 * (lane % 32)
    for c, planes in enumerate((source, coeff)):
        dense = [jnp.take_along_axis(t, pick, axis=1) for t in planes]
        dense = jnp.where(group < 2, dense[0], dense[1])
        dense = jnp.where(row == 4 * (group % 2), dense, 0.0)
        dense = jnp.sum(dense, axis=0, keepdims=True)
        lower[c : c + 1, :] = dense
        higher[c : c + 1, :] = dense


class Coarse:
    def __init__(self, coeff, nxp, nxm, nyp, nym, ylast, yedge, zstep):
        self.nxp, self.nxm, self.nyp, self.nym, self.zstep = nxp, nxm, nyp, nym, zstep
        z = iota(coeff[0].shape, 1) % 32
        zlast = z >= 32 - zstep
        zedge = (z < zstep) | zlast
        self.wp = [k + n for k, n in zip(coeff, nxp(coeff))]
        self.wm = [k + n for k, n in zip(coeff, nxm(coeff))]
        self.wy = [jnp.where(ylast, 0.0, k + nyp(k)) for k in coeff]
        self.wz = [jnp.where(zlast, 0.0, k + lanes(k, zstep)) for k in coeff]
        self.diag = []
        for k, wp, wm, wy, wz in zip(coeff, self.wp, self.wm, self.wy, self.wz):
            diag = wp + wm + (wy + nym(wy)) + (wz + lanes(wz, -zstep))
            self.diag.append(diag + (jnp.where(yedge, k, 0.0) + jnp.where(zedge, k, 0.0)))
        self.inv = [RELAX / d for d in self.diag]

    def around(self, v):
        out = []
        for c, p, m, wp, wm, wy, wz in zip(
            v, self.nxp(v), self.nxm(v), self.wp, self.wm, self.wy, self.wz
        ):
            total = wp * p + wm * m
            total = total + (wy * self.nyp(c) + self.nym(wy * c))
            out.append(total + (wz * lanes(c, self.zstep) + lanes(wz * c, -self.zstep)))
        return out

    def first(self, source):
        return [i * f for i, f in zip(self.inv, source)]

    def sweep(self, v, source):
        around = self.around(v)
        return [KEEP * c + i * (f + t) for c, i, f, t in zip(v, self.inv, source, around)]

    def sweeps(self, v, source, count):
        step = lambda _, v: tuple(self.sweep(list(v), source))
        return list(lax.fori_loop(0, count, step, tuple(v), unroll=True))

    def residual(self, v, source):
        around = self.around(v)
        return [f - d * c + t for c, d, f, t in zip(v, self.diag, source, around)]


def above(c):
    return jnp.concatenate([c[8:], rows(c[:8], 1)], axis=0)


def below(c):
    return jnp.concatenate([rows(c[8:], -1), c[:8]], axis=0)


UNROLL = 6
PAD = 3


def up_kernel(
    mine, other, v0, f0, f1, wx0, wy0, wz0, inv0, wx1, wy1, wz1, inv1, vmid, vfar, vnear, out,
    k2, f2, va, vb, wxi, wxe, wyi, wye, wz2, diag2, inv2, sumk, sumr, e3,
):
    gx, gy = lax.axis_index("gx"), lax.axis_index("gy")
    first = core_mask(8)
    lane = iota((16, 128), 1)
    row = iota((16, 128), 0)
    group, z = lane // 32, lane % 32
    xl, yl = group // 2, group % 2
    zero = jnp.zeros((16, 128), jnp.float32)

    for ref in (k2, f2, va, vb, wxi, wxe, wyi, wye, wz2, inv2):
        for i in range(PAD):
            ref[i] = zero
            ref[32 + PAD + i] = zero
    for i in range(32):
        for c, ref in ((0, f2), (1, k2)):
            here = pl.ds(2 * i + c, 8, stride=64)
            a, b = mine[here, :], other[here, :]
            ref[i + PAD, :8] = jnp.where(first, a, b)
            ref[i + PAD, 8:] = jnp.where(first, b, a)

    def sides(c):
        up, down = lanes(c, 32), lanes(c, -32)
        inner = jnp.where(yl == 0, up, down)
        outer = jnp.where(yl == 1, above(down), below(up))
        return inner, outer

    yout = ((yl == 1) & (row == 15)) | ((yl == 0) & (row == 0))
    zlast = z == 31
    zedge = zlast | (z == 0)

    def advance(i, field, turned, body):
        before, here = turned
        after = lanes(field[i + 1], 64)
        body(i, field[i], here, jnp.where(xl == 1, after, before))
        return here, after

    def summed(k):
        k = k + lanes(k, 64)
        return k + lanes(k, 32)

    def prepare(i, k, inner, outer):
        a, b = k + inner, k + outer
        yi, yo = sides(k)
        c = k + yi
        e = jnp.where(yout, 0.0, k + yo)
        w = jnp.where(zlast, 0.0, k + lanes(k, 1))
        diag = (a + b) + (c + e) + (w + lanes(w, -1))
        diag = diag + (jnp.where(yout, k, 0.0) + jnp.where(zedge, k, 0.0))
        inv = RELAX / diag
        wxi[i], wxe[i], wyi[i], wye[i], wz2[i], diag2[i], inv2[i] = a, b, c, e, w, diag, inv
        va[i] = inv * f2[i]
        sumk[i] = summed(k)

    def around2(i, c, inner, outer):
        yi, yo = sides(c)
        w = wz2[i]
        total = wxi[i] * inner + wxe[i] * outer
        total = total + (wyi[i] * yi + wye[i] * yo)
        return total + (w * lanes(c, 1) + lanes(w * c, -1))

    def sweep2(i, c, inner, outer):
        return KEEP * c + inv2[i] * (f2[i] + around2(i, c, inner, outer))

    def first2(i, c, inner, outer):
        vb[i] = sweep2(i, c, inner, outer)

    def residual2(i, c, inner, outer):
        sumr[i] = summed(f2[i] - diag2[i] * c + around2(i, c, inner, outer))

    def three(i, state):
        ofk, ofa, ofb = state
        ofk = advance(i, k2, ofk, prepare)
        ofa = advance(i - 1, va, ofa, first2)
        return ofk, ofa, advance(i - 2, vb, ofb, residual2)

    ofk = (zero, lanes(k2[PAD], 64))
    ofk = advance(PAD, k2, ofk, prepare)
    ofk = advance(PAD + 1, k2, ofk, prepare)
    ofa = advance(PAD, va, (zero, lanes(va[PAD], 64)), first2)
    ofb = (zero, lanes(vb[PAD], 64))

    def steps(step, state):
        for u in range(UNROLL):
            state = three(PAD + 2 + UNROLL * step + u, state)
        return state

    _, ofa, ofb = lax.fori_loop(0, 30 // UNROLL, steps, (ofk, ofa, ofb))
    advance(PAD + 31, va, ofa, first2)
    ofb = advance(PAD + 30, vb, ofb, residual2)
    advance(PAD + 31, vb, ofb, residual2)

    def four(sums, q):
        t = jnp.where(group == 0, sums[4 * q + PAD], sums[4 * q + PAD + 1])
        t = jnp.where(group == 2, sums[4 * q + PAD + 2], t)
        t = jnp.where(group == 3, sums[4 * q + PAD + 3], t)
        return t + lanes(t, 1)

    c3 = [0.125 * four(sumk, q) for q in range(8)]
    f3 = [0.5 * four(sumr, q) for q in range(8)]

    def plus3(v):
        up = [lanes(c, 32) for c in v] + [zero]
        return [jnp.where(group < 3, up[q], up[q + 1]) for q in range(8)]

    def minus3(v):
        down = [zero] + [lanes(c, -32) for c in v]
        return [jnp.where(group > 0, down[q + 1], down[q]) for q in range(8)]

    level3 = Coarse(c3, plus3, minus3, above, below, row == 15, (row == 0) | (row == 15), 2)
    v3 = level3.sweep(level3.first(f3), f3)
    r3 = level3.residual(v3, f3)

    def restrict(values, x, y, zz):
        s = [t + lanes(t, x) for t in values]
        s = [y(t) for t in s]
        return [t + lanes(t, zz) for t in s]

    cores = lambda t: t[:8] + t[8:]
    f4 = [0.5 * s for s in restrict(r3, 32, cores, 2)]
    c4 = [0.125 * s for s in restrict(c3, 32, cores, 2)]
    zero8 = zero[:8]
    row8, lane8, group8 = row[:8], lane[:8], group[:8]

    def plus4(v):
        turn = [lanes(c, 64) for c in v] + [zero8]
        return [jnp.where(group8 < 2, turn[q], turn[q + 1]) for q in range(8)]

    def minus4(v):
        turn = [zero8] + [lanes(c, 64) for c in v]
        return [jnp.where(group8 < 2, turn[q], turn[q + 1]) for q in range(8)]

    def next_rows(n):
        return lambda c: rows(c, n)

    level4 = Coarse(
        c4, plus4, minus4, next_rows(1), next_rows(-1), row8 == 7, (row8 == 0) | (row8 == 7), 4
    )
    v4 = level4.sweep(level4.first(f4), f4)
    r4 = level4.residual(v4, f4)

    pair = lambda t: t + rows(t, 1)
    f5 = [0.5 * s for s in restrict(r4, 64, pair, 4)]
    c5 = [0.125 * s for s in restrict(c4, 64, pair, 4)]
    level5 = Coarse(
        c5,
        lambda v: v[1:] + [zero8],
        lambda v: [zero8] + v[:-1],
        next_rows(2),
        next_rows(-2),
        row8 >= 6,
        (row8 < 2) | (row8 >= 6),
        8,
    )
    v5 = level5.sweeps(level5.first(f5), f5, COARSE_SWEEPS - 1)

    def spread(c, bit):
        return jnp.where((iota(c.shape, 1) & bit) != 0, lanes(c, -bit), c)

    v5 = [jnp.where((row8 & 1) != 0, rows(c, -1), c) for c in v5]
    v4 = [c + spread(e, 4) for c, e in zip(v4, v5)]
    v4 = level4.sweeps(v4, f4, 2)

    v4 = [spread(jnp.where(group8 % 2 == 1, lanes(c, -32), c), 2) for c in v4]
    v3 = [c + jnp.concatenate([e, e], axis=0) for c, e in zip(v3, v4)]
    v3 = level3.sweeps(v3, f3, 2)

    for q in range(8):
        e3[q] = spread(v3[q], 1)
    for t in range(5):
        p = gx + t - 2
        inside = (p >= 0) & (p < 32)
        p = jnp.clip(p, 0, 31)
        e = jnp.where(group == jnp.where(inside, p % 4, -1), e3[p // 4], 0.0)
        va[gx + t - 2 + PAD] = vb[gx + t - 2 + PAD] + summed(e)

    def some(read, write, first, end):
        turned = [lanes(read[gx + t + PAD], 64) for t in range(first - 1, end + 1)]
        for u, t in enumerate(range(first, end)):
            i = gx + t + PAD
            outer = jnp.where(xl == 1, turned[u + 2], turned[u])
            write[i] = sweep2(i, read[i], turned[u + 1], outer)

    some(va, vb, -2, 3)
    some(vb, va, -1, 2)

    lane8 = iota((8, 128), 1)
    pick = 32 * (iota((8, 128), 0) // 4) + lane8 // 4
    wide = {}
    for t in range(-1, 2):
        for x in range(2):
            parts = []
            for b in range(-1, 2):
                y = gy + b
                inside = (y >= 0) & (y < 16)
                y = jnp.clip(y, 0, 15)
                line = va[gx + t + PAD, pl.ds(8 * (y % 2) + y // 2, 1), :]
                line = jnp.broadcast_to(jnp.where(inside, line, 0.0), (8, 128))
                parts.append(jnp.take_along_axis(line, 64 * x + pick, axis=1))
            wide[t, x] = jnp.concatenate(parts, axis=0)

    def correction(i):
        return wide[i // 4, (i % 4) // 2]

    middle = Window(2, (-2, 6))
    middle.given(wx1, wy1, wz1, inv1)
    source = Stored(f1, -2)
    upper_half = iota((8, 128), 0) >= 4
    second = (iota((ROWS, 128), 0) & 2) != 0

    def received(i):
        n = 2 * i + 6
        c = [jnp.where(upper_half, r[n + 1 : n + 2], r[n : n + 1]) for r in (vmid, vnear, vfar)]
        c = joined(first, *c)
        return jnp.where(second, lanes(c, 1), c)

    v = {i: received(i) + correction(i) for i in range(-3, 7)}
    v = middle.sweep(v, source, -2, 6)
    v = middle.sweep(v, source, -1, 5)

    odd_lane = iota((ROWS, 128), 1) % 2 == 1
    odd_row = iota((ROWS, 128), 0) % 2 == 1
    fine = Window(1, (-1, 9))
    fine.given(wx0, wy0, wz0, inv0)
    source = Stored(f0, -1)
    base = Stored(v0, -2)
    spread1 = {}
    for i in range(-1, 5):
        c = jnp.where(odd_lane, lanes(v[i], -1), v[i])
        spread1[i] = jnp.where(odd_row, rows(c, -1), c)
    v = {i: base[i] + spread1[i // 2] for i in range(-2, 10)}
    v = fine.sweep(v, source, -1, 9)
    v = fine.sweep(v, source, 0, 8)
    for i in range(8):
        out[i] = v[i][8:16]


WINDOW_PLANES = (12, 10, 8, 11, 10, 10, 10, 9, 8, 8, 8)


def f32(*shape):
    return jax.ShapeDtypeStruct(shape, jnp.float32)


def swap(x, axis, first):
    pairs = [(i, i + 1) for i in range(first, lax.axis_size(axis) - 1, 2)]
    return lax.ppermute(x, axis, pairs + [(b, a) for a, b in pairs])


def to_all(x, axis, count, groups=None):
    copies = jnp.broadcast_to(x[None], (count,) + x.shape)
    return lax.all_to_all(copies, axis, 0, 0, axis_index_groups=groups)


def shards(right_side, coefficient, previous):
    even = lax.axis_index("gx") % 2 == 0
    own = lax.optimization_barrier(jnp.concatenate([right_side, coefficient, previous])).reshape(3, 8, 8, 128)
    start, end = own[:, :HALO], own[:, -HALO:]
    near = swap(jnp.where(even, end, start), "gx", 0)
    far = swap(jnp.where(even, start, end), "gx", 1)

    params = pltpu.CompilerParams(vmem_limit_bytes=VMEM)
    array = pl.BlockSpec(memory_space=pltpu.VMEM)
    count = sum(len(tiles) for tiles in TILES)
    to_near, to_far = pl.pallas_call(
        pack_kernel,
        in_specs=[array] * 3,
        out_shape=(f32(count, 8, 128),) * 2,
        compiler_params=params,
        name="pack",
    )(own, far, near)
    from_far = swap(to_far, "gy", 1)
    from_near = swap(to_near, "gy", 0)

    lower, higher, v1, *window = pl.pallas_call(
        down_kernel,
        in_specs=[array] * 5,
        out_shape=(f32(8, 128),) * 3 + tuple(f32(n, ROWS, 128) for n in WINDOW_PLANES),
        compiler_params=params,
        name="down",
    )(own, far, near, from_far, from_near)

    gx = lax.axis_index("gx")
    before = lax.broadcasted_iota(jnp.int32, (32, 1, 1), 0) < gx
    blocks = jnp.where(before, lower.reshape(1, 1, 1024), higher.reshape(1, 1, 1024))
    blocks = lax.all_to_all(blocks, "gx", 0, 0)
    same_core = [[2 * z + c for z in range(8)] for c in range(2)]
    mine = to_all(blocks[:, :, :256].reshape(64, 128), "gy", 8, same_core).reshape(512, 128)
    beside = jnp.pad(blocks[:, 0, 256:], ((1, 1), (0, 0)))
    low = lax.dynamic_slice(beside, (gx, jnp.int32(0)), (1, 768))
    high = lax.dynamic_slice(beside, (gx + 2, jnp.int32(0)), (1, 768))
    vmid = jnp.concatenate([low.reshape(6, 128), v1, high.reshape(6, 128)])
    vnear, vfar = swap(vmid, "gy", 0), swap(vmid, "gy", 1)
    mine, vfar, vnear = lax.optimization_barrier((mine, vfar, vnear))
    other = swap(mine, "gy", 0)

    plane = pltpu.VMEM((32 + 2 * PAD, 16, 128), jnp.float32)
    return pl.pallas_call(
        up_kernel,
        in_specs=[array] * (5 + len(WINDOW_PLANES)),
        out_shape=f32(8, 8, 128),
        scratch_shapes=[plane] * 13 + [pltpu.VMEM((8, 16, 128), jnp.float32)],
        compiler_params=params,
        name="up",
    )(mine, other, *window, vmid, vfar, vnear)


def solution(mesh):
    spec = P("gx", "gy", None)
    return jax.shard_map(
        shards, mesh=mesh, in_specs=(spec,) * 3, out_specs=spec, check_vma=False
    )
```

```python
import jax
import jax.numpy as jnp
from jax import lax
from jax.experimental import pallas as pl
from jax.experimental.pallas import tpu as pltpu
from jax.sharding import PartitionSpec as P

RELAX = 0.8
KEEP = 1.0 - RELAX
HALO = 7
ROWS = 24
COARSE_SWEEPS = 8
VMEM = 48 * 1024 * 1024


def lanes(x, n):
    return pltpu.roll(x, (-n) % x.shape[1], axis=1)


def rows(x, n):
    return pltpu.roll(x, (-n) % x.shape[0], axis=0)


def iota(shape, dim):
    return lax.broadcasted_iota(jnp.int32, shape, dim)


class Window:
    def __init__(self, step, planes):
        self.step = step
        self.planes = planes

    def given(self, wx, wy, wz, inv):
        first = self.planes[0]
        self.wx, self.wy = Stored(wx, first - 1), Stored(wy, first)
        self.wz, self.inv = Stored(wz, first), Stored(inv, first)

    def hand_on(self, planes, wx, wy, wz, inv):
        first, end = planes
        for i in range(first - 1, end):
            wx[i - first + 1] = self.wx[i]
        for i in range(first, end):
            wy[i - first], wz[i - first], inv[i - first] = self.wy[i], self.wz[i], self.inv[i]

    def weights(self, coeff):
        first, end = self.planes
        lane = iota((ROWS, 128), 1)
        last = lane >= 128 - self.step
        edge = (lane < self.step) | last
        self.wx, self.wy, self.wz, self.diag, self.inv = {}, {}, {}, {}, {}
        for i in range(first - 1, end):
            self.wx[i] = coeff[i] + coeff[i + 1]
        for i in range(first, end):
            k = coeff[i]
            wy = k + rows(k, self.step)
            wz = jnp.where(last, 0.0, k + lanes(k, self.step))
            diag = self.wx[i] + self.wx[i - 1] + (wy + rows(wy, -self.step))
            diag = diag + (wz + lanes(wz, -self.step)) + jnp.where(edge, k, 0.0)
            self.wy[i], self.wz[i], self.diag[i] = wy, wz, diag
            self.inv[i] = jnp.where(k > 0.0, RELAX / diag, 0.0)

    def around(self, v, i):
        c = v[i]
        wy, wz, step = self.wy[i], self.wz[i], self.step
        total = self.wx[i] * v[i + 1] + self.wx[i - 1] * v[i - 1]
        total = total + (wy * rows(c, step) + rows(wy * c, -step))
        return total + (wz * lanes(c, step) + lanes(wz * c, -step))

    def sweep(self, v, source, first, end):
        return {
            i: KEEP * v[i] + self.inv[i] * (source[i] + self.around(v, i)) for i in range(first, end)
        }

    def residual(self, v, source, first, end):
        return {i: source[i] - self.diag[i] * v[i] + self.around(v, i) for i in range(first, end)}


class Stored:
    def __init__(self, ref, first):
        self.ref, self.first = ref, first

    def __getitem__(self, i):
        return self.ref[i - self.first]

    def __setitem__(self, i, value):
        self.ref[i - self.first] = value


def block_sum(low, high, step):
    s = low + high
    s = s + rows(s, step)
    return s + lanes(s, step)


def alone(*planes):
    return [(i, 8, None) for i in planes]


INNER = range(8)
NARROW = [(0, 6, -6), (7, 6, 13)] + alone(1, 2, 3, 4, 5, 6, -1, -2, 8, 9)
NARROW += [(-3, 5, -5), (10, 5, 12), (-4, 4, 11)]
WIDE = alone(*INNER, -1, -2, 8, 9)
WIDE += [(-3, 6, -7), (10, 6, 14), (-4, 5, -6), (11, 5, 13), (-5, 4, 12)]
TILES = (NARROW, WIDE, WIDE)


def planes_of(which, own, near, far):
    even = jnp.broadcast_to(lax.rem(lax.axis_index("gx"), 2), (8, 128)) == 0
    planes = {i: own[which, i] for i in INNER}
    for i in range(HALO):
        a, b = near[which, i], far[which, i]
        planes[i - HALO], planes[i + 8] = jnp.where(even, b, a), jnp.where(even, a, b)
    return planes


def pack_kernel(own, far, near, to_near, to_far):
    first = core_mask(8)
    row = iota((8, 128), 0)
    at = 0
    for which, tiles in enumerate(TILES):
        planes = planes_of(which, own, near, far)
        for a, n, b in tiles:
            upward = downward = planes[a]
            if b is not None:
                upward = jnp.where(row >= 8 - n, planes[a], rows(planes[b], n))
                downward = jnp.where(row < n, planes[a], rows(planes[b], -n))
            to_near[at] = jnp.where(first, upward, downward)
            to_far[at] = jnp.where(first, downward, upward)
            at += 1


def core_mask(rows_of):
    core = lax.rem(lax.axis_index("gy"), 2)
    return jnp.broadcast_to(core, (rows_of, 128)) == 0


def joined(first, mid, near, far):
    return jnp.concatenate([jnp.where(first, far, near), mid, jnp.where(first, near, far)], axis=0)


def down_kernel(
    own, xfar, xnear, far, near, lower, higher, v1_out, v0_out, f0_out, f1_out, wx0, wy0, wz0, inv0, wx1, wy1, wz1, inv1
):
    first = core_mask(8)

    fields, at = [], 0
    for which, tiles in enumerate(TILES):
        mid = planes_of(which, own, xnear, xfar)
        low, high = {}, {}
        for i, n, other in tiles:
            below_it, above_it = jnp.where(first, far[at], near[at]), jnp.where(first, near[at], far[at])
            low[i], high[i] = below_it, above_it
            if other is not None:
                low[other], high[other] = rows(below_it, -n), rows(above_it, n)
            at += 1
        fields.append({i: jnp.concatenate([low[i], mid[i], high[i]], axis=0) for i in low})
    source, coeff, v = fields
    source = {i: 2.0 * source[i] for i in range(-6, 14)}

    fine = Window(1, (-6, 14))
    fine.weights(coeff)
    v = fine.sweep(v, source, -6, 14)
    v = fine.sweep(v, source, -5, 13)
    for i in range(-2, 10):
        v0_out[i + 2] = v[i]
    for i in range(-1, 9):
        f0_out[i + 1] = source[i]
    fine.hand_on((-1, 9), wx0, wy0, wz0, inv0)
    r = fine.residual(v, source, -4, 12)

    source = {i: 0.5 * block_sum(r[2 * i], r[2 * i + 1], 1) for i in range(-2, 6)}
    coeff = {i: 0.125 * block_sum(coeff[2 * i], coeff[2 * i + 1], 1) for i in range(-3, 7)}
    for i in range(-2, 6):
        f1_out[i + 2] = source[i]
    middle = Window(2, (-2, 6))
    middle.weights(coeff)
    middle.hand_on((-2, 6), wx1, wy1, wz1, inv1)
    v = {i: middle.inv[i] * source[i] for i in range(-2, 6)}
    v = middle.sweep(v, source, -1, 5)
    even = iota((8, 128), 1) % 2 == 0
    for i in range(4):
        c = v[i][8:16]
        c = jnp.where(even, c, lanes(rows(c, 2), -1))
        for n, line in enumerate((c[0:1], c[4:5])):
            v1_out[2 * i + n : 2 * i + n + 1, :] = line
            if i < 3:
                lower[2 * i + n + 2 : 2 * i + n + 3, :] = line
            if i > 0:
                higher[2 * i + n : 2 * i + n + 1, :] = line
    r = middle.residual(v, source, 0, 4)

    source = [0.5 * block_sum(r[2 * i], r[2 * i + 1], 2)[8:16] for i in range(2)]
    coeff = [0.125 * block_sum(coeff[2 * i], coeff[2 * i + 1], 2)[8:16] for i in range(2)]
    lane, row = iota((8, 128), 1), iota((8, 128), 0)
    group = lane // 32
    pick = 4 * (lane % 32)
    for c, planes in enumerate((source, coeff)):
        dense = [jnp.take_along_axis(t, pick, axis=1) for t in planes]
        dense = jnp.where(group < 2, dense[0], dense[1])
        dense = jnp.where(row == 4 * (group % 2), dense, 0.0)
        dense = jnp.sum(dense, axis=0, keepdims=True)
        lower[c : c + 1, :] = dense
        higher[c : c + 1, :] = dense


class Coarse:
    def __init__(self, coeff, nxp, nxm, nyp, nym, ylast, yedge, zstep):
        self.nxp, self.nxm, self.nyp, self.nym, self.zstep = nxp, nxm, nyp, nym, zstep
        z = iota(coeff[0].shape, 1) % 32
        zlast = z >= 32 - zstep
        zedge = (z < zstep) | zlast
        self.wp = [k + n for k, n in zip(coeff, nxp(coeff))]
        self.wm = [k + n for k, n in zip(coeff, nxm(coeff))]
        self.wy = [jnp.where(ylast, 0.0, k + nyp(k)) for k in coeff]
        self.wz = [jnp.where(zlast, 0.0, k + lanes(k, zstep)) for k in coeff]
        self.diag = []
        for k, wp, wm, wy, wz in zip(coeff, self.wp, self.wm, self.wy, self.wz):
            diag = wp + wm + (wy + nym(wy)) + (wz + lanes(wz, -zstep))
            self.diag.append(diag + (jnp.where(yedge, k, 0.0) + jnp.where(zedge, k, 0.0)))
        self.inv = [RELAX / d for d in self.diag]

    def around(self, v):
        out = []
        for c, p, m, wp, wm, wy, wz in zip(
            v, self.nxp(v), self.nxm(v), self.wp, self.wm, self.wy, self.wz
        ):
            total = wp * p + wm * m
            total = total + (wy * self.nyp(c) + self.nym(wy * c))
            out.append(total + (wz * lanes(c, self.zstep) + lanes(wz * c, -self.zstep)))
        return out

    def first(self, source):
        return [i * f for i, f in zip(self.inv, source)]

    def sweep(self, v, source):
        around = self.around(v)
        return [KEEP * c + i * (f + t) for c, i, f, t in zip(v, self.inv, source, around)]

    def sweeps(self, v, source, count):
        step = lambda _, v: tuple(self.sweep(list(v), source))
        return list(lax.fori_loop(0, count, step, tuple(v), unroll=True))

    def residual(self, v, source):
        around = self.around(v)
        return [f - d * c + t for c, d, f, t in zip(v, self.diag, source, around)]


def above(c):
    return jnp.concatenate([c[8:], rows(c[:8], 1)], axis=0)


def below(c):
    return jnp.concatenate([rows(c[8:], -1), c[:8]], axis=0)


UNROLL = 10
PAD = 3


def up_kernel(
    mine, other, v0, f0, f1, wx0, wy0, wz0, inv0, wx1, wy1, wz1, inv1, vmid, vfar, vnear, out,
    k2, f2, va, vb, wxi, wxe, wyi, wye, wz2, diag2, inv2, sumk, sumr, e3,
):
    gx, gy = lax.axis_index("gx"), lax.axis_index("gy")
    first = core_mask(8)
    lane = iota((16, 128), 1)
    row = iota((16, 128), 0)
    group, z = lane // 32, lane % 32
    xl, yl = group // 2, group % 2
    zero = jnp.zeros((16, 128), jnp.float32)

    for ref in (k2, f2, va, vb, wxi, wxe, wyi, wye, wz2, inv2):
        for i in range(PAD):
            ref[i] = zero
            ref[32 + PAD + i] = zero
    for i in range(32):
        for c, ref in ((0, f2), (1, k2)):
            here = pl.ds(2 * i + c, 8, stride=64)
            a, b = mine[here, :], other[here, :]
            ref[i + PAD, :8] = jnp.where(first, a, b)
            ref[i + PAD, 8:] = jnp.where(first, b, a)

    def sides(c):
        up, down = lanes(c, 32), lanes(c, -32)
        inner = jnp.where(yl == 0, up, down)
        outer = jnp.where(yl == 1, above(down), below(up))
        return inner, outer

    yout = ((yl == 1) & (row == 15)) | ((yl == 0) & (row == 0))
    zlast = z == 31
    zedge = zlast | (z == 0)

    def advance(i, field, turned, body):
        before, here = turned
        after = lanes(field[i + 1], 64)
        body(i, field[i], here, jnp.where(xl == 1, after, before))
        return here, after

    def summed(k):
        k = k + lanes(k, 64)
        return k + lanes(k, 32)

    def prepare(i, k, inner, outer):
        a, b = k + inner, k + outer
        yi, yo = sides(k)
        c = k + yi
        e = jnp.where(yout, 0.0, k + yo)
        w = jnp.where(zlast, 0.0, k + lanes(k, 1))
        diag = (a + b) + (c + e) + (w + lanes(w, -1))
        diag = diag + (jnp.where(yout, k, 0.0) + jnp.where(zedge, k, 0.0))
        inv = RELAX / diag
        wxi[i], wxe[i], wyi[i], wye[i], wz2[i], diag2[i], inv2[i] = a, b, c, e, w, diag, inv
        va[i] = inv * f2[i]
        sumk[i] = summed(k)

    def around2(i, c, inner, outer):
        yi, yo = sides(c)
        w = wz2[i]
        total = wxi[i] * inner + wxe[i] * outer
        total = total + (wyi[i] * yi + wye[i] * yo)
        return total + (w * lanes(c, 1) + lanes(w * c, -1))

    def sweep2(i, c, inner, outer):
        return KEEP * c + inv2[i] * (f2[i] + around2(i, c, inner, outer))

    def first2(i, c, inner, outer):
        vb[i] = sweep2(i, c, inner, outer)

    def residual2(i, c, inner, outer):
        sumr[i] = summed(f2[i] - diag2[i] * c + around2(i, c, inner, outer))

    def three(i, state):
        ofk, ofa, ofb = state
        ofk = advance(i, k2, ofk, prepare)
        ofa = advance(i - 1, va, ofa, first2)
        return ofk, ofa, advance(i - 2, vb, ofb, residual2)

    ofk = (zero, lanes(k2[PAD], 64))
    ofk = advance(PAD, k2, ofk, prepare)
    ofk = advance(PAD + 1, k2, ofk, prepare)
    ofa = advance(PAD, va, (zero, lanes(va[PAD], 64)), first2)
    ofb = (zero, lanes(vb[PAD], 64))

    def steps(step, state):
        for u in range(UNROLL):
            state = three(PAD + 2 + UNROLL * step + u, state)
        return state

    _, ofa, ofb = lax.fori_loop(0, 30 // UNROLL, steps, (ofk, ofa, ofb))
    advance(PAD + 31, va, ofa, first2)
    ofb = advance(PAD + 30, vb, ofb, residual2)
    advance(PAD + 31, vb, ofb, residual2)

    def four(sums, q):
        t = jnp.where(group == 0, sums[4 * q + PAD], sums[4 * q + PAD + 1])
        t = jnp.where(group == 2, sums[4 * q + PAD + 2], t)
        t = jnp.where(group == 3, sums[4 * q + PAD + 3], t)
        return t + lanes(t, 1)

    c3 = [0.125 * four(sumk, q) for q in range(8)]
    f3 = [0.5 * four(sumr, q) for q in range(8)]

    def plus3(v):
        up = [lanes(c, 32) for c in v] + [zero]
        return [jnp.where(group < 3, up[q], up[q + 1]) for q in range(8)]

    def minus3(v):
        down = [zero] + [lanes(c, -32) for c in v]
        return [jnp.where(group > 0, down[q + 1], down[q]) for q in range(8)]

    level3 = Coarse(c3, plus3, minus3, above, below, row == 15, (row == 0) | (row == 15), 2)
    v3 = level3.sweep(level3.first(f3), f3)
    r3 = level3.residual(v3, f3)

    def restrict(values, x, y, zz):
        s = [t + lanes(t, x) for t in values]
        s = [y(t) for t in s]
        return [t + lanes(t, zz) for t in s]

    cores = lambda t: t[:8] + t[8:]
    f4 = [0.5 * s for s in restrict(r3, 32, cores, 2)]
    c4 = [0.125 * s for s in restrict(c3, 32, cores, 2)]
    zero8 = zero[:8]
    row8, lane8, group8 = row[:8], lane[:8], group[:8]

    def plus4(v):
        turn = [lanes(c, 64) for c in v] + [zero8]
        return [jnp.where(group8 < 2, turn[q], turn[q + 1]) for q in range(8)]

    def minus4(v):
        turn = [zero8] + [lanes(c, 64) for c in v]
        return [jnp.where(group8 < 2, turn[q], turn[q + 1]) for q in range(8)]

    def next_rows(n):
        return lambda c: rows(c, n)

    level4 = Coarse(
        c4, plus4, minus4, next_rows(1), next_rows(-1), row8 == 7, (row8 == 0) | (row8 == 7), 4
    )
    v4 = level4.sweep(level4.first(f4), f4)
    r4 = level4.residual(v4, f4)

    pair = lambda t: t + rows(t, 1)
    f5 = [0.5 * s for s in restrict(r4, 64, pair, 4)]
    c5 = [0.125 * s for s in restrict(c4, 64, pair, 4)]
    level5 = Coarse(
        c5,
        lambda v: v[1:] + [zero8],
        lambda v: [zero8] + v[:-1],
        next_rows(2),
        next_rows(-2),
        row8 >= 6,
        (row8 < 2) | (row8 >= 6),
        8,
    )
    v5 = level5.sweeps(level5.first(f5), f5, COARSE_SWEEPS - 1)

    def spread(c, bit):
        return jnp.where((iota(c.shape, 1) & bit) != 0, lanes(c, -bit), c)

    v5 = [jnp.where((row8 & 1) != 0, rows(c, -1), c) for c in v5]
    v4 = [c + spread(e, 4) for c, e in zip(v4, v5)]
    v4 = level4.sweeps(v4, f4, 2)

    v4 = [spread(jnp.where(group8 % 2 == 1, lanes(c, -32), c), 2) for c in v4]
    v3 = [c + jnp.concatenate([e, e], axis=0) for c, e in zip(v3, v4)]
    v3 = level3.sweeps(v3, f3, 2)

    for q in range(8):
        e3[q] = spread(v3[q], 1)
    for t in range(5):
        p = gx + t - 2
        inside = (p >= 0) & (p < 32)
        p = jnp.clip(p, 0, 31)
        e = jnp.where(group == jnp.where(inside, p % 4, -1), e3[p // 4], 0.0)
        va[gx + t - 2 + PAD] = vb[gx + t - 2 + PAD] + summed(e)

    def some(read, write, first, end):
        turned = [lanes(read[gx + t + PAD], 64) for t in range(first - 1, end + 1)]
        for u, t in enumerate(range(first, end)):
            i = gx + t + PAD
            outer = jnp.where(xl == 1, turned[u + 2], turned[u])
            write[i] = sweep2(i, read[i], turned[u + 1], outer)

    some(va, vb, -2, 3)
    some(vb, va, -1, 2)

    lane8 = iota((8, 128), 1)
    pick = 32 * (iota((8, 128), 0) // 4) + lane8 // 4
    wide = {}
    for t in range(-1, 2):
        for x in range(2):
            parts = []
            for b in range(-1, 2):
                y = gy + b
                inside = (y >= 0) & (y < 16)
                y = jnp.clip(y, 0, 15)
                line = va[gx + t + PAD, pl.ds(8 * (y % 2) + y // 2, 1), :]
                line = jnp.broadcast_to(jnp.where(inside, line, 0.0), (8, 128))
                parts.append(jnp.take_along_axis(line, 64 * x + pick, axis=1))
            wide[t, x] = jnp.concatenate(parts, axis=0)

    def correction(i):
        return wide[i // 4, (i % 4) // 2]

    middle = Window(2, (-2, 6))
    middle.given(wx1, wy1, wz1, inv1)
    source = Stored(f1, -2)
    upper_half = iota((8, 128), 0) >= 4
    second = (iota((ROWS, 128), 0) & 2) != 0

    def received(i):
        n = 2 * i + 6
        c = [jnp.where(upper_half, r[n + 1 : n + 2], r[n : n + 1]) for r in (vmid, vnear, vfar)]
        c = joined(first, *c)
        return jnp.where(second, lanes(c, 1), c)

    v = {i: received(i) + correction(i) for i in range(-3, 7)}
    v = middle.sweep(v, source, -2, 6)
    v = middle.sweep(v, source, -1, 5)

    odd_lane = iota((ROWS, 128), 1) % 2 == 1
    odd_row = iota((ROWS, 128), 0) % 2 == 1
    fine = Window(1, (-1, 9))
    fine.given(wx0, wy0, wz0, inv0)
    source = Stored(f0, -1)
    base = Stored(v0, -2)
    spread1 = {}
    for i in range(-1, 5):
        c = jnp.where(odd_lane, lanes(v[i], -1), v[i])
        spread1[i] = jnp.where(odd_row, rows(c, -1), c)
    v = {i: base[i] + spread1[i // 2] for i in range(-2, 10)}
    v = fine.sweep(v, source, -1, 9)
    v = fine.sweep(v, source, 0, 8)
    for i in range(8):
        out[i] = v[i][8:16]


WINDOW_PLANES = (12, 10, 8, 11, 10, 10, 10, 9, 8, 8, 8)


def f32(*shape):
    return jax.ShapeDtypeStruct(shape, jnp.float32)


def swap(x, axis, first):
    pairs = [(i, i + 1) for i in range(first, lax.axis_size(axis) - 1, 2)]
    return lax.ppermute(x, axis, pairs + [(b, a) for a, b in pairs])


def to_all(x, axis, count, groups=None):
    copies = jnp.broadcast_to(x[None], (count,) + x.shape)
    return lax.all_to_all(copies, axis, 0, 0, axis_index_groups=groups)


def shards(right_side, coefficient, previous):
    even = lax.axis_index("gx") % 2 == 0
    own = lax.optimization_barrier(jnp.concatenate([right_side, coefficient, previous])).reshape(3, 8, 8, 128)
    start, end = own[:, :HALO], own[:, -HALO:]
    near = swap(jnp.where(even, end, start), "gx", 0)
    far = swap(jnp.where(even, start, end), "gx", 1)

    params = pltpu.CompilerParams(vmem_limit_bytes=VMEM)
    array = pl.BlockSpec(memory_space=pltpu.VMEM)
    count = sum(len(tiles) for tiles in TILES)
    to_near, to_far = pl.pallas_call(
        pack_kernel,
        in_specs=[array] * 3,
        out_shape=(f32(count, 8, 128),) * 2,
        compiler_params=params,
        name="pack",
    )(own, far, near)
    from_far = swap(to_far, "gy", 1)
    from_near = swap(to_near, "gy", 0)

    lower, higher, v1, *window = pl.pallas_call(
        down_kernel,
        in_specs=[array] * 5,
        out_shape=(f32(8, 128),) * 3 + tuple(f32(n, ROWS, 128) for n in WINDOW_PLANES),
        compiler_params=params,
        name="down",
    )(own, far, near, from_far, from_near)

    gx = lax.axis_index("gx")
    before = lax.broadcasted_iota(jnp.int32, (32, 1, 1), 0) < gx
    blocks = jnp.where(before, lower.reshape(1, 1, 1024), higher.reshape(1, 1, 1024))
    blocks = lax.all_to_all(blocks, "gx", 0, 0)
    same_core = [[2 * z + c for z in range(8)] for c in range(2)]
    mine = to_all(blocks[:, :, :256].reshape(64, 128), "gy", 8, same_core).reshape(512, 128)
    beside = jnp.pad(blocks[:, 0, 256:], ((1, 1), (0, 0)))
    low = lax.dynamic_slice(beside, (gx, jnp.int32(0)), (1, 768))
    high = lax.dynamic_slice(beside, (gx + 2, jnp.int32(0)), (1, 768))
    vmid = jnp.concatenate([low.reshape(6, 128), v1, high.reshape(6, 128)])
    vnear, vfar = swap(vmid, "gy", 0), swap(vmid, "gy", 1)
    mine, vfar, vnear = lax.optimization_barrier((mine, vfar, vnear))
    other = swap(mine, "gy", 0)

    plane = pltpu.VMEM((32 + 2 * PAD, 16, 128), jnp.float32)
    return pl.pallas_call(
        up_kernel,
        in_specs=[array] * (5 + len(WINDOW_PLANES)),
        out_shape=f32(8, 8, 128),
        scratch_shapes=[plane] * 13 + [pltpu.VMEM((8, 16, 128), jnp.float32)],
        compiler_params=params,
        name="up",
    )(mine, other, *window, vmid, vfar, vnear)


def solution(mesh):
    spec = P("gx", "gy", None)
    return jax.shard_map(
        shards, mesh=mesh, in_specs=(spec,) * 3, out_specs=spec, check_vma=False
    )
```

```python
import jax
import jax.numpy as jnp
from jax import lax
from jax.experimental import pallas as pl
from jax.experimental.pallas import tpu as pltpu
from jax.sharding import PartitionSpec as P

RELAX = 0.8
KEEP = 1.0 - RELAX
HALO = 7
ROWS = 24
COARSE_SWEEPS = 8
VMEM = 48 * 1024 * 1024


def lanes(x, n):
    return pltpu.roll(x, (-n) % x.shape[1], axis=1)


def rows(x, n):
    return pltpu.roll(x, (-n) % x.shape[0], axis=0)


def iota(shape, dim):
    return lax.broadcasted_iota(jnp.int32, shape, dim)


class Window:
    def __init__(self, step, planes):
        self.step = step
        self.planes = planes

    def given(self, wx, wy, wz, inv):
        first = self.planes[0]
        self.wx, self.wy = Stored(wx, first - 1), Stored(wy, first)
        self.wz, self.inv = Stored(wz, first), Stored(inv, first)

    def hand_on(self, planes, wx, wy, wz, inv):
        first, end = planes
        for i in range(first - 1, end):
            wx[i - first + 1] = self.wx[i]
        for i in range(first, end):
            wy[i - first], wz[i - first], inv[i - first] = self.wy[i], self.wz[i], self.inv[i]

    def weights(self, coeff):
        first, end = self.planes
        lane = iota((ROWS, 128), 1)
        last = lane >= 128 - self.step
        edge = (lane < self.step) | last
        self.wx, self.wy, self.wz, self.diag, self.inv = {}, {}, {}, {}, {}
        for i in range(first - 1, end):
            self.wx[i] = coeff[i] + coeff[i + 1]
        for i in range(first, end):
            k = coeff[i]
            wy = k + rows(k, self.step)
            wz = jnp.where(last, 0.0, k + lanes(k, self.step))
            diag = self.wx[i] + self.wx[i - 1] + (wy + rows(wy, -self.step))
            diag = diag + (wz + lanes(wz, -self.step)) + jnp.where(edge, k, 0.0)
            self.wy[i], self.wz[i], self.diag[i] = wy, wz, diag
            self.inv[i] = jnp.where(k > 0.0, RELAX / diag, 0.0)

    def around(self, v, i):
        c = v[i]
        wy, wz, step = self.wy[i], self.wz[i], self.step
        total = self.wx[i] * v[i + 1] + self.wx[i - 1] * v[i - 1]
        total = total + (wy * rows(c, step) + rows(wy * c, -step))
        return total + (wz * lanes(c, step) + lanes(wz * c, -step))

    def sweep(self, v, source, first, end):
        return {
            i: KEEP * v[i] + self.inv[i] * (source[i] + self.around(v, i)) for i in range(first, end)
        }

    def residual(self, v, source, first, end):
        return {i: source[i] - self.diag[i] * v[i] + self.around(v, i) for i in range(first, end)}


class Stored:
    def __init__(self, ref, first):
        self.ref, self.first = ref, first

    def __getitem__(self, i):
        return self.ref[i - self.first]

    def __setitem__(self, i, value):
        self.ref[i - self.first] = value


def block_sum(low, high, step):
    s = low + high
    s = s + rows(s, step)
    return s + lanes(s, step)


def alone(*planes):
    return [(i, 8, None) for i in planes]


INNER = range(8)
NARROW = [(0, 6, -6), (7, 6, 13)] + alone(1, 2, 3, 4, 5, 6, -1, -2, 8, 9)
NARROW += [(-3, 5, -5), (10, 5, 12), (-4, 4, 11)]
WIDE = alone(*INNER, -1, -2, 8, 9)
WIDE += [(-3, 6, -7), (10, 6, 14), (-4, 5, -6), (11, 5, 13), (-5, 4, 12)]
TILES = (NARROW, WIDE, WIDE)


def planes_of(which, own, near, far):
    even = jnp.broadcast_to(lax.rem(lax.axis_index("gx"), 2), (8, 128)) == 0
    planes = {i: own[which, i] for i in INNER}
    for i in range(HALO):
        a, b = near[which, i], far[which, i]
        planes[i - HALO], planes[i + 8] = jnp.where(even, b, a), jnp.where(even, a, b)
    return planes


def pack_kernel(own, far, near, to_near, to_far):
    first = core_mask(8)
    row = iota((8, 128), 0)
    at = 0
    for which, tiles in enumerate(TILES):
        planes = planes_of(which, own, near, far)
        for a, n, b in tiles:
            upward = downward = planes[a]
            if b is not None:
                upward = jnp.where(row >= 8 - n, planes[a], rows(planes[b], n))
                downward = jnp.where(row < n, planes[a], rows(planes[b], -n))
            to_near[at] = jnp.where(first, upward, downward)
            to_far[at] = jnp.where(first, downward, upward)
            at += 1


def core_mask(rows_of):
    core = lax.rem(lax.axis_index("gy"), 2)
    return jnp.broadcast_to(core, (rows_of, 128)) == 0


def joined(first, mid, near, far):
    return jnp.concatenate([jnp.where(first, far, near), mid, jnp.where(first, near, far)], axis=0)


def down_kernel(
    own, xfar, xnear, far, near, lower, higher, v1_out, v0_out, f0_out, f1_out, wx0, wy0, wz0, inv0, wx1, wy1, wz1, inv1
):
    first = core_mask(8)

    fields, at = [], 0
    for which, tiles in enumerate(TILES):
        mid = planes_of(which, own, xnear, xfar)
        low, high = {}, {}
        for i, n, other in tiles:
            below_it, above_it = jnp.where(first, far[at], near[at]), jnp.where(first, near[at], far[at])
            low[i], high[i] = below_it, above_it
            if other is not None:
                low[other], high[other] = rows(below_it, -n), rows(above_it, n)
            at += 1
        fields.append({i: jnp.concatenate([low[i], mid[i], high[i]], axis=0) for i in low})
    source, coeff, v = fields
    source = {i: 2.0 * source[i] for i in range(-6, 14)}

    fine = Window(1, (-6, 14))
    fine.weights(coeff)
    v = fine.sweep(v, source, -6, 14)
    v = fine.sweep(v, source, -5, 13)
    for i in range(-2, 10):
        v0_out[i + 2] = v[i]
    for i in range(-1, 9):
        f0_out[i + 1] = source[i]
    fine.hand_on((-1, 9), wx0, wy0, wz0, inv0)
    r = fine.residual(v, source, -4, 12)

    source = {i: 0.5 * block_sum(r[2 * i], r[2 * i + 1], 1) for i in range(-2, 6)}
    coeff = {i: 0.125 * block_sum(coeff[2 * i], coeff[2 * i + 1], 1) for i in range(-3, 7)}
    for i in range(-2, 6):
        f1_out[i + 2] = source[i]
    middle = Window(2, (-2, 6))
    middle.weights(coeff)
    middle.hand_on((-2, 6), wx1, wy1, wz1, inv1)
    v = {i: middle.inv[i] * source[i] for i in range(-2, 6)}
    v = middle.sweep(v, source, -1, 5)
    even = iota((8, 128), 1) % 2 == 0
    for i in range(4):
        c = v[i][8:16]
        c = jnp.where(even, c, lanes(rows(c, 2), -1))
        for n, line in enumerate((c[0:1], c[4:5])):
            v1_out[2 * i + n : 2 * i + n + 1, :] = line
            if i < 3:
                lower[2 * i + n + 2 : 2 * i + n + 3, :] = line
            if i > 0:
                higher[2 * i + n : 2 * i + n + 1, :] = line
    r = middle.residual(v, source, 0, 4)

    source = [0.5 * block_sum(r[2 * i], r[2 * i + 1], 2)[8:16] for i in range(2)]
    coeff = [0.125 * block_sum(coeff[2 * i], coeff[2 * i + 1], 2)[8:16] for i in range(2)]
    lane, row = iota((8, 128), 1), iota((8, 128), 0)
    group = lane // 32
    pick = 4 * (lane % 32)
    for c, planes in enumerate((source, coeff)):
        dense = [jnp.take_along_axis(t, pick, axis=1) for t in planes]
        dense = jnp.where(group < 2, dense[0], dense[1])
        dense = jnp.where(row == 4 * (group % 2), dense, 0.0)
        dense = jnp.sum(dense, axis=0, keepdims=True)
        lower[c : c + 1, :] = dense
        higher[c : c + 1, :] = dense


class Coarse:
    def __init__(self, coeff, nxp, nxm, nyp, nym, ylast, yedge, zstep):
        self.nxp, self.nxm, self.nyp, self.nym, self.zstep = nxp, nxm, nyp, nym, zstep
        z = iota(coeff[0].shape, 1) % 32
        zlast = z >= 32 - zstep
        zedge = (z < zstep) | zlast
        self.wp = [k + n for k, n in zip(coeff, nxp(coeff))]
        self.wm = [k + n for k, n in zip(coeff, nxm(coeff))]
        self.wy = [jnp.where(ylast, 0.0, k + nyp(k)) for k in coeff]
        self.wz = [jnp.where(zlast, 0.0, k + lanes(k, zstep)) for k in coeff]
        self.diag = []
        for k, wp, wm, wy, wz in zip(coeff, self.wp, self.wm, self.wy, self.wz):
            diag = wp + wm + (wy + nym(wy)) + (wz + lanes(wz, -zstep))
            self.diag.append(diag + (jnp.where(yedge, k, 0.0) + jnp.where(zedge, k, 0.0)))
        self.inv = [RELAX / d for d in self.diag]

    def around(self, v):
        out = []
        for c, p, m, wp, wm, wy, wz in zip(
            v, self.nxp(v), self.nxm(v), self.wp, self.wm, self.wy, self.wz
        ):
            total = wp * p + wm * m
            total = total + (wy * self.nyp(c) + self.nym(wy * c))
            out.append(total + (wz * lanes(c, self.zstep) + lanes(wz * c, -self.zstep)))
        return out

    def first(self, source):
        return [i * f for i, f in zip(self.inv, source)]

    def sweep(self, v, source):
        around = self.around(v)
        return [KEEP * c + i * (f + t) for c, i, f, t in zip(v, self.inv, source, around)]

    def sweeps(self, v, source, count):
        step = lambda _, v: tuple(self.sweep(list(v), source))
        return list(lax.fori_loop(0, count, step, tuple(v), unroll=True))

    def residual(self, v, source):
        around = self.around(v)
        return [f - d * c + t for c, d, f, t in zip(v, self.diag, source, around)]


def above(c):
    return jnp.concatenate([c[8:], rows(c[:8], 1)], axis=0)


def below(c):
    return jnp.concatenate([rows(c[8:], -1), c[:8]], axis=0)


UNROLL = 10
PAD = 3


def order_kernel(blocks, planes):
    for c in range(2):
        for i in range(32):
            planes[c, i] = blocks[pl.ds(2 * i + c, 8, stride=64), :]


def up_kernel(
    mine, other, v0, f0, f1, wx0, wy0, wz0, inv0, wx1, wy1, wz1, inv1, vmid, vfar, vnear, out,
    k2, f2, va, vb, wxi, wxe, wyi, wye, wz2, diag2, inv2, sumk, sumr, e3,
):
    gx, gy = lax.axis_index("gx"), lax.axis_index("gy")
    first = core_mask(8)
    lane = iota((16, 128), 1)
    row = iota((16, 128), 0)
    group, z = lane // 32, lane % 32
    xl, yl = group // 2, group % 2
    zero = jnp.zeros((16, 128), jnp.float32)

    for ref in (k2, f2, va, vb, wxi, wxe, wyi, wye, wz2, inv2):
        for i in range(PAD):
            ref[i] = zero
            ref[32 + PAD + i] = zero
    for i in range(32):
        for c, ref in ((0, f2), (1, k2)):
            a, b = mine[c, i], other[c, i]
            ref[i + PAD, :8] = jnp.where(first, a, b)
            ref[i + PAD, 8:] = jnp.where(first, b, a)

    def sides(c):
        up, down = lanes(c, 32), lanes(c, -32)
        inner = jnp.where(yl == 0, up, down)
        outer = jnp.where(yl == 1, above(down), below(up))
        return inner, outer

    yout = ((yl == 1) & (row == 15)) | ((yl == 0) & (row == 0))
    zlast = z == 31
    zedge = zlast | (z == 0)

    def advance(i, field, turned, body):
        before, here = turned
        after = lanes(field[i + 1], 64)
        body(i, field[i], here, jnp.where(xl == 1, after, before))
        return here, after

    def summed(k):
        k = k + lanes(k, 64)
        return k + lanes(k, 32)

    def prepare(i, k, inner, outer):
        a, b = k + inner, k + outer
        yi, yo = sides(k)
        c = k + yi
        e = jnp.where(yout, 0.0, k + yo)
        w = jnp.where(zlast, 0.0, k + lanes(k, 1))
        diag = (a + b) + (c + e) + (w + lanes(w, -1))
        diag = diag + (jnp.where(yout, k, 0.0) + jnp.where(zedge, k, 0.0))
        inv = RELAX / diag
        wxi[i], wxe[i], wyi[i], wye[i], wz2[i], diag2[i], inv2[i] = a, b, c, e, w, diag, inv
        va[i] = inv * f2[i]
        sumk[i] = summed(k)

    def around2(i, c, inner, outer):
        yi, yo = sides(c)
        w = wz2[i]
        total = wxi[i] * inner + wxe[i] * outer
        total = total + (wyi[i] * yi + wye[i] * yo)
        return total + (w * lanes(c, 1) + lanes(w * c, -1))

    def sweep2(i, c, inner, outer):
        return KEEP * c + inv2[i] * (f2[i] + around2(i, c, inner, outer))

    def first2(i, c, inner, outer):
        vb[i] = sweep2(i, c, inner, outer)

    def residual2(i, c, inner, outer):
        sumr[i] = summed(f2[i] - diag2[i] * c + around2(i, c, inner, outer))

    def three(i, state):
        ofk, ofa, ofb = state
        ofk = advance(i, k2, ofk, prepare)
        ofa = advance(i - 1, va, ofa, first2)
        return ofk, ofa, advance(i - 2, vb, ofb, residual2)

    ofk = (zero, lanes(k2[PAD], 64))
    ofk = advance(PAD, k2, ofk, prepare)
    ofk = advance(PAD + 1, k2, ofk, prepare)
    ofa = advance(PAD, va, (zero, lanes(va[PAD], 64)), first2)
    ofb = (zero, lanes(vb[PAD], 64))

    def steps(step, state):
        for u in range(UNROLL):
            state = three(PAD + 2 + UNROLL * step + u, state)
        return state

    _, ofa, ofb = lax.fori_loop(0, 30 // UNROLL, steps, (ofk, ofa, ofb))
    advance(PAD + 31, va, ofa, first2)
    ofb = advance(PAD + 30, vb, ofb, residual2)
    advance(PAD + 31, vb, ofb, residual2)

    def four(sums, q):
        t = jnp.where(group == 0, sums[4 * q + PAD], sums[4 * q + PAD + 1])
        t = jnp.where(group == 2, sums[4 * q + PAD + 2], t)
        t = jnp.where(group == 3, sums[4 * q + PAD + 3], t)
        return t + lanes(t, 1)

    c3 = [0.125 * four(sumk, q) for q in range(8)]
    f3 = [0.5 * four(sumr, q) for q in range(8)]

    def plus3(v):
        up = [lanes(c, 32) for c in v] + [zero]
        return [jnp.where(group < 3, up[q], up[q + 1]) for q in range(8)]

    def minus3(v):
        down = [zero] + [lanes(c, -32) for c in v]
        return [jnp.where(group > 0, down[q + 1], down[q]) for q in range(8)]

    level3 = Coarse(c3, plus3, minus3, above, below, row == 15, (row == 0) | (row == 15), 2)
    v3 = level3.sweep(level3.first(f3), f3)
    r3 = level3.residual(v3, f3)

    def restrict(values, x, y, zz):
        s = [t + lanes(t, x) for t in values]
        s = [y(t) for t in s]
        return [t + lanes(t, zz) for t in s]

    cores = lambda t: t[:8] + t[8:]
    f4 = [0.5 * s for s in restrict(r3, 32, cores, 2)]
    c4 = [0.125 * s for s in restrict(c3, 32, cores, 2)]
    zero8 = zero[:8]
    row8, lane8, group8 = row[:8], lane[:8], group[:8]

    def plus4(v):
        turn = [lanes(c, 64) for c in v] + [zero8]
        return [jnp.where(group8 < 2, turn[q], turn[q + 1]) for q in range(8)]

    def minus4(v):
        turn = [zero8] + [lanes(c, 64) for c in v]
        return [jnp.where(group8 < 2, turn[q], turn[q + 1]) for q in range(8)]

    def next_rows(n):
        return lambda c: rows(c, n)

    level4 = Coarse(
        c4, plus4, minus4, next_rows(1), next_rows(-1), row8 == 7, (row8 == 0) | (row8 == 7), 4
    )
    v4 = level4.sweep(level4.first(f4), f4)
    r4 = level4.residual(v4, f4)

    pair = lambda t: t + rows(t, 1)
    f5 = [0.5 * s for s in restrict(r4, 64, pair, 4)]
    c5 = [0.125 * s for s in restrict(c4, 64, pair, 4)]
    level5 = Coarse(
        c5,
        lambda v: v[1:] + [zero8],
        lambda v: [zero8] + v[:-1],
        next_rows(2),
        next_rows(-2),
        row8 >= 6,
        (row8 < 2) | (row8 >= 6),
        8,
    )
    v5 = level5.sweeps(level5.first(f5), f5, COARSE_SWEEPS - 1)

    def spread(c, bit):
        return jnp.where((iota(c.shape, 1) & bit) != 0, lanes(c, -bit), c)

    v5 = [jnp.where((row8 & 1) != 0, rows(c, -1), c) for c in v5]
    v4 = [c + spread(e, 4) for c, e in zip(v4, v5)]
    v4 = level4.sweeps(v4, f4, 2)

    v4 = [spread(jnp.where(group8 % 2 == 1, lanes(c, -32), c), 2) for c in v4]
    v3 = [c + jnp.concatenate([e, e], axis=0) for c, e in zip(v3, v4)]
    v3 = level3.sweeps(v3, f3, 2)

    for q in range(8):
        e3[q] = spread(v3[q], 1)
    for t in range(5):
        p = gx + t - 2
        inside = (p >= 0) & (p < 32)
        p = jnp.clip(p, 0, 31)
        e = jnp.where(group == jnp.where(inside, p % 4, -1), e3[p // 4], 0.0)
        va[gx + t - 2 + PAD] = vb[gx + t - 2 + PAD] + summed(e)

    def some(read, write, first, end):
        turned = [lanes(read[gx + t + PAD], 64) for t in range(first - 1, end + 1)]
        for u, t in enumerate(range(first, end)):
            i = gx + t + PAD
            outer = jnp.where(xl == 1, turned[u + 2], turned[u])
            write[i] = sweep2(i, read[i], turned[u + 1], outer)

    some(va, vb, -2, 3)
    some(vb, va, -1, 2)

    lane8 = iota((8, 128), 1)
    pick = 32 * (iota((8, 128), 0) // 4) + lane8 // 4
    wide = {}
    for t in range(-1, 2):
        for x in range(2):
            parts = []
            for b in range(-1, 2):
                y = gy + b
                inside = (y >= 0) & (y < 16)
                y = jnp.clip(y, 0, 15)
                line = va[gx + t + PAD, pl.ds(8 * (y % 2) + y // 2, 1), :]
                line = jnp.broadcast_to(jnp.where(inside, line, 0.0), (8, 128))
                parts.append(jnp.take_along_axis(line, 64 * x + pick, axis=1))
            wide[t, x] = jnp.concatenate(parts, axis=0)

    def correction(i):
        return wide[i // 4, (i % 4) // 2]

    middle = Window(2, (-2, 6))
    middle.given(wx1, wy1, wz1, inv1)
    source = Stored(f1, -2)
    upper_half = iota((8, 128), 0) >= 4
    second = (iota((ROWS, 128), 0) & 2) != 0

    def received(i):
        n = 2 * i + 6
        c = [jnp.where(upper_half, r[n + 1 : n + 2], r[n : n + 1]) for r in (vmid, vnear, vfar)]
        c = joined(first, *c)
        return jnp.where(second, lanes(c, 1), c)

    v = {i: received(i) + correction(i) for i in range(-3, 7)}
    v = middle.sweep(v, source, -2, 6)
    v = middle.sweep(v, source, -1, 5)

    odd_lane = iota((ROWS, 128), 1) % 2 == 1
    odd_row = iota((ROWS, 128), 0) % 2 == 1
    fine = Window(1, (-1, 9))
    fine.given(wx0, wy0, wz0, inv0)
    source = Stored(f0, -1)
    base = Stored(v0, -2)
    spread1 = {}
    for i in range(-1, 5):
        c = jnp.where(odd_lane, lanes(v[i], -1), v[i])
        spread1[i] = jnp.where(odd_row, rows(c, -1), c)
    v = {i: base[i] + spread1[i // 2] for i in range(-2, 10)}
    v = fine.sweep(v, source, -1, 9)
    v = fine.sweep(v, source, 0, 8)
    for i in range(8):
        out[i] = v[i][8:16]


WINDOW_PLANES = (12, 10, 8, 11, 10, 10, 10, 9, 8, 8, 8)


def f32(*shape):
    return jax.ShapeDtypeStruct(shape, jnp.float32)


def swap(x, axis, first):
    pairs = [(i, i + 1) for i in range(first, lax.axis_size(axis) - 1, 2)]
    return lax.ppermute(x, axis, pairs + [(b, a) for a, b in pairs])


def to_all(x, axis, count, groups=None):
    copies = jnp.broadcast_to(x[None], (count,) + x.shape)
    return lax.all_to_all(copies, axis, 0, 0, axis_index_groups=groups)


def shards(right_side, coefficient, previous):
    even = lax.axis_index("gx") % 2 == 0
    own = lax.optimization_barrier(jnp.concatenate([right_side, coefficient, previous])).reshape(3, 8, 8, 128)
    start, end = own[:, :HALO], own[:, -HALO:]
    near = swap(jnp.where(even, end, start), "gx", 0)
    far = swap(jnp.where(even, start, end), "gx", 1)

    params = pltpu.CompilerParams(vmem_limit_bytes=VMEM)
    array = pl.BlockSpec(memory_space=pltpu.VMEM)
    count = sum(len(tiles) for tiles in TILES)
    to_near, to_far = pl.pallas_call(
        pack_kernel,
        in_specs=[array] * 3,
        out_shape=(f32(count, 8, 128),) * 2,
        compiler_params=params,
        name="pack",
    )(own, far, near)
    from_far = swap(to_far, "gy", 1)
    from_near = swap(to_near, "gy", 0)

    lower, higher, v1, *window = pl.pallas_call(
        down_kernel,
        in_specs=[array] * 5,
        out_shape=(f32(8, 128),) * 3 + tuple(f32(n, ROWS, 128) for n in WINDOW_PLANES),
        compiler_params=params,
        name="down",
    )(own, far, near, from_far, from_near)

    gx = lax.axis_index("gx")
    before = lax.broadcasted_iota(jnp.int32, (32, 1, 1), 0) < gx
    blocks = jnp.where(before, lower.reshape(1, 1, 1024), higher.reshape(1, 1, 1024))
    blocks = lax.all_to_all(blocks, "gx", 0, 0)
    same_core = [[2 * z + c for z in range(8)] for c in range(2)]
    mine = to_all(blocks[:, :, :256].reshape(64, 128), "gy", 8, same_core).reshape(512, 128)
    mine = pl.pallas_call(
        order_kernel,
        in_specs=[array],
        out_shape=f32(2, 32, 8, 128),
        compiler_params=params,
        name="order",
    )(mine)
    beside = jnp.pad(blocks[:, 0, 256:], ((1, 1), (0, 0)))
    low = lax.dynamic_slice(beside, (gx, jnp.int32(0)), (1, 768))
    high = lax.dynamic_slice(beside, (gx + 2, jnp.int32(0)), (1, 768))
    vmid = jnp.concatenate([low.reshape(6, 128), v1, high.reshape(6, 128)])
    vnear, vfar = swap(vmid, "gy", 0), swap(vmid, "gy", 1)
    mine, vfar, vnear = lax.optimization_barrier((mine, vfar, vnear))
    other = swap(mine, "gy", 0)

    plane = pltpu.VMEM((32 + 2 * PAD, 16, 128), jnp.float32)
    return pl.pallas_call(
        up_kernel,
        in_specs=[array] * (5 + len(WINDOW_PLANES)),
        out_shape=f32(8, 8, 128),
        scratch_shapes=[plane] * 13 + [pltpu.VMEM((8, 16, 128), jnp.float32)],
        compiler_params=params,
        name="up",
    )(mine, other, *window, vmid, vfar, vnear)


def solution(mesh):
    spec = P("gx", "gy", None)
    return jax.shard_map(
        shards, mesh=mesh, in_specs=(spec,) * 3, out_specs=spec, check_vma=False
    )
```

```python
import jax
import jax.numpy as jnp
from jax import lax
from jax.experimental import pallas as pl
from jax.experimental.pallas import tpu as pltpu
from jax.sharding import PartitionSpec as P

RELAX = 0.8
KEEP = 1.0 - RELAX
HALO = 7
ROWS = 24
COARSE_SWEEPS = 8
VMEM = 48 * 1024 * 1024


def lanes(x, n):
    return pltpu.roll(x, (-n) % x.shape[1], axis=1)


def rows(x, n):
    return pltpu.roll(x, (-n) % x.shape[0], axis=0)


def iota(shape, dim):
    return lax.broadcasted_iota(jnp.int32, shape, dim)


class Window:
    def __init__(self, step, planes):
        self.step = step
        self.planes = planes

    def given(self, wx, wy, wz, inv):
        first = self.planes[0]
        self.wx, self.wy = Stored(wx, first - 1), Stored(wy, first)
        self.wz, self.inv = Stored(wz, first), Stored(inv, first)

    def hand_on(self, planes, wx, wy, wz, inv):
        first, end = planes
        for i in range(first - 1, end):
            wx[i - first + 1] = self.wx[i]
        for i in range(first, end):
            wy[i - first], wz[i - first], inv[i - first] = self.wy[i], self.wz[i], self.inv[i]

    def weights(self, coeff):
        first, end = self.planes
        lane = iota((ROWS, 128), 1)
        last = lane >= 128 - self.step
        edge = (lane < self.step) | last
        self.wx, self.wy, self.wz, self.diag, self.inv = {}, {}, {}, {}, {}
        for i in range(first - 1, end):
            self.wx[i] = coeff[i] + coeff[i + 1]
        for i in range(first, end):
            k = coeff[i]
            wy = k + rows(k, self.step)
            wz = jnp.where(last, 0.0, k + lanes(k, self.step))
            diag = self.wx[i] + self.wx[i - 1] + (wy + rows(wy, -self.step))
            diag = diag + (wz + lanes(wz, -self.step)) + jnp.where(edge, k, 0.0)
            self.wy[i], self.wz[i], self.diag[i] = wy, wz, diag
            self.inv[i] = jnp.where(k > 0.0, RELAX / diag, 0.0)

    def around(self, v, i):
        c = v[i]
        wy, wz, step = self.wy[i], self.wz[i], self.step
        total = self.wx[i] * v[i + 1] + self.wx[i - 1] * v[i - 1]
        total = total + (wy * rows(c, step) + rows(wy * c, -step))
        return total + (wz * lanes(c, step) + lanes(wz * c, -step))

    def sweep(self, v, source, first, end):
        return {
            i: KEEP * v[i] + self.inv[i] * (source[i] + self.around(v, i)) for i in range(first, end)
        }

    def residual(self, v, source, first, end):
        return {i: source[i] - self.diag[i] * v[i] + self.around(v, i) for i in range(first, end)}


class Stored:
    def __init__(self, ref, first):
        self.ref, self.first = ref, first

    def __getitem__(self, i):
        return self.ref[i - self.first]

    def __setitem__(self, i, value):
        self.ref[i - self.first] = value


def block_sum(low, high, step):
    s = low + high
    s = s + rows(s, step)
    return s + lanes(s, step)


def alone(*planes):
    return [(i, 8, None) for i in planes]


INNER = range(8)
NARROW = [(0, 6, -6), (7, 6, 13)] + alone(1, 2, 3, 4, 5, 6, -1, -2, 8, 9)
NARROW += [(-3, 5, -5), (10, 5, 12), (-4, 4, 11)]
WIDE = alone(*INNER, -1, -2, 8, 9)
WIDE += [(-3, 6, -7), (10, 6, 14), (-4, 5, -6), (11, 5, 13), (-5, 4, 12)]
TILES = (NARROW, WIDE, WIDE)


def planes_of(which, own, near, far):
    even = jnp.broadcast_to(lax.rem(lax.axis_index("gx"), 2), (8, 128)) == 0
    planes = {i: own[which, i] for i in INNER}
    for i in range(HALO):
        a, b = near[which, i], far[which, i]
        planes[i - HALO], planes[i + 8] = jnp.where(even, b, a), jnp.where(even, a, b)
    return planes


def pack_kernel(own, far, near, to_near, to_far):
    first = core_mask(8)
    row = iota((8, 128), 0)
    at = 0
    for which, tiles in enumerate(TILES):
        planes = planes_of(which, own, near, far)
        for a, n, b in tiles:
            upward = downward = planes[a]
            if b is not None:
                upward = jnp.where(row >= 8 - n, planes[a], rows(planes[b], n))
                downward = jnp.where(row < n, planes[a], rows(planes[b], -n))
            to_near[at] = jnp.where(first, upward, downward)
            to_far[at] = jnp.where(first, downward, upward)
            at += 1


def core_mask(rows_of):
    core = lax.rem(lax.axis_index("gy"), 2)
    return jnp.broadcast_to(core, (rows_of, 128)) == 0


def joined(first, mid, near, far):
    return jnp.concatenate([jnp.where(first, far, near), mid, jnp.where(first, near, far)], axis=0)


def down_kernel(
    own, xfar, xnear, far, near, lower, higher, v1_out, v0_out, f0_out, f1_out, wx0, wy0, wz0, inv0, wx1, wy1, wz1, inv1
):
    first = core_mask(8)

    fields, at = [], 0
    for which, tiles in enumerate(TILES):
        mid = planes_of(which, own, xnear, xfar)
        low, high = {}, {}
        for i, n, other in tiles:
            below_it, above_it = jnp.where(first, far[at], near[at]), jnp.where(first, near[at], far[at])
            low[i], high[i] = below_it, above_it
            if other is not None:
                low[other], high[other] = rows(below_it, -n), rows(above_it, n)
            at += 1
        fields.append({i: jnp.concatenate([low[i], mid[i], high[i]], axis=0) for i in low})
    source, coeff, v = fields
    source = {i: 2.0 * source[i] for i in range(-6, 14)}

    fine = Window(1, (-6, 14))
    fine.weights(coeff)
    v = fine.sweep(v, source, -6, 14)
    v = fine.sweep(v, source, -5, 13)
    for i in range(-2, 10):
        v0_out[i + 2] = v[i]
    for i in range(-1, 9):
        f0_out[i + 1] = source[i]
    fine.hand_on((-1, 9), wx0, wy0, wz0, inv0)
    r = fine.residual(v, source, -4, 12)

    source = {i: 0.5 * block_sum(r[2 * i], r[2 * i + 1], 1) for i in range(-2, 6)}
    coeff = {i: 0.125 * block_sum(coeff[2 * i], coeff[2 * i + 1], 1) for i in range(-3, 7)}
    for i in range(-2, 6):
        f1_out[i + 2] = source[i]
    middle = Window(2, (-2, 6))
    middle.weights(coeff)
    middle.hand_on((-2, 6), wx1, wy1, wz1, inv1)
    v = {i: middle.inv[i] * source[i] for i in range(-2, 6)}
    v = middle.sweep(v, source, -1, 5)
    even = iota((8, 128), 1) % 2 == 0
    for i in range(4):
        c = v[i][8:16]
        c = jnp.where(even, c, lanes(rows(c, 2), -1))
        for n, line in enumerate((c[0:1], c[4:5])):
            v1_out[2 * i + n : 2 * i + n + 1, :] = line
            if i < 3:
                lower[2 * i + n + 2 : 2 * i + n + 3, :] = line
            if i > 0:
                higher[2 * i + n : 2 * i + n + 1, :] = line
    r = middle.residual(v, source, 0, 4)

    source = [0.5 * block_sum(r[2 * i], r[2 * i + 1], 2)[8:16] for i in range(2)]
    coeff = [0.125 * block_sum(coeff[2 * i], coeff[2 * i + 1], 2)[8:16] for i in range(2)]
    lane, row = iota((8, 128), 1), iota((8, 128), 0)
    group = lane // 32
    pick = 4 * (lane % 32)
    for c, planes in enumerate((source, coeff)):
        dense = [jnp.take_along_axis(t, pick, axis=1) for t in planes]
        dense = jnp.where(group < 2, dense[0], dense[1])
        dense = jnp.where(row == 4 * (group % 2), dense, 0.0)
        dense = jnp.sum(dense, axis=0, keepdims=True)
        lower[c : c + 1, :] = dense
        higher[c : c + 1, :] = dense


class Coarse:
    def __init__(self, coeff, nxp, nxm, nyp, nym, ylast, yedge, zstep):
        self.nxp, self.nxm, self.nyp, self.nym, self.zstep = nxp, nxm, nyp, nym, zstep
        z = iota(coeff[0].shape, 1) % 32
        zlast = z >= 32 - zstep
        zedge = (z < zstep) | zlast
        self.wp = [k + n for k, n in zip(coeff, nxp(coeff))]
        self.wm = [k + n for k, n in zip(coeff, nxm(coeff))]
        self.wy = [jnp.where(ylast, 0.0, k + nyp(k)) for k in coeff]
        self.wz = [jnp.where(zlast, 0.0, k + lanes(k, zstep)) for k in coeff]
        self.diag = []
        for k, wp, wm, wy, wz in zip(coeff, self.wp, self.wm, self.wy, self.wz):
            diag = wp + wm + (wy + nym(wy)) + (wz + lanes(wz, -zstep))
            self.diag.append(diag + (jnp.where(yedge, k, 0.0) + jnp.where(zedge, k, 0.0)))
        self.inv = [RELAX / d for d in self.diag]

    def around(self, v):
        out = []
        for c, p, m, wp, wm, wy, wz in zip(
            v, self.nxp(v), self.nxm(v), self.wp, self.wm, self.wy, self.wz
        ):
            total = wp * p + wm * m
            total = total + (wy * self.nyp(c) + self.nym(wy * c))
            out.append(total + (wz * lanes(c, self.zstep) + lanes(wz * c, -self.zstep)))
        return out

    def first(self, source):
        return [i * f for i, f in zip(self.inv, source)]

    def sweep(self, v, source):
        around = self.around(v)
        return [KEEP * c + i * (f + t) for c, i, f, t in zip(v, self.inv, source, around)]

    def sweeps(self, v, source, count):
        step = lambda _, v: tuple(self.sweep(list(v), source))
        return list(lax.fori_loop(0, count, step, tuple(v), unroll=True))

    def residual(self, v, source):
        around = self.around(v)
        return [f - d * c + t for c, d, f, t in zip(v, self.diag, source, around)]


def above(c):
    return jnp.concatenate([c[8:], rows(c[:8], 1)], axis=0)


def below(c):
    return jnp.concatenate([rows(c[8:], -1), c[:8]], axis=0)


UNROLL = 10
PAD = 3


def copies_kernel(block, copies):
    for i in range(copies.shape[0]):
        copies[i] = block[...]


def order_kernel(blocks, planes):
    for c in range(2):
        for i in range(32):
            planes[c, i] = blocks[pl.ds(2 * i + c, 8, stride=64), :]


def up_kernel(
    mine, other, v0, f0, f1, wx0, wy0, wz0, inv0, wx1, wy1, wz1, inv1, vmid, vfar, vnear, out,
    k2, f2, va, vb, wxi, wxe, wyi, wye, wz2, diag2, inv2, sumk, sumr, e3,
):
    gx, gy = lax.axis_index("gx"), lax.axis_index("gy")
    first = core_mask(8)
    lane = iota((16, 128), 1)
    row = iota((16, 128), 0)
    group, z = lane // 32, lane % 32
    xl, yl = group // 2, group % 2
    zero = jnp.zeros((16, 128), jnp.float32)

    for ref in (k2, f2, va, vb, wxi, wxe, wyi, wye, wz2, inv2):
        for i in range(PAD):
            ref[i] = zero
            ref[32 + PAD + i] = zero
    for i in range(32):
        for c, ref in ((0, f2), (1, k2)):
            a, b = mine[c, i], other[c, i]
            ref[i + PAD, :8] = jnp.where(first, a, b)
            ref[i + PAD, 8:] = jnp.where(first, b, a)

    def sides(c):
        up, down = lanes(c, 32), lanes(c, -32)
        inner = jnp.where(yl == 0, up, down)
        outer = jnp.where(yl == 1, above(down), below(up))
        return inner, outer

    yout = ((yl == 1) & (row == 15)) | ((yl == 0) & (row == 0))
    zlast = z == 31
    zedge = zlast | (z == 0)

    def advance(i, field, turned, body):
        before, here = turned
        after = lanes(field[i + 1], 64)
        body(i, field[i], here, jnp.where(xl == 1, after, before))
        return here, after

    def summed(k):
        k = k + lanes(k, 64)
        return k + lanes(k, 32)

    def prepare(i, k, inner, outer):
        a, b = k + inner, k + outer
        yi, yo = sides(k)
        c = k + yi
        e = jnp.where(yout, 0.0, k + yo)
        w = jnp.where(zlast, 0.0, k + lanes(k, 1))
        diag = (a + b) + (c + e) + (w + lanes(w, -1))
        diag = diag + (jnp.where(yout, k, 0.0) + jnp.where(zedge, k, 0.0))
        inv = RELAX / diag
        wxi[i], wxe[i], wyi[i], wye[i], wz2[i], diag2[i], inv2[i] = a, b, c, e, w, diag, inv
        va[i] = inv * f2[i]
        sumk[i] = summed(k)

    def around2(i, c, inner, outer):
        yi, yo = sides(c)
        w = wz2[i]
        total = wxi[i] * inner + wxe[i] * outer
        total = total + (wyi[i] * yi + wye[i] * yo)
        return total + (w * lanes(c, 1) + lanes(w * c, -1))

    def sweep2(i, c, inner, outer):
        return KEEP * c + inv2[i] * (f2[i] + around2(i, c, inner, outer))

    def first2(i, c, inner, outer):
        vb[i] = sweep2(i, c, inner, outer)

    def residual2(i, c, inner, outer):
        sumr[i] = summed(f2[i] - diag2[i] * c + around2(i, c, inner, outer))

    def three(i, state):
        ofk, ofa, ofb = state
        ofk = advance(i, k2, ofk, prepare)
        ofa = advance(i - 1, va, ofa, first2)
        return ofk, ofa, advance(i - 2, vb, ofb, residual2)

    ofk = (zero, lanes(k2[PAD], 64))
    ofk = advance(PAD, k2, ofk, prepare)
    ofk = advance(PAD + 1, k2, ofk, prepare)
    ofa = advance(PAD, va, (zero, lanes(va[PAD], 64)), first2)
    ofb = (zero, lanes(vb[PAD], 64))

    def steps(step, state):
        for u in range(UNROLL):
            state = three(PAD + 2 + UNROLL * step + u, state)
        return state

    _, ofa, ofb = lax.fori_loop(0, 30 // UNROLL, steps, (ofk, ofa, ofb))
    advance(PAD + 31, va, ofa, first2)
    ofb = advance(PAD + 30, vb, ofb, residual2)
    advance(PAD + 31, vb, ofb, residual2)

    def four(sums, q):
        t = jnp.where(group == 0, sums[4 * q + PAD], sums[4 * q + PAD + 1])
        t = jnp.where(group == 2, sums[4 * q + PAD + 2], t)
        t = jnp.where(group == 3, sums[4 * q + PAD + 3], t)
        return t + lanes(t, 1)

    c3 = [0.125 * four(sumk, q) for q in range(8)]
    f3 = [0.5 * four(sumr, q) for q in range(8)]

    def plus3(v):
        up = [lanes(c, 32) for c in v] + [zero]
        return [jnp.where(group < 3, up[q], up[q + 1]) for q in range(8)]

    def minus3(v):
        down = [zero] + [lanes(c, -32) for c in v]
        return [jnp.where(group > 0, down[q + 1], down[q]) for q in range(8)]

    level3 = Coarse(c3, plus3, minus3, above, below, row == 15, (row == 0) | (row == 15), 2)
    v3 = level3.sweep(level3.first(f3), f3)
    r3 = level3.residual(v3, f3)

    def restrict(values, x, y, zz):
        s = [t + lanes(t, x) for t in values]
        s = [y(t) for t in s]
        return [t + lanes(t, zz) for t in s]

    cores = lambda t: t[:8] + t[8:]
    f4 = [0.5 * s for s in restrict(r3, 32, cores, 2)]
    c4 = [0.125 * s for s in restrict(c3, 32, cores, 2)]
    zero8 = zero[:8]
    row8, lane8, group8 = row[:8], lane[:8], group[:8]

    def plus4(v):
        turn = [lanes(c, 64) for c in v] + [zero8]
        return [jnp.where(group8 < 2, turn[q], turn[q + 1]) for q in range(8)]

    def minus4(v):
        turn = [zero8] + [lanes(c, 64) for c in v]
        return [jnp.where(group8 < 2, turn[q], turn[q + 1]) for q in range(8)]

    def next_rows(n):
        return lambda c: rows(c, n)

    level4 = Coarse(
        c4, plus4, minus4, next_rows(1), next_rows(-1), row8 == 7, (row8 == 0) | (row8 == 7), 4
    )
    v4 = level4.sweep(level4.first(f4), f4)
    r4 = level4.residual(v4, f4)

    pair = lambda t: t + rows(t, 1)
    f5 = [0.5 * s for s in restrict(r4, 64, pair, 4)]
    c5 = [0.125 * s for s in restrict(c4, 64, pair, 4)]
    level5 = Coarse(
        c5,
        lambda v: v[1:] + [zero8],
        lambda v: [zero8] + v[:-1],
        next_rows(2),
        next_rows(-2),
        row8 >= 6,
        (row8 < 2) | (row8 >= 6),
        8,
    )
    v5 = level5.sweeps(level5.first(f5), f5, COARSE_SWEEPS - 1)

    def spread(c, bit):
        return jnp.where((iota(c.shape, 1) & bit) != 0, lanes(c, -bit), c)

    v5 = [jnp.where((row8 & 1) != 0, rows(c, -1), c) for c in v5]
    v4 = [c + spread(e, 4) for c, e in zip(v4, v5)]
    v4 = level4.sweeps(v4, f4, 2)

    v4 = [spread(jnp.where(group8 % 2 == 1, lanes(c, -32), c), 2) for c in v4]
    v3 = [c + jnp.concatenate([e, e], axis=0) for c, e in zip(v3, v4)]
    v3 = level3.sweeps(v3, f3, 2)

    for q in range(8):
        e3[q] = spread(v3[q], 1)
    for t in range(5):
        p = gx + t - 2
        inside = (p >= 0) & (p < 32)
        p = jnp.clip(p, 0, 31)
        e = jnp.where(group == jnp.where(inside, p % 4, -1), e3[p // 4], 0.0)
        va[gx + t - 2 + PAD] = vb[gx + t - 2 + PAD] + summed(e)

    def some(read, write, first, end):
        turned = [lanes(read[gx + t + PAD], 64) for t in range(first - 1, end + 1)]
        for u, t in enumerate(range(first, end)):
            i = gx + t + PAD
            outer = jnp.where(xl == 1, turned[u + 2], turned[u])
            write[i] = sweep2(i, read[i], turned[u + 1], outer)

    some(va, vb, -2, 3)
    some(vb, va, -1, 2)

    lane8 = iota((8, 128), 1)
    pick = 32 * (iota((8, 128), 0) // 4) + lane8 // 4
    wide = {}
    for t in range(-1, 2):
        for x in range(2):
            parts = []
            for b in range(-1, 2):
                y = gy + b
                inside = (y >= 0) & (y < 16)
                y = jnp.clip(y, 0, 15)
                line = va[gx + t + PAD, pl.ds(8 * (y % 2) + y // 2, 1), :]
                line = jnp.broadcast_to(jnp.where(inside, line, 0.0), (8, 128))
                parts.append(jnp.take_along_axis(line, 64 * x + pick, axis=1))
            wide[t, x] = jnp.concatenate(parts, axis=0)

    def correction(i):
        return wide[i // 4, (i % 4) // 2]

    middle = Window(2, (-2, 6))
    middle.given(wx1, wy1, wz1, inv1)
    source = Stored(f1, -2)
    upper_half = iota((8, 128), 0) >= 4
    second = (iota((ROWS, 128), 0) & 2) != 0

    def received(i):
        n = 2 * i + 6
        c = [jnp.where(upper_half, r[n + 1 : n + 2], r[n : n + 1]) for r in (vmid, vnear, vfar)]
        c = joined(first, *c)
        return jnp.where(second, lanes(c, 1), c)

    v = {i: received(i) + correction(i) for i in range(-3, 7)}
    v = middle.sweep(v, source, -2, 6)
    v = middle.sweep(v, source, -1, 5)

    odd_lane = iota((ROWS, 128), 1) % 2 == 1
    odd_row = iota((ROWS, 128), 0) % 2 == 1
    fine = Window(1, (-1, 9))
    fine.given(wx0, wy0, wz0, inv0)
    source = Stored(f0, -1)
    base = Stored(v0, -2)
    spread1 = {}
    for i in range(-1, 5):
        c = jnp.where(odd_lane, lanes(v[i], -1), v[i])
        spread1[i] = jnp.where(odd_row, rows(c, -1), c)
    v = {i: base[i] + spread1[i // 2] for i in range(-2, 10)}
    v = fine.sweep(v, source, -1, 9)
    v = fine.sweep(v, source, 0, 8)
    for i in range(8):
        out[i] = v[i][8:16]


WINDOW_PLANES = (12, 10, 8, 11, 10, 10, 10, 9, 8, 8, 8)


def f32(*shape):
    return jax.ShapeDtypeStruct(shape, jnp.float32)


def swap(x, axis, first):
    pairs = [(i, i + 1) for i in range(first, lax.axis_size(axis) - 1, 2)]
    return lax.ppermute(x, axis, pairs + [(b, a) for a, b in pairs])


def shards(right_side, coefficient, previous):
    even = lax.axis_index("gx") % 2 == 0
    own = lax.optimization_barrier(jnp.concatenate([right_side, coefficient, previous])).reshape(3, 8, 8, 128)
    start, end = own[:, :HALO], own[:, -HALO:]
    near = swap(jnp.where(even, end, start), "gx", 0)
    far = swap(jnp.where(even, start, end), "gx", 1)

    params = pltpu.CompilerParams(vmem_limit_bytes=VMEM)
    array = pl.BlockSpec(memory_space=pltpu.VMEM)
    count = sum(len(tiles) for tiles in TILES)
    to_near, to_far = pl.pallas_call(
        pack_kernel,
        in_specs=[array] * 3,
        out_shape=(f32(count, 8, 128),) * 2,
        compiler_params=params,
        name="pack",
    )(own, far, near)
    from_far = swap(to_far, "gy", 1)
    from_near = swap(to_near, "gy", 0)

    lower, higher, v1, *window = pl.pallas_call(
        down_kernel,
        in_specs=[array] * 5,
        out_shape=(f32(8, 128),) * 3 + tuple(f32(n, ROWS, 128) for n in WINDOW_PLANES),
        compiler_params=params,
        name="down",
    )(own, far, near, from_far, from_near)

    gx = lax.axis_index("gx")
    before = lax.broadcasted_iota(jnp.int32, (32, 1, 1), 0) < gx
    blocks = jnp.where(before, lower.reshape(1, 1, 1024), higher.reshape(1, 1, 1024))
    blocks = lax.all_to_all(blocks, "gx", 0, 0)
    same_core = [[2 * z + c for z in range(8)] for c in range(2)]
    copies = pl.pallas_call(
        copies_kernel,
        in_specs=[array],
        out_shape=f32(8, 64, 128),
        compiler_params=params,
        name="copies",
    )(blocks[:, :, :256].reshape(64, 128))
    mine = lax.all_to_all(copies, "gy", 0, 0, axis_index_groups=same_core).reshape(512, 128)
    mine = pl.pallas_call(
        order_kernel,
        in_specs=[array],
        out_shape=f32(2, 32, 8, 128),
        compiler_params=params,
        name="order",
    )(mine)
    beside = jnp.pad(blocks[:, 0, 256:], ((1, 1), (0, 0)))
    low = lax.dynamic_slice(beside, (gx, jnp.int32(0)), (1, 768))
    high = lax.dynamic_slice(beside, (gx + 2, jnp.int32(0)), (1, 768))
    vmid = jnp.concatenate([low.reshape(6, 128), v1, high.reshape(6, 128)])
    vnear, vfar = swap(vmid, "gy", 0), swap(vmid, "gy", 1)
    mine, vfar, vnear = lax.optimization_barrier((mine, vfar, vnear))
    other = swap(mine, "gy", 0)

    plane = pltpu.VMEM((32 + 2 * PAD, 16, 128), jnp.float32)
    return pl.pallas_call(
        up_kernel,
        in_specs=[array] * (5 + len(WINDOW_PLANES)),
        out_shape=f32(8, 8, 128),
        scratch_shapes=[plane] * 13 + [pltpu.VMEM((8, 16, 128), jnp.float32)],
        compiler_params=params,
        name="up",
    )(mine, other, *window, vmid, vfar, vnear)


def solution(mesh):
    spec = P("gx", "gy", None)
    return jax.shard_map(
        shards, mesh=mesh, in_specs=(spec,) * 3, out_specs=spec, check_vma=False
    )
```

```python
import jax
import jax.numpy as jnp
from jax import lax
from jax.experimental import pallas as pl
from jax.experimental.pallas import tpu as pltpu
from jax.sharding import PartitionSpec as P

RELAX = 0.8
KEEP = 1.0 - RELAX
HALO = 7
ROWS = 24
COARSE_SWEEPS = 8
VMEM = 48 * 1024 * 1024


def lanes(x, n):
    return pltpu.roll(x, (-n) % x.shape[1], axis=1)


def rows(x, n):
    return pltpu.roll(x, (-n) % x.shape[0], axis=0)


def iota(shape, dim):
    return lax.broadcasted_iota(jnp.int32, shape, dim)


class Window:
    def __init__(self, step, planes):
        self.step = step
        self.planes = planes

    def given(self, wx, wy, wz, inv):
        first = self.planes[0]
        self.wx, self.wy = Stored(wx, first - 1), Stored(wy, first)
        self.wz, self.inv = Stored(wz, first), Stored(inv, first)

    def hand_on(self, planes, wx, wy, wz, inv):
        first, end = planes
        for i in range(first - 1, end):
            wx[i - first + 1] = self.wx[i]
        for i in range(first, end):
            wy[i - first], wz[i - first], inv[i - first] = self.wy[i], self.wz[i], self.inv[i]

    def weights(self, coeff):
        first, end = self.planes
        lane = iota((ROWS, 128), 1)
        last = lane >= 128 - self.step
        edge = (lane < self.step) | last
        self.wx, self.wy, self.wz, self.diag, self.inv = {}, {}, {}, {}, {}
        for i in range(first - 1, end):
            self.wx[i] = coeff[i] + coeff[i + 1]
        for i in range(first, end):
            k = coeff[i]
            wy = k + rows(k, self.step)
            wz = jnp.where(last, 0.0, k + lanes(k, self.step))
            diag = self.wx[i] + self.wx[i - 1] + (wy + rows(wy, -self.step))
            diag = diag + (wz + lanes(wz, -self.step)) + jnp.where(edge, k, 0.0)
            self.wy[i], self.wz[i], self.diag[i] = wy, wz, diag
            self.inv[i] = jnp.where(k > 0.0, RELAX / diag, 0.0)

    def around(self, v, i):
        c = v[i]
        wy, wz, step = self.wy[i], self.wz[i], self.step
        total = self.wx[i] * v[i + 1] + self.wx[i - 1] * v[i - 1]
        total = total + (wy * rows(c, step) + rows(wy * c, -step))
        return total + (wz * lanes(c, step) + lanes(wz * c, -step))

    def sweep(self, v, source, first, end):
        return {
            i: KEEP * v[i] + self.inv[i] * (source[i] + self.around(v, i)) for i in range(first, end)
        }

    def residual(self, v, source, first, end):
        return {i: source[i] - self.diag[i] * v[i] + self.around(v, i) for i in range(first, end)}


class Stored:
    def __init__(self, ref, first):
        self.ref, self.first = ref, first

    def __getitem__(self, i):
        return self.ref[i - self.first]

    def __setitem__(self, i, value):
        self.ref[i - self.first] = value


def block_sum(low, high, step):
    s = low + high
    s = s + rows(s, step)
    return s + lanes(s, step)


def alone(*planes):
    return [(i, 8, None) for i in planes]


INNER = range(8)
NARROW = [(0, 6, -6), (7, 6, 13)] + alone(1, 2, 3, 4, 5, 6, -1, -2, 8, 9)
NARROW += [(-3, 5, -5), (10, 5, 12), (-4, 4, 11)]
WIDE = alone(*INNER, -1, -2, 8, 9)
WIDE += [(-3, 6, -7), (10, 6, 14), (-4, 5, -6), (11, 5, 13), (-5, 4, 12)]
TILES = (NARROW, WIDE, WIDE)


def planes_of(which, own, near, far):
    even = jnp.broadcast_to(lax.rem(lax.axis_index("gx"), 2), (8, 128)) == 0
    planes = {i: own[which, i] for i in INNER}
    for i in range(HALO):
        a, b = near[which, i], far[which, i]
        planes[i - HALO], planes[i + 8] = jnp.where(even, b, a), jnp.where(even, a, b)
    return planes


def pack_kernel(own, far, near, to_near, to_far):
    first = core_mask(8)
    row = iota((8, 128), 0)
    at = 0
    for which, tiles in enumerate(TILES):
        planes = planes_of(which, own, near, far)
        for a, n, b in tiles:
            upward = downward = planes[a]
            if b is not None:
                upward = jnp.where(row >= 8 - n, planes[a], rows(planes[b], n))
                downward = jnp.where(row < n, planes[a], rows(planes[b], -n))
            to_near[at] = jnp.where(first, upward, downward)
            to_far[at] = jnp.where(first, downward, upward)
            at += 1


def core_mask(rows_of):
    core = lax.rem(lax.axis_index("gy"), 2)
    return jnp.broadcast_to(core, (rows_of, 128)) == 0


def joined(first, mid, near, far):
    return jnp.concatenate([jnp.where(first, far, near), mid, jnp.where(first, near, far)], axis=0)


def down_kernel(
    own, xfar, xnear, far, near, lower, higher, v1_out, v0_out, f0_out, f1_out, wx0, wy0, wz0, inv0, wx1, wy1, wz1, inv1
):
    first = core_mask(8)

    fields, at = [], 0
    for which, tiles in enumerate(TILES):
        mid = planes_of(which, own, xnear, xfar)
        low, high = {}, {}
        for i, n, other in tiles:
            below_it, above_it = jnp.where(first, far[at], near[at]), jnp.where(first, near[at], far[at])
            low[i], high[i] = below_it, above_it
            if other is not None:
                low[other], high[other] = rows(below_it, -n), rows(above_it, n)
            at += 1
        fields.append({i: jnp.concatenate([low[i], mid[i], high[i]], axis=0) for i in low})
    source, coeff, v = fields
    source = {i: 2.0 * source[i] for i in range(-6, 14)}

    fine = Window(1, (-6, 14))
    fine.weights(coeff)
    v = fine.sweep(v, source, -6, 14)
    v = fine.sweep(v, source, -5, 13)
    for i in range(-2, 10):
        v0_out[i + 2] = v[i]
    for i in range(-1, 9):
        f0_out[i + 1] = source[i]
    fine.hand_on((-1, 9), wx0, wy0, wz0, inv0)
    r = fine.residual(v, source, -4, 12)

    source = {i: 0.5 * block_sum(r[2 * i], r[2 * i + 1], 1) for i in range(-2, 6)}
    coeff = {i: 0.125 * block_sum(coeff[2 * i], coeff[2 * i + 1], 1) for i in range(-3, 7)}
    for i in range(-2, 6):
        f1_out[i + 2] = source[i]
    middle = Window(2, (-2, 6))
    middle.weights(coeff)
    middle.hand_on((-2, 6), wx1, wy1, wz1, inv1)
    v = {i: middle.inv[i] * source[i] for i in range(-2, 6)}
    v = middle.sweep(v, source, -1, 5)
    even = iota((8, 128), 1) % 2 == 0
    for i in range(4):
        c = v[i][8:16]
        c = jnp.where(even, c, lanes(rows(c, 2), -1))
        for n, line in enumerate((c[0:1], c[4:5])):
            v1_out[2 * i + n : 2 * i + n + 1, :] = line
            if i < 3:
                lower[2 * i + n + 2 : 2 * i + n + 3, :] = line
            if i > 0:
                higher[2 * i + n : 2 * i + n + 1, :] = line
    r = middle.residual(v, source, 0, 4)

    source = [0.5 * block_sum(r[2 * i], r[2 * i + 1], 2)[8:16] for i in range(2)]
    coeff = [0.125 * block_sum(coeff[2 * i], coeff[2 * i + 1], 2)[8:16] for i in range(2)]
    lane, row = iota((8, 128), 1), iota((8, 128), 0)
    group = lane // 32
    pick = 4 * (lane % 32)
    for c, planes in enumerate((source, coeff)):
        dense = [jnp.take_along_axis(t, pick, axis=1) for t in planes]
        dense = jnp.where(group < 2, dense[0], dense[1])
        dense = jnp.where(row == 4 * (group % 2), dense, 0.0)
        dense = jnp.sum(dense, axis=0, keepdims=True)
        lower[c : c + 1, :] = dense
        higher[c : c + 1, :] = dense


class Coarse:
    def __init__(self, coeff, nxp, nxm, nyp, nym, ylast, yedge, zstep):
        self.nxp, self.nxm, self.nyp, self.nym, self.zstep = nxp, nxm, nyp, nym, zstep
        z = iota(coeff[0].shape, 1) % 32
        zlast = z >= 32 - zstep
        zedge = (z < zstep) | zlast
        self.wp = [k + n for k, n in zip(coeff, nxp(coeff))]
        self.wm = [k + n for k, n in zip(coeff, nxm(coeff))]
        self.wy = [jnp.where(ylast, 0.0, k + nyp(k)) for k in coeff]
        self.wz = [jnp.where(zlast, 0.0, k + lanes(k, zstep)) for k in coeff]
        self.diag = []
        for k, wp, wm, wy, wz in zip(coeff, self.wp, self.wm, self.wy, self.wz):
            diag = wp + wm + (wy + nym(wy)) + (wz + lanes(wz, -zstep))
            self.diag.append(diag + (jnp.where(yedge, k, 0.0) + jnp.where(zedge, k, 0.0)))
        self.inv = [RELAX / d for d in self.diag]

    def around(self, v):
        out = []
        for c, p, m, wp, wm, wy, wz in zip(
            v, self.nxp(v), self.nxm(v), self.wp, self.wm, self.wy, self.wz
        ):
            total = wp * p + wm * m
            total = total + (wy * self.nyp(c) + self.nym(wy * c))
            out.append(total + (wz * lanes(c, self.zstep) + lanes(wz * c, -self.zstep)))
        return out

    def first(self, source):
        return [i * f for i, f in zip(self.inv, source)]

    def sweep(self, v, source):
        around = self.around(v)
        return [KEEP * c + i * (f + t) for c, i, f, t in zip(v, self.inv, source, around)]

    def sweeps(self, v, source, count):
        step = lambda _, v: tuple(self.sweep(list(v), source))
        return list(lax.fori_loop(0, count, step, tuple(v), unroll=True))

    def residual(self, v, source):
        around = self.around(v)
        return [f - d * c + t for c, d, f, t in zip(v, self.diag, source, around)]


def above(c):
    return jnp.concatenate([c[8:], rows(c[:8], 1)], axis=0)


def below(c):
    return jnp.concatenate([rows(c[8:], -1), c[:8]], axis=0)


UNROLL = 10
PAD = 3


def copies_kernel(block, copies, sems):
    started = [pltpu.make_async_copy(block, copies.at[i], sems.at[i]) for i in range(8)]
    for copy in started:
        copy.start()
    for copy in started:
        copy.wait()


def order_kernel(blocks, planes):
    for c in range(2):
        for i in range(32):
            planes[c, i] = blocks[pl.ds(2 * i + c, 8, stride=64), :]


def up_kernel(
    mine, other, v0, f0, f1, wx0, wy0, wz0, inv0, wx1, wy1, wz1, inv1, vmid, vfar, vnear, out,
    k2, f2, va, vb, wxi, wxe, wyi, wye, wz2, diag2, inv2, sumk, sumr, e3,
):
    gx, gy = lax.axis_index("gx"), lax.axis_index("gy")
    first = core_mask(8)
    lane = iota((16, 128), 1)
    row = iota((16, 128), 0)
    group, z = lane // 32, lane % 32
    xl, yl = group // 2, group % 2
    zero = jnp.zeros((16, 128), jnp.float32)

    for ref in (k2, f2, va, vb, wxi, wxe, wyi, wye, wz2, inv2):
        for i in range(PAD):
            ref[i] = zero
            ref[32 + PAD + i] = zero
    for i in range(32):
        for c, ref in ((0, f2), (1, k2)):
            a, b = mine[c, i], other[c, i]
            ref[i + PAD, :8] = jnp.where(first, a, b)
            ref[i + PAD, 8:] = jnp.where(first, b, a)

    def sides(c):
        up, down = lanes(c, 32), lanes(c, -32)
        inner = jnp.where(yl == 0, up, down)
        outer = jnp.where(yl == 1, above(down), below(up))
        return inner, outer

    yout = ((yl == 1) & (row == 15)) | ((yl == 0) & (row == 0))
    zlast = z == 31
    zedge = zlast | (z == 0)

    def advance(i, field, turned, body):
        before, here = turned
        after = lanes(field[i + 1], 64)
        body(i, field[i], here, jnp.where(xl == 1, after, before))
        return here, after

    def summed(k):
        k = k + lanes(k, 64)
        return k + lanes(k, 32)

    def prepare(i, k, inner, outer):
        a, b = k + inner, k + outer
        yi, yo = sides(k)
        c = k + yi
        e = jnp.where(yout, 0.0, k + yo)
        w = jnp.where(zlast, 0.0, k + lanes(k, 1))
        diag = (a + b) + (c + e) + (w + lanes(w, -1))
        diag = diag + (jnp.where(yout, k, 0.0) + jnp.where(zedge, k, 0.0))
        inv = RELAX / diag
        wxi[i], wxe[i], wyi[i], wye[i], wz2[i], diag2[i], inv2[i] = a, b, c, e, w, diag, inv
        va[i] = inv * f2[i]
        sumk[i] = summed(k)

    def around2(i, c, inner, outer):
        yi, yo = sides(c)
        w = wz2[i]
        total = wxi[i] * inner + wxe[i] * outer
        total = total + (wyi[i] * yi + wye[i] * yo)
        return total + (w * lanes(c, 1) + lanes(w * c, -1))

    def sweep2(i, c, inner, outer):
        return KEEP * c + inv2[i] * (f2[i] + around2(i, c, inner, outer))

    def first2(i, c, inner, outer):
        vb[i] = sweep2(i, c, inner, outer)

    def residual2(i, c, inner, outer):
        sumr[i] = summed(f2[i] - diag2[i] * c + around2(i, c, inner, outer))

    def three(i, state):
        ofk, ofa, ofb = state
        ofk = advance(i, k2, ofk, prepare)
        ofa = advance(i - 1, va, ofa, first2)
        return ofk, ofa, advance(i - 2, vb, ofb, residual2)

    ofk = (zero, lanes(k2[PAD], 64))
    ofk = advance(PAD, k2, ofk, prepare)
    ofk = advance(PAD + 1, k2, ofk, prepare)
    ofa = advance(PAD, va, (zero, lanes(va[PAD], 64)), first2)
    ofb = (zero, lanes(vb[PAD], 64))

    def steps(step, state):
        for u in range(UNROLL):
            state = three(PAD + 2 + UNROLL * step + u, state)
        return state

    _, ofa, ofb = lax.fori_loop(0, 30 // UNROLL, steps, (ofk, ofa, ofb))
    advance(PAD + 31, va, ofa, first2)
    ofb = advance(PAD + 30, vb, ofb, residual2)
    advance(PAD + 31, vb, ofb, residual2)

    def four(sums, q):
        t = jnp.where(group == 0, sums[4 * q + PAD], sums[4 * q + PAD + 1])
        t = jnp.where(group == 2, sums[4 * q + PAD + 2], t)
        t = jnp.where(group == 3, sums[4 * q + PAD + 3], t)
        return t + lanes(t, 1)

    c3 = [0.125 * four(sumk, q) for q in range(8)]
    f3 = [0.5 * four(sumr, q) for q in range(8)]

    def plus3(v):
        up = [lanes(c, 32) for c in v] + [zero]
        return [jnp.where(group < 3, up[q], up[q + 1]) for q in range(8)]

    def minus3(v):
        down = [zero] + [lanes(c, -32) for c in v]
        return [jnp.where(group > 0, down[q + 1], down[q]) for q in range(8)]

    level3 = Coarse(c3, plus3, minus3, above, below, row == 15, (row == 0) | (row == 15), 2)
    v3 = level3.sweep(level3.first(f3), f3)
    r3 = level3.residual(v3, f3)

    def restrict(values, x, y, zz):
        s = [t + lanes(t, x) for t in values]
        s = [y(t) for t in s]
        return [t + lanes(t, zz) for t in s]

    cores = lambda t: t[:8] + t[8:]
    f4 = [0.5 * s for s in restrict(r3, 32, cores, 2)]
    c4 = [0.125 * s for s in restrict(c3, 32, cores, 2)]
    zero8 = zero[:8]
    row8, lane8, group8 = row[:8], lane[:8], group[:8]

    def plus4(v):
        turn = [lanes(c, 64) for c in v] + [zero8]
        return [jnp.where(group8 < 2, turn[q], turn[q + 1]) for q in range(8)]

    def minus4(v):
        turn = [zero8] + [lanes(c, 64) for c in v]
        return [jnp.where(group8 < 2, turn[q], turn[q + 1]) for q in range(8)]

    def next_rows(n):
        return lambda c: rows(c, n)

    level4 = Coarse(
        c4, plus4, minus4, next_rows(1), next_rows(-1), row8 == 7, (row8 == 0) | (row8 == 7), 4
    )
    v4 = level4.sweep(level4.first(f4), f4)
    r4 = level4.residual(v4, f4)

    pair = lambda t: t + rows(t, 1)
    f5 = [0.5 * s for s in restrict(r4, 64, pair, 4)]
    c5 = [0.125 * s for s in restrict(c4, 64, pair, 4)]
    level5 = Coarse(
        c5,
        lambda v: v[1:] + [zero8],
        lambda v: [zero8] + v[:-1],
        next_rows(2),
        next_rows(-2),
        row8 >= 6,
        (row8 < 2) | (row8 >= 6),
        8,
    )
    v5 = level5.sweeps(level5.first(f5), f5, COARSE_SWEEPS - 1)

    def spread(c, bit):
        return jnp.where((iota(c.shape, 1) & bit) != 0, lanes(c, -bit), c)

    v5 = [jnp.where((row8 & 1) != 0, rows(c, -1), c) for c in v5]
    v4 = [c + spread(e, 4) for c, e in zip(v4, v5)]
    v4 = level4.sweeps(v4, f4, 2)

    v4 = [spread(jnp.where(group8 % 2 == 1, lanes(c, -32), c), 2) for c in v4]
    v3 = [c + jnp.concatenate([e, e], axis=0) for c, e in zip(v3, v4)]
    v3 = level3.sweeps(v3, f3, 2)

    for q in range(8):
        e3[q] = spread(v3[q], 1)
    for t in range(5):
        p = gx + t - 2
        inside = (p >= 0) & (p < 32)
        p = jnp.clip(p, 0, 31)
        e = jnp.where(group == jnp.where(inside, p % 4, -1), e3[p // 4], 0.0)
        va[gx + t - 2 + PAD] = vb[gx + t - 2 + PAD] + summed(e)

    def some(read, write, first, end):
        turned = [lanes(read[gx + t + PAD], 64) for t in range(first - 1, end + 1)]
        for u, t in enumerate(range(first, end)):
            i = gx + t + PAD
            outer = jnp.where(xl == 1, turned[u + 2], turned[u])
            write[i] = sweep2(i, read[i], turned[u + 1], outer)

    some(va, vb, -2, 3)
    some(vb, va, -1, 2)

    lane8 = iota((8, 128), 1)
    pick = 32 * (iota((8, 128), 0) // 4) + lane8 // 4
    wide = {}
    for t in range(-1, 2):
        for x in range(2):
            parts = []
            for b in range(-1, 2):
                y = gy + b
                inside = (y >= 0) & (y < 16)
                y = jnp.clip(y, 0, 15)
                line = va[gx + t + PAD, pl.ds(8 * (y % 2) + y // 2, 1), :]
                line = jnp.broadcast_to(jnp.where(inside, line, 0.0), (8, 128))
                parts.append(jnp.take_along_axis(line, 64 * x + pick, axis=1))
            wide[t, x] = jnp.concatenate(parts, axis=0)

    def correction(i):
        return wide[i // 4, (i % 4) // 2]

    middle = Window(2, (-2, 6))
    middle.given(wx1, wy1, wz1, inv1)
    source = Stored(f1, -2)
    upper_half = iota((8, 128), 0) >= 4
    second = (iota((ROWS, 128), 0) & 2) != 0

    def received(i):
        n = 2 * i + 6
        c = [jnp.where(upper_half, r[n + 1 : n + 2], r[n : n + 1]) for r in (vmid, vnear, vfar)]
        c = joined(first, *c)
        return jnp.where(second, lanes(c, 1), c)

    v = {i: received(i) + correction(i) for i in range(-3, 7)}
    v = middle.sweep(v, source, -2, 6)
    v = middle.sweep(v, source, -1, 5)

    odd_lane = iota((ROWS, 128), 1) % 2 == 1
    odd_row = iota((ROWS, 128), 0) % 2 == 1
    fine = Window(1, (-1, 9))
    fine.given(wx0, wy0, wz0, inv0)
    source = Stored(f0, -1)
    base = Stored(v0, -2)
    spread1 = {}
    for i in range(-1, 5):
        c = jnp.where(odd_lane, lanes(v[i], -1), v[i])
        spread1[i] = jnp.where(odd_row, rows(c, -1), c)
    v = {i: base[i] + spread1[i // 2] for i in range(-2, 10)}
    v = fine.sweep(v, source, -1, 9)
    v = fine.sweep(v, source, 0, 8)
    for i in range(8):
        out[i] = v[i][8:16]


WINDOW_PLANES = (12, 10, 8, 11, 10, 10, 10, 9, 8, 8, 8)


def f32(*shape):
    return jax.ShapeDtypeStruct(shape, jnp.float32)


def swap(x, axis, first):
    pairs = [(i, i + 1) for i in range(first, lax.axis_size(axis) - 1, 2)]
    return lax.ppermute(x, axis, pairs + [(b, a) for a, b in pairs])


def shards(right_side, coefficient, previous):
    even = lax.axis_index("gx") % 2 == 0
    own = lax.optimization_barrier(jnp.concatenate([right_side, coefficient, previous])).reshape(3, 8, 8, 128)
    start, end = own[:, :HALO], own[:, -HALO:]
    near = swap(jnp.where(even, end, start), "gx", 0)
    far = swap(jnp.where(even, start, end), "gx", 1)

    params = pltpu.CompilerParams(vmem_limit_bytes=VMEM)
    array = pl.BlockSpec(memory_space=pltpu.VMEM)
    count = sum(len(tiles) for tiles in TILES)
    to_near, to_far = pl.pallas_call(
        pack_kernel,
        in_specs=[array] * 3,
        out_shape=(f32(count, 8, 128),) * 2,
        compiler_params=params,
        name="pack",
    )(own, far, near)
    from_far = swap(to_far, "gy", 1)
    from_near = swap(to_near, "gy", 0)

    lower, higher, v1, *window = pl.pallas_call(
        down_kernel,
        in_specs=[array] * 5,
        out_shape=(f32(8, 128),) * 3 + tuple(f32(n, ROWS, 128) for n in WINDOW_PLANES),
        compiler_params=params,
        name="down",
    )(own, far, near, from_far, from_near)

    gx = lax.axis_index("gx")
    before = lax.broadcasted_iota(jnp.int32, (32, 1, 1), 0) < gx
    blocks = jnp.where(before, lower.reshape(1, 1, 1024), higher.reshape(1, 1, 1024))
    blocks = lax.all_to_all(blocks, "gx", 0, 0)
    same_core = [[2 * z + c for z in range(8)] for c in range(2)]
    copies = pl.pallas_call(
        copies_kernel,
        in_specs=[array],
        out_specs=pl.BlockSpec(memory_space=pl.ANY),
        out_shape=f32(8, 64, 128),
        scratch_shapes=[pltpu.SemaphoreType.DMA((8,))],
        compiler_params=params,
        name="copies",
    )(blocks[:, :, :256].reshape(64, 128))
    mine = lax.all_to_all(copies, "gy", 0, 0, axis_index_groups=same_core).reshape(512, 128)
    mine = pl.pallas_call(
        order_kernel,
        in_specs=[array],
        out_shape=f32(2, 32, 8, 128),
        compiler_params=params,
        name="order",
    )(mine)
    beside = jnp.pad(blocks[:, 0, 256:], ((1, 1), (0, 0)))
    low = lax.dynamic_slice(beside, (gx, jnp.int32(0)), (1, 768))
    high = lax.dynamic_slice(beside, (gx + 2, jnp.int32(0)), (1, 768))
    vmid = jnp.concatenate([low.reshape(6, 128), v1, high.reshape(6, 128)])
    vnear, vfar = swap(vmid, "gy", 0), swap(vmid, "gy", 1)
    mine, vfar, vnear = lax.optimization_barrier((mine, vfar, vnear))
    other = swap(mine, "gy", 0)

    plane = pltpu.VMEM((32 + 2 * PAD, 16, 128), jnp.float32)
    return pl.pallas_call(
        up_kernel,
        in_specs=[array] * (5 + len(WINDOW_PLANES)),
        out_shape=f32(8, 8, 128),
        scratch_shapes=[plane] * 13 + [pltpu.VMEM((8, 16, 128), jnp.float32)],
        compiler_params=params,
        name="up",
    )(mine, other, *window, vmid, vfar, vnear)


def solution(mesh):
    spec = P("gx", "gy", None)
    return jax.shard_map(
        shards, mesh=mesh, in_specs=(spec,) * 3, out_specs=spec, check_vma=False
    )
```
